32 devices in a mesh: section: 2 (over core), dp: 16 (over z, y, x).
Axes of the slice: x: 2, y: 2, z: 4, core: 2. Of those that a mesh axis runs over, the one named last changes fastest.
Arguments:
- tokens: bfloat16 [2, 16, 256, 768], P(None, 'dp'), may hold values from -6 to 6
- order: int32 [2, 16, 1024], P(None, 'dp'), may hold values from 0 to 1023, each once within a row
- sensor: int32 [2, 16], P(None, 'dp'), may hold values from 0 to 3
- cotangent: bfloat16 [2, 16, 1024, 512], P(None, 'dp'), may hold values from -6 to 6
- enc_norm: bfloat16 [4, 768], replicated, may hold values from 0.099609375 to 1.8984375
- enc_qkv: bfloat16 [768, 2304], replicated, may hold values from -0.21875 to 0.21875
- enc_out: bfloat16 [768, 768], replicated, may hold values from -0.875 to 0.875
- enc_bias: bfloat16 [2, 768], replicated, may hold values from -3 to 3
- enc_up: bfloat16 [768, 3072], replicated, may hold values from -0.21875 to 0.21875
- enc_up_bias: bfloat16 [3072], replicated, may hold values from -3 to 3
- enc_down: bfloat16 [3072, 768], replicated, may hold values from -0.109375 to 0.109375
- sensor_table: bfloat16 [4, 768], replicated, may hold values from -3 to 3
- dec_embed: bfloat16 [768, 512], replicated, may hold values from -0.21875 to 0.21875
- dec_norm: bfloat16 [4, 512], replicated, may hold values from 0.099609375 to 1.8984375
- dec_qkv: bfloat16 [512, 768], replicated, may hold values from -0.25 to 0.25
- dec_out: bfloat16 [256, 512], replicated, may hold values from -1.5 to 1.5
- dec_bias: bfloat16 [4, 512], replicated, may hold values from -3 to 3
- dec_up: bfloat16 [512, 2048], replicated, may hold values from -0.25 to 0.25
- dec_up_bias: bfloat16 [2048], replicated, may hold values from -3 to 3
- dec_down: bfloat16 [2048, 512], replicated, may hold values from -0.125 to 0.125
- dec_pos: bfloat16 [1024, 512], replicated, may hold values from -5 to 5
Outputs:
- decoded: float32 [2, 16, 1024, 512], P('section', 'dp')
- input_grad: float32 [2, 16, 256, 768], P('section', 'dp')
- grad_enc_norm: float32 [4, 768], P('section', 'dp')
- grad_enc_qkv: float32 [768, 2304], P('dp', 'section')
- grad_enc_out: float32 [768, 768], P('dp', 'section')
- grad_enc_bias: float32 [2, 768], P('section', 'dp')
- grad_enc_up: float32 [768, 3072], P('dp', 'section')
- grad_enc_up_bias: float32 [3072], P(('section', 'dp'))
- grad_enc_down: float32 [3072, 768], P('dp', 'section')
- grad_sensor_table: float32 [4, 768], P('section', 'dp')
- grad_dec_embed: float32 [768, 512], P('dp', 'section')
- grad_dec_norm: float32 [4, 512], P('section', 'dp')
- grad_dec_qkv: float32 [512, 768], P('dp', 'section')
- grad_dec_out: float32 [256, 512], P('dp', 'section')
- grad_dec_bias: float32 [4, 512], P('section', 'dp')
- grad_dec_up: float32 [512, 2048], P('dp', 'section')
- grad_dec_up_bias: float32 [2048], P(('section', 'dp'))
- grad_dec_down: float32 [2048, 512], P('dp', 'section')
- grad_dec_pos: float32 [1024, 512], P('section', 'dp')
The draws below stay inside these ranges and needn't reach their ends.
Inputs may be any that keep to these rules, and one draw needn't show every extreme that they name: `order`: each image's row is a permutation of the 1024 patch positions; its first 256 entries are the visible patches, the rest are masked.
All inputs are finite; a program needn't handle non-finite values.
Results may differ from the reference program's by a relative error of at most 0.015.
Values may be sent and summed in bfloat16 or wider, within the bound.
A program may use at most 256 MiB of HBM per device.

```python
import jax
import jax.numpy as jnp
from jax import lax

D = 768
HEAD_DIM = 64
FF = 3072
DEC_D = 512
DEC_INNER = 256
DEC_FF = 2048
PATCHES = 1024
VISIBLE = 256
SENSORS = 4
MICRO = 2
IMAGES = 16


def with_ends(drawn, own_key, low, high):
    extent = drawn.shape
    spot = [jax.random.randint(jax.random.fold_in(own_key, axis), (), 0, extent[axis]) for axis in range(len(extent))]
    drawn = drawn.at[tuple(spot)].set(low)
    longest = extent.index(max(extent))
    spot[longest] = (spot[longest] + 1) % extent[longest]
    return drawn.at[tuple(spot)].set(high)


def shard_levels(own_key, dims, split, smallest, largest):
    factor_of = 1.0
    for position, blocks in split:
        heights = jax.random.uniform(jax.random.fold_in(jax.random.fold_in(own_key, 6), position), (blocks,), jnp.float32, smallest / len(split), largest / len(split))
        factor_of = factor_of * jnp.repeat(jnp.exp(heights), dims[position] // blocks).reshape((-1,) + (1,) * (len(dims) - 1 - position))
    return factor_of


def normal_values(stream_key, extent, scale, limit, shards=(), kind=jnp.bfloat16):
    result = scale * jax.random.normal(stream_key, extent, jnp.float32)
    if shards:
        result = result * shard_levels(stream_key, extent, shards, -0.22, 0.18)
    return jnp.clip(result, -limit, limit).astype(kind)


def setup_inputs(seed: int = 0) -> dict:
    key_list = jax.random.split(jax.random.key(seed), 22)
    return {
        "tokens": normal_values(key_list[0], (MICRO, IMAGES, VISIBLE, D), 1.0, 6.0, ((1, 16),)),
        "order": jax.vmap(lambda own: jax.random.permutation(own, PATCHES))(jax.random.split(key_list[1], MICRO * IMAGES)).reshape((MICRO, IMAGES, PATCHES)).astype(jnp.int32),
        "sensor": with_ends(jax.random.randint(key_list[2], (MICRO, IMAGES), 0, SENSORS), jax.random.fold_in(key_list[2], 1), 0, SENSORS - 1).astype(jnp.int32),
        "cotangent": normal_values(key_list[3], (MICRO, IMAGES, PATCHES, DEC_D), 1.0, 6.0, ((1, 16),)),
        "enc_norm": jnp.clip(1.0 + 0.18 * jax.random.normal(key_list[4], (4, D), jnp.float32), 0.099609375, 1.8984375).astype(jnp.bfloat16),
        "enc_qkv": normal_values(key_list[5], (D, 3 * D), D ** -0.5, 0.21875),
        "enc_out": normal_values(key_list[6], (D, D), (D // 16) ** -0.5, 0.875),
        "enc_bias": normal_values(key_list[7], (2, D), 0.5, 3.0),
        "enc_up": normal_values(key_list[8], (D, FF), D ** -0.5, 0.21875),
        "enc_up_bias": normal_values(key_list[9], (FF,), 0.5, 3.0),
        "enc_down": normal_values(key_list[10], (FF, D), FF ** -0.5, 0.109375),
        "sensor_table": normal_values(key_list[11], (SENSORS, D), 0.5, 3.0),
        "dec_embed": normal_values(key_list[12], (D, DEC_D), D ** -0.5, 0.21875),
        "dec_norm": jnp.clip(1.0 + 0.18 * jax.random.normal(key_list[13], (4, DEC_D), jnp.float32), 0.099609375, 1.8984375).astype(jnp.bfloat16),
        "dec_qkv": normal_values(key_list[14], (DEC_D, 3 * DEC_INNER), DEC_D ** -0.5, 0.25),
        "dec_out": normal_values(key_list[15], (DEC_INNER, DEC_D), (DEC_INNER // 16) ** -0.5, 1.5),
        "dec_bias": normal_values(key_list[16], (4, DEC_D), 0.5, 3.0),
        "dec_up": normal_values(key_list[17], (DEC_D, DEC_FF), DEC_D ** -0.5, 0.25),
        "dec_up_bias": normal_values(key_list[18], (DEC_FF,), 0.5, 3.0),
        "dec_down": normal_values(key_list[19], (DEC_FF, DEC_D), DEC_FF ** -0.5, 0.125),
        "dec_pos": normal_values(key_list[20], (PATCHES, DEC_D), 1.0, 5.0),
    }


@jax.custom_vjp
def low(v):
    return lax.optimization_barrier(v.astype(jnp.bfloat16)).astype(jnp.float32)

@jax.custom_vjp
def low_back(v):
    return v

def low_keep(v):
    return (low(v), None)

def low_pass(kept, grad):
    return (grad,)

def back_keep(v):
    return (v, None)

def back_low(kept, grad):
    return (low(grad),)
low.defvjp(low_keep, low_pass)
low_back.defvjp(back_keep, back_low)

def product(left_side, right_side):
    return jnp.matmul(left_side, right_side, precision=lax.Precision.HIGHEST)

def layer_norm(hidden, scales, shifts):
    center = hidden - lax.optimization_barrier(jnp.mean(hidden, axis=-1, keepdims=True))
    spread = lax.optimization_barrier(jnp.mean(center * center, axis=-1, keepdims=True))
    return center * lax.rsqrt(spread + 1e-05) * scales + shifts

def block(hidden, norms, qkv_w, out_w, biases, up_w, up_bias, down_w):
    length = hidden.shape[0]
    head_count = qkv_w.shape[1] // (3 * HEAD_DIM)
    inner_width = head_count * HEAD_DIM
    normed = low(layer_norm(hidden, norms[0], norms[1]))
    packed = low(low_back(product(normed, qkv_w)))
    queries = packed[:, :inner_width].reshape(length, head_count, HEAD_DIM)
    keys_all = packed[:, inner_width:2 * inner_width].reshape(length, head_count, HEAD_DIM)
    values_all = packed[:, 2 * inner_width:].reshape(length, head_count, HEAD_DIM)
    scores = low_back(jnp.einsum('qhd,khd->hqk', queries, keys_all, precision=lax.Precision.HIGHEST) * HEAD_DIM ** (-0.5))
    probability = low(jax.nn.softmax(scores, axis=-1))
    attended = jnp.einsum('hqk,khd->qhd', probability, values_all, precision=lax.Precision.HIGHEST)
    attended = low(low_back(attended.reshape(length, inner_width)))
    middle = hidden + low_back(product(attended, out_w) + biases[0])
    second = low(layer_norm(middle, norms[2], norms[3]))
    lifted = low_back(product(second, up_w) + up_bias)
    active = low(jax.nn.gelu(lifted, approximate=False))
    return middle + low_back(product(active, down_w) + biases[1])

def image_forward(source, place, kind, weights):
    enc_norm, enc_qkv, enc_out, enc_bias, enc_up, enc_up_bias, enc_down, sensor_table, dec_embed, dec_norm, dec_qkv, dec_out, dec_bias, dec_up, dec_up_bias, dec_down, dec_pos = weights
    picks = (jnp.arange(SENSORS) == kind).astype(jnp.float32)
    start = source + lax.optimization_barrier(jnp.sum(picks[:, None] * sensor_table, axis=0))
    hidden = block(start, enc_norm, enc_qkv, enc_out, enc_bias, enc_up, enc_up_bias, enc_down)
    encoded = low(low_back(hidden))
    embedded = low_back(product(encoded, dec_embed) + dec_bias[0])
    filler = jnp.broadcast_to(dec_bias[3], (PATCHES - VISIBLE, DEC_D))
    sequence = jnp.concatenate([embedded, filler], axis=0)
    placed = jnp.zeros((PATCHES, DEC_D), jnp.float32).at[place].set(sequence) + dec_pos
    return block(placed, dec_norm, dec_qkv, dec_out, dec_bias[1:3], dec_up, dec_up_bias, dec_down)

def reference(tokens, order, sensor, cotangent, enc_norm, enc_qkv, enc_out, enc_bias, enc_up, enc_up_bias, enc_down, sensor_table, dec_embed, dec_norm, dec_qkv, dec_out, dec_bias, dec_up, dec_up_bias, dec_down, dec_pos):
    weights = tuple((item.astype(jnp.float32) for item in (enc_norm, enc_qkv, enc_out, enc_bias, enc_up, enc_up_bias, enc_down, sensor_table, dec_embed, dec_norm, dec_qkv, dec_out, dec_bias, dec_up, dec_up_bias, dec_down, dec_pos)))
    count = MICRO * IMAGES
    sources = tokens.reshape(count, VISIBLE, D).astype(jnp.float32)
    places = order.reshape(count, PATCHES).astype(jnp.int32)
    kinds = sensor.reshape(count).astype(jnp.int32)
    upstream = cotangent.reshape(count, PATCHES, DEC_D).astype(jnp.float32)

    def step(totals, item):
        source, place, kind, grad_out = item

        def inner_forward(source_in, weights_in):
            return image_forward(source_in, place, kind, weights_in)
        output, pull = jax.vjp(inner_forward, source, weights)
        grad_source, grad_weights = pull(grad_out)
        totals = jax.tree.map(jnp.add, totals, grad_weights)
        return (totals, (output, grad_source))
    zeros_init = tuple((jnp.zeros(item.shape, jnp.float32) for item in weights))
    totals, (outputs, grads) = lax.scan(step, zeros_init, (sources, places, kinds, upstream))
    decoded = outputs.reshape(MICRO, IMAGES, PATCHES, DEC_D)
    input_grad = grads.reshape(MICRO, IMAGES, VISIBLE, D)
    return (decoded, input_grad, totals[0], totals[1], totals[2], totals[3], totals[4], totals[5], totals[6], totals[7], totals[8], totals[9], totals[10], totals[11], totals[12], totals[13], totals[14], totals[15], totals[16])
```

```python
from functools import partial

import jax
import jax.numpy as jnp
from jax import lax
from jax.experimental import pallas as pl
from jax.experimental.pallas import tpu as pltpu
from jax.sharding import PartitionSpec as P

HEAD_DIM = 64
MESH = pl.DeviceIdType.MESH
SMALL_ROWS = 32


def layer_norm(hidden, scales, shifts):
    center = hidden - jnp.mean(hidden, axis=-1, keepdims=True)
    spread = jnp.mean(center * center, axis=-1, keepdims=True)
    return center * lax.rsqrt(spread + 1e-05) * scales + shifts


def matmul(left_side, right_side):
    return jnp.dot(left_side, right_side, preferred_element_type=jnp.float32)


def row_contract(left_side, right_side):
    return lax.dot_general(
        left_side, right_side, (((0,), (0,)), ((), ())), preferred_element_type=jnp.float32
    )


def col_contract(left_side, right_side):
    return lax.dot_general(
        left_side, right_side, (((1,), (1,)), ((), ())), preferred_element_type=jnp.float32
    )


def gelu_exact(values):
    return jax.nn.gelu(values, approximate=False)


def block_forward(hidden, weights):
    norms, qkv_w, out_w, biases, up_w, up_bias, down_w = weights
    batch_size, length, feature_width = hidden.shape
    row_count = batch_size * length
    head_count = qkv_w.shape[1] // (3 * HEAD_DIM)
    inner_width = head_count * HEAD_DIM
    norm_rows = norms.astype(jnp.float32)
    bias_rows = biases.astype(jnp.float32)
    normed = (
        layer_norm(hidden, norm_rows[0], norm_rows[1])
        .astype(jnp.bfloat16)
        .reshape(row_count, feature_width)
    )
    packed = (
        matmul(normed, qkv_w)
        .astype(jnp.bfloat16)
        .reshape(batch_size, length, 3, head_count, HEAD_DIM)
    )
    queries = packed[:, :, 0]
    keys_all = packed[:, :, 1]
    values_all = packed[:, :, 2]
    scores = jnp.einsum(
        "bqhd,bkhd->bhqk", queries, keys_all, preferred_element_type=jnp.float32
    ) * HEAD_DIM ** (-0.5)
    row_peak = jnp.max(scores, axis=-1, keepdims=True)
    logsum = row_peak + jnp.log(jnp.sum(jnp.exp(scores - row_peak), axis=-1, keepdims=True))
    probability = jnp.exp(scores - logsum).astype(jnp.bfloat16)
    attended = jnp.einsum(
        "bhqk,bkhd->bqhd", probability, values_all, preferred_element_type=jnp.float32
    )
    attended = attended.astype(jnp.bfloat16).reshape(row_count, inner_width)
    middle = hidden + (matmul(attended, out_w) + bias_rows[0]).reshape(
        batch_size, length, feature_width
    )
    second = (
        layer_norm(middle, norm_rows[2], norm_rows[3])
        .astype(jnp.bfloat16)
        .reshape(row_count, feature_width)
    )
    lifted = matmul(second, up_w) + up_bias.astype(jnp.float32)
    active = gelu_exact(lifted).astype(jnp.bfloat16)
    output = middle + (matmul(active, down_w) + bias_rows[1]).reshape(
        batch_size, length, feature_width
    )
    stored = (hidden, normed, packed, logsum, attended, middle, second, lifted, active)
    return (output, stored)


def block_backward(stored, upstream, weights):
    norms, qkv_w, out_w, biases, up_w, up_bias, down_w = weights
    hidden, normed, packed, logsum, attended, middle, second, lifted, active = stored
    batch_size, length, feature_width = hidden.shape
    row_count = batch_size * length
    head_count = qkv_w.shape[1] // (3 * HEAD_DIM)
    inner_width = head_count * HEAD_DIM
    score_scale = HEAD_DIM ** (-0.5)
    norm_rows = norms.astype(jnp.float32)
    branch_grad = upstream.reshape(row_count, feature_width).astype(jnp.bfloat16)
    grad_down = row_contract(active, branch_grad)
    grad_bias_down = jnp.sum(branch_grad.astype(jnp.float32), axis=0)
    grad_active = col_contract(branch_grad, down_w)
    grad_lifted = jax.vjp(gelu_exact, lifted)[1](grad_active)[0].astype(jnp.bfloat16)
    grad_up = row_contract(second, grad_lifted)
    grad_up_bias = jnp.sum(grad_lifted.astype(jnp.float32), axis=0)
    grad_second = col_contract(grad_lifted, up_w).reshape(batch_size, length, feature_width)
    grad_middle, grad_scale_two, grad_shift_two = jax.vjp(
        layer_norm, middle, norm_rows[2], norm_rows[3]
    )[1](grad_second)
    grad_middle = upstream + grad_middle
    attn_grad = grad_middle.reshape(row_count, feature_width).astype(jnp.bfloat16)
    grad_out = row_contract(attended, attn_grad)
    grad_bias_out = jnp.sum(attn_grad.astype(jnp.float32), axis=0)
    grad_attended = (
        col_contract(attn_grad, out_w)
        .astype(jnp.bfloat16)
        .reshape(batch_size, length, head_count, HEAD_DIM)
    )
    queries = packed[:, :, 0]
    keys_all = packed[:, :, 1]
    values_all = packed[:, :, 2]
    scores = (
        jnp.einsum("bqhd,bkhd->bhqk", queries, keys_all, preferred_element_type=jnp.float32)
        * score_scale
    )
    probability = jnp.exp(scores - logsum)
    grad_probs = jnp.einsum(
        "bqhd,bkhd->bhqk", grad_attended, values_all, preferred_element_type=jnp.float32
    )
    grad_values = jnp.einsum(
        "bhqk,bqhd->bkhd",
        probability.astype(jnp.bfloat16),
        grad_attended,
        preferred_element_type=jnp.float32,
    )
    row_dots = jnp.sum(grad_probs * probability, axis=-1, keepdims=True)
    grad_scores = (probability * (grad_probs - row_dots)).astype(jnp.bfloat16)
    grad_queries = (
        jnp.einsum("bhqk,bkhd->bqhd", grad_scores, keys_all, preferred_element_type=jnp.float32)
        * score_scale
    )
    grad_keys = (
        jnp.einsum("bhqk,bqhd->bkhd", grad_scores, queries, preferred_element_type=jnp.float32)
        * score_scale
    )
    grad_packed = (
        jnp.stack([grad_queries, grad_keys, grad_values], axis=2)
        .astype(jnp.bfloat16)
        .reshape(row_count, 3 * inner_width)
    )
    grad_qkv = row_contract(normed, grad_packed)
    grad_normed = col_contract(grad_packed, qkv_w).reshape(batch_size, length, feature_width)
    grad_hidden, grad_scale_one, grad_shift_one = jax.vjp(
        layer_norm, hidden, norm_rows[0], norm_rows[1]
    )[1](grad_normed)
    grad_hidden = grad_middle + grad_hidden
    grad_norms = jnp.stack([grad_scale_one, grad_shift_one, grad_scale_two, grad_shift_two])
    grad_biases = jnp.stack([grad_bias_out, grad_bias_down])
    return (
        grad_hidden,
        (grad_norms, grad_qkv, grad_out, grad_biases, grad_up, grad_up_bias, grad_down),
    )


def encode(tokens_part, sensor_part, enc_w):
    table = enc_w[7].astype(jnp.float32)
    picks = (sensor_part[:, None] == jnp.arange(table.shape[0])[None, :]).astype(jnp.float32)
    start = (
        tokens_part.astype(jnp.float32)
        + jnp.sum(picks[:, :, None] * table[None], axis=1)[:, None, :]
    )
    output, stored = block_forward(start, enc_w[:7])
    return (output.astype(jnp.bfloat16), stored, picks)


def encode_back(stored, picks, returned, enc_w):
    grad_input, grads = block_backward(stored, returned.astype(jnp.float32), enc_w[:7])
    grad_table = jnp.sum(picks[:, :, None] * jnp.sum(grad_input, axis=1)[:, None, :], axis=0)
    return (grad_input, grads + (grad_table,))


def decode(arrived, place, cotangent_part, dec_w):
    dec_embed, dec_norm, dec_qkv, dec_out, dec_bias, dec_up, dec_up_bias, dec_down, dec_pos = dec_w
    batch_size, visible, model_width = arrived.shape
    patches = place.shape[1]
    bias_rows = dec_bias.astype(jnp.float32)
    flat_rows = arrived.reshape(batch_size * visible, model_width)
    embedded = (matmul(flat_rows, dec_embed) + bias_rows[0]).reshape(
        batch_size, visible, bias_rows.shape[1]
    )
    filler = jnp.broadcast_to(bias_rows[3], (batch_size, patches - visible, bias_rows.shape[1]))
    sequence = jnp.concatenate([embedded, filler], axis=1)
    image_rows = jnp.arange(batch_size)[:, None]
    placed = jnp.zeros_like(sequence).at[image_rows, place].set(sequence) + dec_pos.astype(
        jnp.float32
    )
    block_w = (dec_norm, dec_qkv, dec_out, bias_rows[1:3], dec_up, dec_up_bias, dec_down)
    output, stored = block_forward(placed, block_w)
    grad_placed, grads = block_backward(stored, cotangent_part.astype(jnp.float32), block_w)
    grad_pos = jnp.sum(grad_placed, axis=0)
    grad_sequence = jnp.take_along_axis(grad_placed, place[:, :, None], axis=1)
    grad_embedded = (
        grad_sequence[:, :visible]
        .reshape(batch_size * visible, bias_rows.shape[1])
        .astype(jnp.bfloat16)
    )
    grad_filler = jnp.sum(grad_sequence[:, visible:], axis=(0, 1))
    grad_embed = row_contract(flat_rows, grad_embedded)
    grad_bias_embed = jnp.sum(grad_embedded.astype(jnp.float32), axis=0)
    returned = (
        col_contract(grad_embedded, dec_embed)
        .astype(jnp.bfloat16)
        .reshape(batch_size, visible, model_width)
    )
    grad_norms, grad_qkv, grad_out, grad_biases, grad_up, grad_up_bias, grad_down = grads
    grad_bias = jnp.stack([grad_bias_embed, grad_biases[0], grad_biases[1], grad_filler])
    return (
        output,
        returned,
        (
            grad_embed,
            grad_norms,
            grad_qkv,
            grad_out,
            grad_bias,
            grad_up,
            grad_up_bias,
            grad_down,
            grad_pos,
        ),
    )


CORE = -1


def partner_of(stage):
    section, data = lax.axis_index("section"), lax.axis_index("dp")
    if stage == CORE:
        return (1 - section, data)
    weight = 2**stage
    bit = lax.rem(data // weight, 2)
    return (section, data + weight * (1 - 2 * bit))


def bit_of(stage):
    if stage == CORE:
        return lax.axis_index("section")
    return lax.rem(lax.axis_index("dp") // 2**stage, 2)


def split_index(flat, count):
    return tuple(lax.rem(flat // 2 ** (count - 1 - place), 2) for place in range(count))


def greet(bits):
    barrier = pltpu.get_barrier_semaphore()
    stages = [CORE] + list(range(bits))
    for stage in stages:
        pl.semaphore_signal(barrier, inc=1, device_id=partner_of(stage), device_id_type=MESH)
    pl.semaphore_wait(barrier, len(stages))


class Chunk:
    def __init__(self, source, rows, cols, stages, lands, send_sems, recv_sems, result):
        self.source, self.rows, self.cols, self.stages = source, rows, cols, stages
        self.lands, self.send_sems, self.recv_sems = lands, send_sems, recv_sems
        self.result = result
        self.dims = list(range(len(stages) - 2, -1, -1))

    def halves(self, step):
        stage = self.stages[step]
        bit = bit_of(stage)
        if stage == CORE:
            width = self.source.shape[-1] // 2
            start, extent = self.cols

            def part(side):
                offset = pl.multiple_of(side * width + start, 128)
                return self.source.at[
                    (slice(None),) * len(self.dims)
                    + (pl.ds(self.rows[0], self.rows[1]), pl.ds(offset, extent))
                ]

            return part(1 - bit), part(bit)
        held = self.lands[step - 1]
        left = [item for item in self.dims if item not in self.stages[1:step]]
        place = left.index(stage)

        def part(side):
            return held.at[(slice(None),) * place + (side,)]

        return part(1 - bit), part(bit)

    def copy(self, step):
        return pltpu.make_async_remote_copy(
            src_ref=self.halves(step)[0],
            dst_ref=self.lands[step],
            send_sem=self.send_sems.at[step],
            recv_sem=self.recv_sems.at[step],
            device_id=partner_of(self.stages[step]),
            device_id_type=MESH,
        )

    def start(self, step):
        self.copy(step).start()

    def finish(self, step):
        self.copy(step).wait_recv()
        kept, land = self.halves(step)[1], self.lands[step]
        count = len(land.shape) - 2

        def add(flat, carry):
            index = split_index(flat, count)
            land[index] = land[index] + kept[index]
            return carry

        if count:
            lax.fori_loop(0, 2**count, add, 0)
            self.start(step + 1)
        else:
            self.result[pl.ds(*self.rows), pl.ds(*self.cols)] = land[...].astype(
                jnp.float32
            ) + kept[...].astype(jnp.float32)

    def close(self):
        for step in range(len(self.stages)):
            self.copy(step).wait_send()


class Whole:
    def __init__(self, source, bits, lands, send_sems, recv_sems, result):
        self.source, self.lands, self.send_sems, self.recv_sems = source, lands, send_sems, recv_sems
        self.stages = [CORE] + list(range(bits))
        self.result = result

    def held(self, step):
        return self.source if step == 0 else self.lands.at[step - 1]

    def copy(self, step):
        return pltpu.make_async_remote_copy(
            src_ref=self.held(step),
            dst_ref=self.lands.at[step],
            send_sem=self.send_sems.at[step],
            recv_sem=self.recv_sems.at[step],
            device_id=partner_of(self.stages[step]),
            device_id_type=MESH,
        )

    def start(self, step):
        self.copy(step).start()

    def finish(self, step):
        self.copy(step).wait_recv()
        total = self.lands[step] + self.held(step)[...]
        if step == len(self.stages) - 1:
            self.result[...] = total
        else:
            self.lands[step] = total
            self.start(step + 1)

    def close(self):
        for step in range(len(self.stages)):
            self.copy(step).wait_send()


class Flow:
    def __init__(self, steps, lag):
        self.steps, self.lag = steps, lag
        self.waves, self.tick_now = [], 0

    def add(self, chunks):
        for chunk in chunks:
            chunk.start(0)
        self.waves.append([chunks, 0, self.tick_now + 1])

    def tick(self):
        self.tick_now += 1
        for wave in self.waves:
            chunks, step, due = wave
            if step < self.steps and due <= self.tick_now:
                for chunk in chunks:
                    chunk.finish(step)
                wave[1], wave[2] = step + 1, self.tick_now + self.lag

    def drain(self):
        while any(wave[1] < self.steps for wave in self.waves):
            self.tick()
        for wave in self.waves:
            for chunk in wave[0]:
                chunk.close()


def orders_of(bits):
    rest = list(range(bits - 1, 1, -1))
    return [[CORE, 0, 1] + rest, [CORE, 1, 0] + rest]


def wave_plan(rows, width):
    area = rows * width
    if rows >= 64:
        parts = 4 if area > 64 * 1024 else 2
        cuts = [((rows // parts * item, rows // parts), (0, width)) for item in range(parts)]
    else:
        tiles = width // 128
        parts = min(4 if area > 64 * 1024 else 2, tiles)
        edges = [tiles * item // parts for item in range(parts + 1)]
        cuts = [
            ((0, rows), (128 * low, 128 * (high - low))) for low, high in zip(edges, edges[1:])
        ]
    return [cuts[item : item + 2] for item in range(0, len(cuts), 2)]


F32, BF16 = jnp.float32, jnp.bfloat16
BLOCK = 256
LANES = 256


def dot(left, right):
    return jnp.dot(left, right, preferred_element_type=F32)


def dot_nt(left, right):
    return lax.dot_general(left, right, (((1,), (1,)), ((), ())), preferred_element_type=F32)


def head_of_lane(rows, width=LANES):
    return lax.broadcasted_iota(jnp.int32, (rows, width), 1) // HEAD_DIM


def only_head(rows, head):
    lane = lax.broadcasted_iota(jnp.int32, rows.shape, 1)
    keep = (lane >= head * HEAD_DIM) & (lane < (head + 1) * HEAD_DIM)
    return jnp.where(keep, rows, jnp.zeros_like(rows))


def normalize(values):
    center = values - jnp.mean(values, axis=-1, keepdims=True)
    inverse = lax.rsqrt(jnp.mean(center * center, axis=-1, keepdims=True) + 1e-05)
    return center * inverse, inverse


def gelu_pair(values):
    area = 0.5 + 0.5 * lax.erf(values * 0.7071067811865476)
    slope = jnp.exp(values * values * -0.5) * 0.3989422804014327
    return values * area, area + values * slope


def softmax_columns(scores):
    peak = jnp.max(scores, axis=0, keepdims=True)
    raised = jnp.exp(scores - peak)
    return (raised * (1.0 / jnp.sum(raised, axis=0, keepdims=True))).astype(BF16)


class Loads:
    def __init__(self, sources, targets, sems):
        self.copies = [
            pltpu.make_async_copy(source, target, sems.at[item])
            for item, (source, target) in enumerate(zip(sources, targets))
        ]
        for copy in self.copies:
            copy.start()

    def wait(self, *items):
        for item in items:
            self.copies[item].wait()


def row(ref, index):
    return ref[pl.ds(index, 1), :].astype(F32)


def encode_kernel(
    sensor,
    tokens_hbm,
    norm,
    bias,
    up_bias,
    table,
    dec_bias,
    qkv_hbm,
    out_hbm,
    up_hbm,
    down_hbm,
    embed_hbm,
    start_out,
    normed_out,
    packed_out,
    probs_out,
    attended_out,
    middle_out,
    second_out,
    active_out,
    slope_out,
    encoded_out,
    embedded_out,
    tokens,
    qkv_w,
    out_w,
    up_w,
    down_w,
    embed_w,
    load_sems,
):
    part = lax.axis_index("section")
    loads = Loads(
        [tokens_hbm.at[part, 0], qkv_hbm, out_hbm, up_hbm, down_hbm, embed_hbm],
        [tokens, qkv_w, out_w, up_w, down_w, embed_w],
        load_sems,
    )
    inner = out_w.shape[0]
    kind = sensor[part, 0]
    added = jnp.zeros((1, table.shape[1]), F32)
    for item in range(table.shape[0]):
        added = added + jnp.where(kind == item, row(table, item), 0.0)
    loads.wait(0)
    start = tokens[...].astype(F32) + added
    start_out[...] = start
    normed = (normalize(start)[0] * row(norm, 0) + row(norm, 1)).astype(BF16)
    normed_out[...] = normed
    loads.wait(1)
    packed_out[...] = dot(normed, qkv_w[...]).astype(BF16)

    columns = []
    for group in range(inner // LANES):
        base = group * LANES
        queries = packed_out[:, base : base + LANES] * jnp.asarray(HEAD_DIM**-0.5, BF16)
        keys = packed_out[:, inner + base : inner + base + LANES]
        values = packed_out[:, 2 * inner + base : 2 * inner + base + LANES].T
        for head in range(LANES // HEAD_DIM):
            probs = softmax_columns(dot_nt(keys, only_head(queries, head)))
            probs_out[group * (LANES // HEAD_DIM) + head] = probs
            columns.append(dot(values[head * HEAD_DIM : (head + 1) * HEAD_DIM], probs).astype(BF16))
    attended = jnp.concatenate(columns, axis=0).T
    attended_out[...] = attended
    loads.wait(2)
    middle = start + (dot(attended, out_w[...]) + row(bias, 0))
    middle_out[...] = middle
    second = (normalize(middle)[0] * row(norm, 2) + row(norm, 3)).astype(BF16)
    second_out[...] = second
    loads.wait(3)
    total = middle + row(bias, 1)
    panel = 768
    for base in range(0, up_w.shape[1], panel):
        cols = slice(base, base + panel)
        lifted = dot(second, up_w[:, cols]) + up_bias[:, cols].astype(F32)
        active, slope = gelu_pair(lifted)
        active_out[:, cols] = active.astype(BF16)
        slope_out[:, cols] = slope.astype(BF16)
    loads.wait(4)
    encoded = (total + dot(active_out[...], down_w[...])).astype(BF16)
    encoded_out[...] = encoded
    loads.wait(5)
    embedded_out[...] = dot(encoded, embed_w[...]) + row(dec_bias, 0)


def decode_kernel(
    embedded,
    places_hbm,
    norm,
    bias,
    up_bias,
    pos_hbm,
    qkv_hbm,
    out_hbm,
    up_hbm,
    down_hbm,
    decoded_hbm,
    placed_hbm,
    normed_hbm,
    packed_hbm,
    probs_hbm,
    attended_hbm,
    middle_hbm,
    second_hbm,
    active_hbm,
    slope_hbm,
    places,
    pos,
    qkv_w,
    out_w,
    up_w,
    down_w,
    decoded,
    placed,
    normed,
    packed,
    probs,
    attended,
    middle,
    second,
    active,
    slope,
    values_t,
    load_sems,
    store_sems,
):
    part = lax.axis_index("section")
    loads = Loads(
        [places_hbm.at[part], pos_hbm, qkv_hbm, out_hbm, up_hbm, down_hbm],
        [places, pos, qkv_w, out_w, up_w, down_w],
        load_sems,
    )
    length = pos.shape[0]
    inner = out_w.shape[0]
    visible = embedded.shape[0]
    heads = inner // HEAD_DIM
    blocks = length // BLOCK
    high = embedded[...].astype(BF16)
    rest = (embedded[...] - high.astype(F32)).astype(BF16)
    loads.wait(0, 1, 2)
    spots = places[:, pl.ds(0, visible)]

    def first(block, carry):
        base = pl.multiple_of(block * BLOCK, BLOCK)
        rows = pl.ds(base, BLOCK)
        hit = lax.broadcasted_iota(jnp.int32, (BLOCK, visible), 0) + base == spots
        pick = jnp.where(hit, 1.0, 0.0).astype(BF16)
        seen = jnp.sum(jnp.where(hit, 1.0, 0.0), axis=1, keepdims=True)
        here = dot(pick, high) + dot(pick, rest) + (1.0 - seen) * row(bias, 3)
        here = here + pos[rows, :].astype(F32)
        placed[rows, :] = here
        norm_here = (normalize(here)[0] * row(norm, 0) + row(norm, 1)).astype(BF16)
        normed[rows, :] = norm_here
        packed[rows, :] = dot(norm_here, qkv_w[...]).astype(BF16)
        return carry

    lax.fori_loop(0, blocks, first, 0)
    stores = [
        pltpu.make_async_copy(source, target, store_sems.at[item])
        for item, (source, target) in enumerate(
            [(placed, placed_hbm), (normed, normed_hbm), (packed, packed_hbm)]
        )
    ]
    for copy in stores:
        copy.start()
    values_t[...] = packed[:, 2 * inner :].T
    loads.wait(3, 4, 5)
    bound = [
        (probs, probs_hbm, 0),
        (attended, attended_hbm, 1),
        (middle, middle_hbm, 1),
        (second, second_hbm, 1),
        (active, active_hbm, 1),
        (slope, slope_hbm, 1),
        (decoded, decoded_hbm, 1),
    ]

    def second_pass(block, carry):
        base = pl.multiple_of(block * BLOCK, BLOCK)
        rows = pl.ds(base, BLOCK)
        queries = packed[rows, :inner] * jnp.asarray(HEAD_DIM**-0.5, BF16)
        keys = packed[:, inner : 2 * inner]
        columns = []
        for head in range(heads):
            probs_here = softmax_columns(dot_nt(keys, only_head(queries, head)))
            probs[block, :, pl.ds(head * BLOCK, BLOCK)] = probs_here
            columns.append(
                dot(values_t[head * HEAD_DIM : (head + 1) * HEAD_DIM, :], probs_here).astype(BF16)
            )
        attended_here = jnp.concatenate(columns, axis=0).T
        attended[rows, :] = attended_here
        middle_here = placed[rows, :] + (dot(attended_here, out_w[...]) + row(bias, 1))
        middle[rows, :] = middle_here
        second_here = (normalize(middle_here)[0] * row(norm, 2) + row(norm, 3)).astype(BF16)
        second[rows, :] = second_here
        panel = 512
        for low in range(0, up_w.shape[1], panel):
            cols = slice(low, low + panel)
            lifted = dot(second_here, up_w[:, cols]) + up_bias[:, cols].astype(F32)
            active_here, slope_here = gelu_pair(lifted)
            active[rows, cols] = active_here.astype(BF16)
            slope[rows, cols] = slope_here.astype(BF16)
        decoded[rows, :] = middle_here + (dot(active[rows, :], down_w[...]) + row(bias, 2))
        for item, (source, target, by_rows) in enumerate(bound):
            spot = rows if by_rows else block
            pltpu.make_async_copy(
                source.at[spot], target.at[spot], store_sems.at[3 + item]
            ).start()
        return carry

    lax.fori_loop(0, blocks, second_pass, 0)
    for copy in stores:
        copy.wait()
    for item, (source, target, by_rows) in enumerate(bound):
        pltpu.make_async_copy(source, target, store_sems.at[3 + item]).wait()


WHOLE = pl.BlockSpec(memory_space=pltpu.VMEM)
APART = pl.BlockSpec(memory_space=pl.ANY)
SCALARS = pl.BlockSpec(memory_space=pltpu.SMEM)
LIMIT = pltpu.CompilerParams(vmem_limit_bytes=60 * 2**20)


def like(array):
    return pltpu.VMEM(array.shape, array.dtype)


def run_encode(tokens, sensor, enc_w, embed_w, dec_bias):
    norm, qkv_w, out_w, bias, up_w, up_bias, down_w, table = enc_w
    rows, width = tokens.shape[2:]
    inner, hidden = out_w.shape[0], up_w.shape[1]
    shaped = jax.ShapeDtypeStruct
    weights = [qkv_w, out_w, up_w, down_w, embed_w]
    return pl.pallas_call(
        encode_kernel,
        out_shape=[
            shaped((rows, width), F32),
            shaped((rows, width), BF16),
            shaped((rows, 3 * inner), BF16),
            shaped((inner // HEAD_DIM, rows, rows), BF16),
            shaped((rows, inner), BF16),
            shaped((rows, width), F32),
            shaped((rows, width), BF16),
            shaped((rows, hidden), BF16),
            shaped((rows, hidden), BF16),
            shaped((rows, width), BF16),
            shaped((rows, embed_w.shape[1]), F32),
        ],
        in_specs=[SCALARS, APART] + [WHOLE] * 5 + [APART] * 5,
        out_specs=[WHOLE] * 11,
        scratch_shapes=[pltpu.VMEM((rows, width), BF16)]
        + [like(item) for item in weights]
        + [pltpu.SemaphoreType.DMA((6,))],
        compiler_params=LIMIT,
        name="encode",
    )(sensor, tokens, norm, bias, up_bias.reshape(1, -1), table, dec_bias, *weights)


def run_decode(embedded, order, dec_w):
    embed_w, norm, qkv_w, out_w, bias, up_w, up_bias, down_w, pos = dec_w
    length, width = pos.shape
    inner, hidden = out_w.shape[0], up_w.shape[1]
    shaped = jax.ShapeDtypeStruct
    blocks, heads = length // BLOCK, inner // HEAD_DIM
    kept = [
        shaped((length, width), F32),
        shaped((length, width), F32),
        shaped((length, width), BF16),
        shaped((length, 3 * inner), BF16),
        shaped((blocks, length, heads * BLOCK), BF16),
        shaped((length, inner), BF16),
        shaped((length, width), F32),
        shaped((length, width), BF16),
        shaped((length, hidden), BF16),
        shaped((length, hidden), BF16),
    ]
    weights = [pos, qkv_w, out_w, up_w, down_w]
    return pl.pallas_call(
        decode_kernel,
        out_shape=kept,
        in_specs=[WHOLE, APART] + [WHOLE] * 3 + [APART] * 5,
        out_specs=[APART] * 10,
        scratch_shapes=[pltpu.VMEM((1, length), jnp.int32)]
        + [like(item) for item in weights + kept]
        + [
            pltpu.VMEM((inner, length), BF16),
            pltpu.SemaphoreType.DMA((6,)),
            pltpu.SemaphoreType.DMA((10,)),
        ],
        compiler_params=LIMIT,
        name="decode",
    )(embedded, order, norm, bias, up_bias.reshape(1, -1), *weights)


def column_sum(values):
    return jnp.sum(values, axis=0, keepdims=True)


def norm_back(grad, values, scale):
    normal, inverse = normalize(values)
    inner = grad * scale
    mean_inner = jnp.mean(inner, axis=-1, keepdims=True)
    mean_both = jnp.mean(inner * normal, axis=-1, keepdims=True)
    return (
        inverse * (inner - mean_inner - normal * mean_both),
        column_sum(grad * normal),
        column_sum(grad),
    )


def attention_back(queries, keys, values, keys_t, probs, grad_rows, attended):
    block = queries.shape[0]
    heads = LANES // HEAD_DIM
    product = (grad_rows.astype(F32) * attended.astype(F32)).T
    scores_back, query_grads = [], []
    for head in range(heads):
        lanes = slice(head * HEAD_DIM, (head + 1) * HEAD_DIM)
        probs_back = dot_nt(values, only_head(grad_rows, head))
        row_dots = column_sum(product[lanes])
        probs_here = probs[:, head * block : (head + 1) * block].astype(F32)
        scores_here = (probs_here * (probs_back - row_dots)).astype(BF16)
        scores_back.append(scores_here)
        query_grads.append(dot(keys_t[lanes], scores_here))
    stacked_grad = jnp.concatenate([only_head(grad_rows, head) for head in range(heads)], axis=0)
    stacked_queries = jnp.concatenate([only_head(queries, head) for head in range(heads)], axis=0)
    grad_values = dot(probs, stacked_grad)
    grad_keys = dot(jnp.concatenate(scores_back, axis=1), stacked_queries)
    grad_queries = jnp.concatenate(query_grads, axis=0).T
    return grad_queries, grad_keys, grad_values


class Plan:
    def __init__(self, bits, blocks):
        self.bits, self.steps = bits, bits + 1
        self.waves, self.cuts = [], []
        orders = orders_of(bits)
        for rows, width in blocks:
            waves = []
            for wave in wave_plan(rows, width):
                waves.append([])
                for which, (row_cut, col_cut) in enumerate(wave):
                    waves[-1].append((len(self.cuts), row_cut, col_cut, orders[which]))
                    self.cuts.append((row_cut[1], col_cut[1]))
            self.waves.append(waves)

    def scratch(self):
        lands = [
            pltpu.VMEM((2,) * (self.bits - step) + cut, BF16)
            for cut in self.cuts
            for step in range(self.steps)
        ]
        sems = pltpu.SemaphoreType.DMA((len(self.cuts), self.steps))
        return lands + [sems, sems]

    def scratch_count(self):
        return len(self.cuts) * self.steps + 2

    def bind(self, refs):
        self.refs = refs

    def chunks(self, slot, source, result):
        send_sems, recv_sems = self.refs[-2:]
        return [
            [
                Chunk(
                    source,
                    rows,
                    cols,
                    order,
                    self.refs[item * self.steps : (item + 1) * self.steps],
                    send_sems.at[item],
                    recv_sems.at[item],
                    result,
                )
                for item, rows, cols, order in wave
            ]
            for wave in self.waves[slot]
        ]


def fold(values, target):
    return values.astype(BF16).reshape(target.shape[:-1] + (values.shape[-1],))


def decode_back_kernel(plan, bits, *refs):
    (cotangent_hbm, places_hbm, norm, *refs) = refs
    load_hbm, refs = refs[:15], refs[15:]
    (returned, qkv_out, pos_out, embed_out, norm_sum, bias_sum, up_sum, *refs) = refs
    (down_done, up_done, out_done, *refs) = refs
    (cotangent, places, *refs) = refs
    load_vmem, refs = refs[:15], refs[15:]
    (
        active, down_w, slope, second, up_w, middle, attended, out_w, probs, packed,
        normed, placed, qkv_w, encoded, embed_w,
    ) = load_vmem
    (down_grad, up_grad, out_grad, grad_middle, attn_grad, grad_rows, grad_keys, grad_values,
     grad_packed, picked, load_sems, *refs) = refs
    plan.bind(refs)
    part = lax.axis_index("section")
    loads = Loads(
        [cotangent_hbm.at[part, 0], places_hbm.at[part], *load_hbm],
        [cotangent, places, *load_vmem],
        load_sems,
    )
    names = [
        "cotangent", "places", "active", "down_w", "slope", "second", "up_w", "middle", "attended",
        "out_w", "probs", "packed", "normed", "placed", "qkv_w", "encoded", "embed_w",
    ]

    def need(*wanted):
        loads.wait(*[names.index(item) for item in wanted])

    length, width = placed.shape
    inner, hidden = out_w.shape[0], up_w.shape[1]
    visible = encoded.shape[0]
    blocks = length // BLOCK
    greet(bits)
    flow = Flow(bits + 1, 2)

    def send(slot, source, result):
        for wave in plan.chunks(slot, source, result):
            flow.add(wave)

    need("cotangent", "active")
    panel = hidden // 4
    for item in range(4):
        cols = slice(item * panel, (item + 1) * panel)
        piece = dot(active[:, cols].T, cotangent[...]).astype(BF16)
        target = down_grad.at[item // 2, item % 2]
        target[...] = piece.reshape(target.shape)
    send(0, down_grad, down_done)
    bias_sum[0:1, :] = jnp.zeros((1, width), F32)
    bias_sum[2:3, :] = column_sum(cotangent[...].astype(F32))
    need("down_w", "slope", "up_w", "middle", "out_w", "second")
    for block in range(blocks):
        rows = slice(block * BLOCK, (block + 1) * BLOCK)
        branch = cotangent[rows, :]
        lifted_back = (dot_nt(branch, down_w[...]) * slope[rows, :].astype(F32)).astype(BF16)
        slope[rows, :] = lifted_back
        up_part = column_sum(lifted_back.astype(F32))
        grad_second = dot_nt(lifted_back, up_w[...])
        inward, scale_part, shift_part = norm_back(grad_second, middle[rows, :], row(norm, 2))
        total = branch.astype(F32) + inward
        grad_middle[rows, :] = total
        rounded = total.astype(BF16)
        attn_grad[rows, :] = rounded
        bias_part = column_sum(rounded.astype(F32))
        grad_rows[rows, :] = dot_nt(rounded, out_w[...]).astype(BF16)
        if block:
            up_part = up_part + up_sum[...]
            scale_part = scale_part + norm_sum[2:3, :]
            shift_part = shift_part + norm_sum[3:4, :]
            bias_part = bias_part + bias_sum[1:2, :]
        up_sum[...] = up_part
        norm_sum[2:3, :] = scale_part
        norm_sum[3:4, :] = shift_part
        bias_sum[1:2, :] = bias_part
        if block % 2:
            flow.tick()
    second_t = second[...].T
    for item in range(4):
        cols = slice(item * panel, (item + 1) * panel)
        up_grad[:, :, :, :, :, cols] = fold(dot(second_t, slope[:, cols]), up_grad)
    send(1, up_grad, up_done)
    need("attended")
    out_grad[...] = fold(dot(attended[...].T, attn_grad[...]), out_grad)
    send(2, out_grad, out_done)
    need("probs", "packed")
    keys = packed[:, inner : 2 * inner]
    values = packed[:, 2 * inner :]
    keys_t = keys.T
    scale = HEAD_DIM**-0.5
    for block in range(blocks):
        rows = slice(block * BLOCK, (block + 1) * BLOCK)
        query_part, key_part, value_part = attention_back(
            packed[rows, :inner], keys, values, keys_t, probs[block], grad_rows[rows, :],
            attended[rows, :],
        )
        grad_packed[rows, :inner] = (query_part * scale).astype(BF16)
        if block:
            key_part = key_part + grad_keys[...]
            value_part = value_part + grad_values[...]
        if block < blocks - 1:
            grad_keys[...] = key_part
            grad_values[...] = value_part
        else:
            grad_packed[:, inner : 2 * inner] = (key_part * scale).astype(BF16)
            grad_packed[:, 2 * inner :] = value_part.astype(BF16)
        flow.tick()
    need("normed", "placed", "qkv_w", "places")
    qkv_out[...] = fold(dot(normed[...].T, grad_packed[...]), qkv_out)
    flow.tick()
    spots = places[:, pl.ds(0, visible)]
    for block in range(blocks):
        rows = slice(block * BLOCK, (block + 1) * BLOCK)
        grad_normed = dot_nt(grad_packed[rows, :], qkv_w[...])
        inward, scale_part, shift_part = norm_back(grad_normed, placed[rows, :], row(norm, 0))
        total = grad_middle[rows, :] + inward
        hit = lax.broadcasted_iota(jnp.int32, (BLOCK, visible), 0) + block * BLOCK == spots
        pick = jnp.where(hit, 1.0, 0.0).astype(BF16)
        seen = jnp.sum(jnp.where(hit, 1.0, 0.0), axis=1, keepdims=True)
        fill_part = column_sum(total * (1.0 - seen))
        rounded = total.astype(BF16)
        pick_part = dot(pick.T, rounded)
        if block:
            scale_part = scale_part + norm_sum[0:1, :]
            shift_part = shift_part + norm_sum[1:2, :]
            fill_part = fill_part + bias_sum[3:4, :]
            pick_part = pick_part + picked[...]
        norm_sum[0:1, :] = scale_part
        norm_sum[1:2, :] = shift_part
        bias_sum[3:4, :] = fill_part
        picked[...] = pick_part
        pos_out[:, :, :, :, :, rows] = fold(rounded.T, pos_out)
        flow.tick()
    need("encoded", "embed_w")
    grad_embedded = picked[...].astype(BF16)
    bias_sum[0:1, :] = column_sum(picked[...])
    embed_out[...] = fold(dot(encoded[...].T, grad_embedded), embed_out)
    returned[...] = dot_nt(grad_embedded, embed_w[...]).astype(BF16)
    flow.drain()


def encode_back_kernel(plan, bits, *refs):
    (returned, kind, norm, dec_norm_sum, dec_bias_sum, dec_up_sum, *refs) = refs
    early, refs = refs[:3], refs[3:]
    load_hbm, refs = refs[:13], refs[13:]
    (input_grad, small_done, *refs) = refs
    done, refs = refs[:7], refs[7:]
    load_vmem, refs = refs[:13], refs[13:]
    (
        active, down_w, slope, second, up_w, middle, attended, out_w, probs, packed,
        normed, start, qkv_w,
    ) = load_vmem
    (down_grad, up_grad, out_grad, qkv_grad, grad_packed, small, small_lands, small_send,
     small_recv, load_sems, *refs) = refs
    plan.bind(refs)
    loads = Loads(load_hbm, load_vmem, load_sems)
    names = [
        "active", "down_w", "slope", "second", "up_w", "middle", "attended", "out_w", "probs",
        "packed", "normed", "start", "qkv_w",
    ]

    def need(*wanted):
        loads.wait(*[names.index(item) for item in wanted])

    inner, hidden = out_w.shape[0], up_w.shape[1]
    width = start.shape[1]
    greet(bits)
    flow = Flow(bits + 1, 2)

    def send(slot, source, result, part=None):
        waves = plan.chunks(slot, source, result)
        for wave in waves if part is None else waves[part : part + 1]:
            flow.add(wave)

    for slot, source in enumerate(early):
        send(slot, source, done[slot])
    branch = returned[...]
    small[...] = jnp.zeros_like(small)
    small[5:6, :] = column_sum(branch.astype(F32))
    need("active")
    panel = hidden // 4
    for item in range(4):
        cols = slice(item * panel, (item + 1) * panel)
        target = down_grad.at[item // 2, item % 2]
        target[...] = dot(active[:, cols].T, branch).astype(BF16).reshape(target.shape)
    flow.tick()
    send(3, down_grad, done[3], 0)
    need("second", "slope", "down_w")
    second_t = second[...].T
    for item in range(4):
        cols = slice(item * panel, (item + 1) * panel)
        lifted_back = (dot_nt(branch, down_w[cols, :]) * slope[:, cols].astype(F32)).astype(BF16)
        slope[:, cols] = lifted_back
        small[10 + item : 11 + item, :] = column_sum(lifted_back.astype(F32))
        up_grad[:, :, :, :, :, cols] = fold(dot(second_t, lifted_back), up_grad)
    flow.tick()
    send(3, down_grad, done[3], 1)
    need("up_w", "middle", "out_w", "attended")
    grad_second = dot_nt(slope[...], up_w[...])
    inward, small[2:3, :], small[3:4, :] = norm_back(grad_second, middle[...], row(norm, 2))
    grad_middle = branch.astype(F32) + inward
    attn_grad = grad_middle.astype(BF16)
    small[4:5, :] = column_sum(attn_grad.astype(F32))
    flow.tick()
    send(4, up_grad, done[4], 0)
    out_grad[...] = fold(dot(attended[...].T, attn_grad), out_grad)
    grad_rows = dot_nt(attn_grad, out_w[...]).astype(BF16)
    flow.tick()
    send(4, up_grad, done[4], 1)
    need("probs", "packed")
    scale = HEAD_DIM**-0.5
    heads = LANES // HEAD_DIM
    for group in range(inner // LANES):
        base = group * LANES
        lanes = slice(base, base + LANES)
        keys = packed[:, inner + base : inner + base + LANES]
        query_part, key_part, value_part = attention_back(
            packed[:, lanes],
            keys,
            packed[:, 2 * inner + base : 2 * inner + base + LANES],
            keys.T,
            jnp.concatenate([probs[group * heads + head] for head in range(heads)], axis=1),
            grad_rows[:, lanes],
            attended[:, lanes],
        )
        grad_packed[:, lanes] = (query_part * scale).astype(BF16)
        grad_packed[:, inner + base : inner + base + LANES] = (key_part * scale).astype(BF16)
        grad_packed[:, 2 * inner + base : 2 * inner + base + LANES] = value_part.astype(BF16)
    flow.tick()
    need("normed", "start", "qkv_w")
    send(5, out_grad, done[5])
    normed_t = normed[...].T
    for item in range(3):
        cols = slice(item * inner, (item + 1) * inner)
        qkv_grad[:, :, :, :, :, cols] = fold(dot(normed_t, grad_packed[:, cols]), qkv_grad)
    flow.tick()
    send(6, qkv_grad, done[6])
    grad_normed = dot_nt(grad_packed[...], qkv_w[...])
    inward, small[0:1, :], small[1:2, :] = norm_back(grad_normed, start[...], row(norm, 0))
    grad_start = grad_middle + inward
    input_grad[...] = grad_start
    kinds = lax.broadcasted_iota(jnp.int32, (4, 1), 0)
    mine = kind[pl.ds(lax.axis_index("section"), 1), :]
    small[6:10, :] = jnp.where(kinds == mine, 1.0, 0.0) * column_sum(grad_start)
    dec_width = dec_norm_sum.shape[1]
    small[14:18, :dec_width] = dec_norm_sum[...]
    small[18:22, :dec_width] = dec_bias_sum[...]
    for item in range(4):
        small[22 + item : 23 + item, :dec_width] = dec_up_sum[
            :, item * dec_width : (item + 1) * dec_width
        ]
    flow.add([Whole(small, bits, small_lands, small_send, small_recv, small_done)])
    flow.drain()


def communicating(number):
    return pltpu.CompilerParams(
        collective_id=number, has_side_effects=True, vmem_limit_bytes=63 * 2**20
    )


def blocked(rows, cols, bits):
    return (2,) * bits + (rows // 2**bits, cols)


def run_decode_back(cotangent, order, stored, encoded, dec_w, bits):
    embed_w, norm, qkv_w, out_w, bias, up_w, up_bias, down_w, pos = dec_w
    placed, normed, packed, probs, attended, middle, second, active, slope = stored
    length, width = pos.shape
    inner, hidden = out_w.shape[0], up_w.shape[1]
    shaped = jax.ShapeDtypeStruct
    loaded = [
        active, down_w, slope, second, up_w, middle, attended, out_w, probs, packed, normed,
        placed, qkv_w, encoded, embed_w,
    ]
    sent = [blocked(*item.shape, bits) for item in (down_w, up_w, out_w)]
    plan = Plan(bits, [(item[-2], item[-1] // 2) for item in sent])
    later = [blocked(*qkv_w.shape, bits), blocked(width, length, bits), blocked(*embed_w.shape, bits)]
    return pl.pallas_call(
        partial(decode_back_kernel, plan, bits),
        out_shape=[shaped(encoded.shape, BF16)]
        + [shaped(item, BF16) for item in later]
        + [shaped((4, width), F32), shaped((4, width), F32), shaped((1, hidden), F32)]
        + [shaped((item[-2], item[-1] // 2), F32) for item in sent],
        in_specs=[APART, APART, WHOLE] + [APART] * len(loaded),
        out_specs=[WHOLE] * 10,
        scratch_shapes=[
            pltpu.VMEM((length, width), BF16),
            pltpu.VMEM((1, length), jnp.int32),
        ]
        + [like(item) for item in loaded]
        + [pltpu.VMEM(item, BF16) for item in sent]
        + [
            pltpu.VMEM((length, width), F32),
            pltpu.VMEM((length, width), BF16),
            pltpu.VMEM((length, inner), BF16),
            pltpu.VMEM((length, inner), F32),
            pltpu.VMEM((length, inner), F32),
            pltpu.VMEM((length, 3 * inner), BF16),
            pltpu.VMEM((encoded.shape[0], width), F32),
            pltpu.SemaphoreType.DMA((len(loaded) + 2,)),
        ]
        + plan.scratch(),
        compiler_params=communicating(1),
        name="decode_back",
    )(cotangent, order, norm, *loaded)


def run_encode_back(returned, sensor, stored, enc_w, early, dec_sums, bits):
    norm, qkv_w, out_w, bias, up_w, up_bias, down_w, table = enc_w
    start, normed, packed, probs, attended, middle, second, active, slope = stored
    shaped = jax.ShapeDtypeStruct
    loaded = [
        active, down_w, slope, second, up_w, middle, attended, out_w, probs, packed, normed,
        start, qkv_w,
    ]
    own = [blocked(*item.shape, bits) for item in (down_w, up_w, out_w, qkv_w)]
    sent = [item.shape for item in early] + own
    plan = Plan(bits, [(item[-2], item[-1] // 2) for item in sent])
    width = start.shape[1]
    small = (SMALL_ROWS, width)
    return pl.pallas_call(
        partial(encode_back_kernel, plan, bits),
        out_shape=[shaped(start.shape, F32), shaped(small, F32)]
        + [shaped((item[-2], item[-1] // 2), F32) for item in sent],
        in_specs=[WHOLE] * 9 + [APART] * len(loaded),
        out_specs=[WHOLE] * 9,
        scratch_shapes=[like(item) for item in loaded]
        + [pltpu.VMEM(item, BF16) for item in own]
        + [
            pltpu.VMEM(packed.shape, BF16),
            pltpu.VMEM(small, F32),
            pltpu.VMEM((bits + 1,) + small, F32),
            pltpu.SemaphoreType.DMA((bits + 1,)),
            pltpu.SemaphoreType.DMA((bits + 1,)),
            pltpu.SemaphoreType.DMA((len(loaded),)),
        ]
        + plan.scratch(),
        compiler_params=communicating(2),
        name="encode_back",
    )(returned, sensor, norm, *dec_sums, *early, *loaded)


def local_rows(whole, shape):
    section, data = lax.axis_index("section"), lax.axis_index("dp")
    sections, datas = lax.axis_size("section"), lax.axis_size("dp")
    if len(shape) == 1:
        count = shape[0] // (sections * datas)
        return lax.dynamic_slice_in_dim(
            whole.reshape(-1)[: shape[0]], (section * datas + data) * count, count, 0
        )
    rows, cols = shape[0] // sections, shape[1] // datas
    return lax.dynamic_slice(whole, (section * rows, data * cols), (rows, cols))


def plain_shards(tokens, order, sensor, cotangent, enc_w, dec_w):
    section_count = lax.axis_size("section")
    section_index = lax.axis_index("section")
    half_count = tokens.shape[0] // section_count

    def mine(array):
        part = lax.dynamic_slice_in_dim(array, section_index * half_count, half_count, 0)
        return part.reshape((half_count * array.shape[1],) + array.shape[2:])

    encoded, stored, picks = encode(mine(tokens), mine(sensor), enc_w)
    output, returned, dec_grads = decode(encoded, mine(order), mine(cotangent), dec_w)
    grad_input, enc_grads = encode_back(stored, picks, returned, enc_w)
    done = []
    for slot, grad in enumerate(enc_grads + dec_grads):
        if slot in (0, 3, 5, 7, 9, 12, 14):
            total = local_rows(lax.psum(grad, ("section", "dp")), grad.shape)
        else:
            side = 0 if slot == 16 else 1
            total = lax.psum_scatter(
                grad.astype(jnp.bfloat16), "section", scatter_dimension=side, tiled=True
            )
            total = lax.psum_scatter(total, "dp", scatter_dimension=1 - side, tiled=True)
        done.append(total.astype(jnp.float32))
    decoded = output.reshape((half_count,) + cotangent.shape[1:])
    input_grad = grad_input.reshape((half_count,) + tokens.shape[1:])
    return (decoded, input_grad) + tuple(done)


def shards(tokens, order, sensor, cotangent, *weights):
    enc_w, dec_w = weights[:8], weights[8:]
    sections, datas = lax.axis_size("section"), lax.axis_size("dp")
    split_rows = [enc_w[1], enc_w[2], enc_w[4], enc_w[6], dec_w[0], dec_w[2], dec_w[3], dec_w[5]]
    fits = (
        sections == 2
        and tokens.shape[:2] == (sections, 1)
        and datas & (datas - 1) == 0
        and datas >= 4
        and all(item.shape[0] % (16 * datas) == 0 for item in split_rows)
    )
    if not fits:
        return plain_shards(tokens, order, sensor, cotangent, enc_w, dec_w)
    bits = datas.bit_length() - 1
    *enc_kept, encoded, embedded = run_encode(tokens, sensor, enc_w, dec_w[0], dec_w[4])
    decoded, *dec_kept = run_decode(embedded, order, dec_w)
    back = run_decode_back(cotangent, order, dec_kept, encoded, dec_w, bits)
    returned, early, dec_sums, dec_done = back[0], back[1:4], back[4:7], back[7:]
    input_grad, small, *rest = run_encode_back(
        returned, sensor, enc_kept, enc_w, early, dec_sums, bits
    )
    qkv_dec, pos, embed, down, up, out, qkv = rest
    width, dec_width = enc_w[0].shape[1], dec_w[1].shape[1]

    def tiny(first, count, shape, cols):
        return local_rows(small[first : first + count, :cols], shape)

    done = (
        tiny(0, 4, enc_w[0].shape, width),
        qkv,
        out,
        tiny(4, 2, enc_w[3].shape, width),
        up,
        tiny(10, 4, enc_w[5].shape, width),
        down,
        tiny(6, 4, enc_w[7].shape, width),
        embed,
        tiny(14, 4, dec_w[1].shape, dec_width),
        qkv_dec,
        dec_done[2],
        tiny(18, 4, dec_w[4].shape, dec_width),
        dec_done[1],
        tiny(22, 4, dec_w[6].shape, dec_width),
        dec_done[0],
        pos.T,
    )
    return (decoded[None, None], input_grad[None, None]) + done


def solution(mesh):
    placed = (
        P(None, "dp", None, None),
        P(None, "dp", None),
        P(None, "dp"),
        P(None, "dp", None, None),
        P(),
        P(),
        P(),
        P(),
        P(),
        P(),
        P(),
        P(),
        P(),
        P(),
        P(),
        P(),
        P(),
        P(),
        P(),
        P(),
        P(),
    )
    return jax.shard_map(
        shards,
        mesh=mesh,
        in_specs=placed,
        out_specs=(
            P("section", "dp", None, None),
            P("section", "dp", None, None),
            P("section", "dp"),
            P("dp", "section"),
            P("dp", "section"),
            P("section", "dp"),
            P("dp", "section"),
            P(("section", "dp")),
            P("dp", "section"),
            P("section", "dp"),
            P("dp", "section"),
            P("section", "dp"),
            P("dp", "section"),
            P("dp", "section"),
            P("section", "dp"),
            P("dp", "section"),
            P(("section", "dp")),
            P("dp", "section"),
            P("section", "dp"),
        ),
        check_vma=False,
    )
```

```python
from functools import partial

import jax
import jax.numpy as jnp
from jax import lax
from jax.experimental import pallas as pl
from jax.experimental.pallas import tpu as pltpu
from jax.sharding import PartitionSpec as P

HEAD_DIM = 64
MESH = pl.DeviceIdType.MESH
SMALL_ROWS = 32


def layer_norm(hidden, scales, shifts):
    center = hidden - jnp.mean(hidden, axis=-1, keepdims=True)
    spread = jnp.mean(center * center, axis=-1, keepdims=True)
    return center * lax.rsqrt(spread + 1e-05) * scales + shifts


def matmul(left_side, right_side):
    return jnp.dot(left_side, right_side, preferred_element_type=jnp.float32)


def row_contract(left_side, right_side):
    return lax.dot_general(
        left_side, right_side, (((0,), (0,)), ((), ())), preferred_element_type=jnp.float32
    )


def col_contract(left_side, right_side):
    return lax.dot_general(
        left_side, right_side, (((1,), (1,)), ((), ())), preferred_element_type=jnp.float32
    )


def gelu_exact(values):
    return jax.nn.gelu(values, approximate=False)


def block_forward(hidden, weights):
    norms, qkv_w, out_w, biases, up_w, up_bias, down_w = weights
    batch_size, length, feature_width = hidden.shape
    row_count = batch_size * length
    head_count = qkv_w.shape[1] // (3 * HEAD_DIM)
    inner_width = head_count * HEAD_DIM
    norm_rows = norms.astype(jnp.float32)
    bias_rows = biases.astype(jnp.float32)
    normed = (
        layer_norm(hidden, norm_rows[0], norm_rows[1])
        .astype(jnp.bfloat16)
        .reshape(row_count, feature_width)
    )
    packed = (
        matmul(normed, qkv_w)
        .astype(jnp.bfloat16)
        .reshape(batch_size, length, 3, head_count, HEAD_DIM)
    )
    queries = packed[:, :, 0]
    keys_all = packed[:, :, 1]
    values_all = packed[:, :, 2]
    scores = jnp.einsum(
        "bqhd,bkhd->bhqk", queries, keys_all, preferred_element_type=jnp.float32
    ) * HEAD_DIM ** (-0.5)
    row_peak = jnp.max(scores, axis=-1, keepdims=True)
    logsum = row_peak + jnp.log(jnp.sum(jnp.exp(scores - row_peak), axis=-1, keepdims=True))
    probability = jnp.exp(scores - logsum).astype(jnp.bfloat16)
    attended = jnp.einsum(
        "bhqk,bkhd->bqhd", probability, values_all, preferred_element_type=jnp.float32
    )
    attended = attended.astype(jnp.bfloat16).reshape(row_count, inner_width)
    middle = hidden + (matmul(attended, out_w) + bias_rows[0]).reshape(
        batch_size, length, feature_width
    )
    second = (
        layer_norm(middle, norm_rows[2], norm_rows[3])
        .astype(jnp.bfloat16)
        .reshape(row_count, feature_width)
    )
    lifted = matmul(second, up_w) + up_bias.astype(jnp.float32)
    active = gelu_exact(lifted).astype(jnp.bfloat16)
    output = middle + (matmul(active, down_w) + bias_rows[1]).reshape(
        batch_size, length, feature_width
    )
    stored = (hidden, normed, packed, logsum, attended, middle, second, lifted, active)
    return (output, stored)


def block_backward(stored, upstream, weights):
    norms, qkv_w, out_w, biases, up_w, up_bias, down_w = weights
    hidden, normed, packed, logsum, attended, middle, second, lifted, active = stored
    batch_size, length, feature_width = hidden.shape
    row_count = batch_size * length
    head_count = qkv_w.shape[1] // (3 * HEAD_DIM)
    inner_width = head_count * HEAD_DIM
    score_scale = HEAD_DIM ** (-0.5)
    norm_rows = norms.astype(jnp.float32)
    branch_grad = upstream.reshape(row_count, feature_width).astype(jnp.bfloat16)
    grad_down = row_contract(active, branch_grad)
    grad_bias_down = jnp.sum(branch_grad.astype(jnp.float32), axis=0)
    grad_active = col_contract(branch_grad, down_w)
    grad_lifted = jax.vjp(gelu_exact, lifted)[1](grad_active)[0].astype(jnp.bfloat16)
    grad_up = row_contract(second, grad_lifted)
    grad_up_bias = jnp.sum(grad_lifted.astype(jnp.float32), axis=0)
    grad_second = col_contract(grad_lifted, up_w).reshape(batch_size, length, feature_width)
    grad_middle, grad_scale_two, grad_shift_two = jax.vjp(
        layer_norm, middle, norm_rows[2], norm_rows[3]
    )[1](grad_second)
    grad_middle = upstream + grad_middle
    attn_grad = grad_middle.reshape(row_count, feature_width).astype(jnp.bfloat16)
    grad_out = row_contract(attended, attn_grad)
    grad_bias_out = jnp.sum(attn_grad.astype(jnp.float32), axis=0)
    grad_attended = (
        col_contract(attn_grad, out_w)
        .astype(jnp.bfloat16)
        .reshape(batch_size, length, head_count, HEAD_DIM)
    )
    queries = packed[:, :, 0]
    keys_all = packed[:, :, 1]
    values_all = packed[:, :, 2]
    scores = (
        jnp.einsum("bqhd,bkhd->bhqk", queries, keys_all, preferred_element_type=jnp.float32)
        * score_scale
    )
    probability = jnp.exp(scores - logsum)
    grad_probs = jnp.einsum(
        "bqhd,bkhd->bhqk", grad_attended, values_all, preferred_element_type=jnp.float32
    )
    grad_values = jnp.einsum(
        "bhqk,bqhd->bkhd",
        probability.astype(jnp.bfloat16),
        grad_attended,
        preferred_element_type=jnp.float32,
    )
    row_dots = jnp.sum(grad_probs * probability, axis=-1, keepdims=True)
    grad_scores = (probability * (grad_probs - row_dots)).astype(jnp.bfloat16)
    grad_queries = (
        jnp.einsum("bhqk,bkhd->bqhd", grad_scores, keys_all, preferred_element_type=jnp.float32)
        * score_scale
    )
    grad_keys = (
        jnp.einsum("bhqk,bqhd->bkhd", grad_scores, queries, preferred_element_type=jnp.float32)
        * score_scale
    )
    grad_packed = (
        jnp.stack([grad_queries, grad_keys, grad_values], axis=2)
        .astype(jnp.bfloat16)
        .reshape(row_count, 3 * inner_width)
    )
    grad_qkv = row_contract(normed, grad_packed)
    grad_normed = col_contract(grad_packed, qkv_w).reshape(batch_size, length, feature_width)
    grad_hidden, grad_scale_one, grad_shift_one = jax.vjp(
        layer_norm, hidden, norm_rows[0], norm_rows[1]
    )[1](grad_normed)
    grad_hidden = grad_middle + grad_hidden
    grad_norms = jnp.stack([grad_scale_one, grad_shift_one, grad_scale_two, grad_shift_two])
    grad_biases = jnp.stack([grad_bias_out, grad_bias_down])
    return (
        grad_hidden,
        (grad_norms, grad_qkv, grad_out, grad_biases, grad_up, grad_up_bias, grad_down),
    )


def encode(tokens_part, sensor_part, enc_w):
    table = enc_w[7].astype(jnp.float32)
    picks = (sensor_part[:, None] == jnp.arange(table.shape[0])[None, :]).astype(jnp.float32)
    start = (
        tokens_part.astype(jnp.float32)
        + jnp.sum(picks[:, :, None] * table[None], axis=1)[:, None, :]
    )
    output, stored = block_forward(start, enc_w[:7])
    return (output.astype(jnp.bfloat16), stored, picks)


def encode_back(stored, picks, returned, enc_w):
    grad_input, grads = block_backward(stored, returned.astype(jnp.float32), enc_w[:7])
    grad_table = jnp.sum(picks[:, :, None] * jnp.sum(grad_input, axis=1)[:, None, :], axis=0)
    return (grad_input, grads + (grad_table,))


def decode(arrived, place, cotangent_part, dec_w):
    dec_embed, dec_norm, dec_qkv, dec_out, dec_bias, dec_up, dec_up_bias, dec_down, dec_pos = dec_w
    batch_size, visible, model_width = arrived.shape
    patches = place.shape[1]
    bias_rows = dec_bias.astype(jnp.float32)
    flat_rows = arrived.reshape(batch_size * visible, model_width)
    embedded = (matmul(flat_rows, dec_embed) + bias_rows[0]).reshape(
        batch_size, visible, bias_rows.shape[1]
    )
    filler = jnp.broadcast_to(bias_rows[3], (batch_size, patches - visible, bias_rows.shape[1]))
    sequence = jnp.concatenate([embedded, filler], axis=1)
    image_rows = jnp.arange(batch_size)[:, None]
    placed = jnp.zeros_like(sequence).at[image_rows, place].set(sequence) + dec_pos.astype(
        jnp.float32
    )
    block_w = (dec_norm, dec_qkv, dec_out, bias_rows[1:3], dec_up, dec_up_bias, dec_down)
    output, stored = block_forward(placed, block_w)
    grad_placed, grads = block_backward(stored, cotangent_part.astype(jnp.float32), block_w)
    grad_pos = jnp.sum(grad_placed, axis=0)
    grad_sequence = jnp.take_along_axis(grad_placed, place[:, :, None], axis=1)
    grad_embedded = (
        grad_sequence[:, :visible]
        .reshape(batch_size * visible, bias_rows.shape[1])
        .astype(jnp.bfloat16)
    )
    grad_filler = jnp.sum(grad_sequence[:, visible:], axis=(0, 1))
    grad_embed = row_contract(flat_rows, grad_embedded)
    grad_bias_embed = jnp.sum(grad_embedded.astype(jnp.float32), axis=0)
    returned = (
        col_contract(grad_embedded, dec_embed)
        .astype(jnp.bfloat16)
        .reshape(batch_size, visible, model_width)
    )
    grad_norms, grad_qkv, grad_out, grad_biases, grad_up, grad_up_bias, grad_down = grads
    grad_bias = jnp.stack([grad_bias_embed, grad_biases[0], grad_biases[1], grad_filler])
    return (
        output,
        returned,
        (
            grad_embed,
            grad_norms,
            grad_qkv,
            grad_out,
            grad_bias,
            grad_up,
            grad_up_bias,
            grad_down,
            grad_pos,
        ),
    )


CORE = -1


def partner_of(stage):
    section, data = lax.axis_index("section"), lax.axis_index("dp")
    if stage == CORE:
        return (1 - section, data)
    weight = 2**stage
    bit = lax.rem(data // weight, 2)
    return (section, data + weight * (1 - 2 * bit))


def bit_of(stage):
    if stage == CORE:
        return lax.axis_index("section")
    return lax.rem(lax.axis_index("dp") // 2**stage, 2)


def split_index(flat, count):
    return tuple(lax.rem(flat // 2 ** (count - 1 - place), 2) for place in range(count))


def greet(bits):
    barrier = pltpu.get_barrier_semaphore()
    stages = [CORE] + list(range(bits))
    for stage in stages:
        pl.semaphore_signal(barrier, inc=1, device_id=partner_of(stage), device_id_type=MESH)
    pl.semaphore_wait(barrier, len(stages))


class Chunk:
    def __init__(self, source, rows, cols, stages, lands, send_sems, recv_sems, result):
        self.source, self.rows, self.cols, self.stages = source, rows, cols, stages
        self.lands, self.send_sems, self.recv_sems = lands, send_sems, recv_sems
        self.result = result
        self.dims = list(range(len(stages) - 2, -1, -1))

    def halves(self, step):
        stage = self.stages[step]
        bit = bit_of(stage)
        if stage == CORE:
            width = self.source.shape[-1] // 2
            start, extent = self.cols

            def part(side):
                offset = pl.multiple_of(side * width + start, 128)
                return self.source.at[
                    (slice(None),) * len(self.dims)
                    + (pl.ds(self.rows[0], self.rows[1]), pl.ds(offset, extent))
                ]

            return part(1 - bit), part(bit)
        held = self.lands[step - 1]
        left = [item for item in self.dims if item not in self.stages[1:step]]
        place = left.index(stage)

        def part(side):
            return held.at[(slice(None),) * place + (side,)]

        return part(1 - bit), part(bit)

    def copy(self, step):
        return pltpu.make_async_remote_copy(
            src_ref=self.halves(step)[0],
            dst_ref=self.lands[step],
            send_sem=self.send_sems.at[step],
            recv_sem=self.recv_sems.at[step],
            device_id=partner_of(self.stages[step]),
            device_id_type=MESH,
        )

    def start(self, step):
        self.copy(step).start()

    def finish(self, step):
        self.copy(step).wait_recv()
        kept, land = self.halves(step)[1], self.lands[step]
        count = len(land.shape) - 2

        def add(flat, carry):
            index = split_index(flat, count)
            land[index] = land[index] + kept[index]
            return carry

        if count:
            lax.fori_loop(0, 2**count, add, 0)
            self.start(step + 1)
        else:
            self.result[pl.ds(*self.rows), pl.ds(*self.cols)] = land[...].astype(
                jnp.float32
            ) + kept[...].astype(jnp.float32)

    def close(self):
        for step in range(len(self.stages)):
            self.copy(step).wait_send()


class Whole:
    def __init__(self, source, bits, lands, send_sems, recv_sems, result):
        self.source, self.lands, self.send_sems, self.recv_sems = source, lands, send_sems, recv_sems
        self.stages = [CORE] + list(range(bits))
        self.result = result

    def held(self, step):
        return self.source if step == 0 else self.lands.at[step - 1]

    def copy(self, step):
        return pltpu.make_async_remote_copy(
            src_ref=self.held(step),
            dst_ref=self.lands.at[step],
            send_sem=self.send_sems.at[step],
            recv_sem=self.recv_sems.at[step],
            device_id=partner_of(self.stages[step]),
            device_id_type=MESH,
        )

    def start(self, step):
        self.copy(step).start()

    def finish(self, step):
        self.copy(step).wait_recv()
        total = self.lands[step] + self.held(step)[...]
        if step == len(self.stages) - 1:
            self.result[...] = total
        else:
            self.lands[step] = total
            self.start(step + 1)

    def close(self):
        for step in range(len(self.stages)):
            self.copy(step).wait_send()


class Flow:
    def __init__(self, steps, lag):
        self.steps, self.lag = steps, lag
        self.waves, self.tick_now = [], 0

    def add(self, chunks):
        for chunk in chunks:
            chunk.start(0)
        self.waves.append([chunks, 0, self.tick_now + 1])

    def tick(self):
        self.tick_now += 1
        for wave in self.waves:
            chunks, step, due = wave
            if step < self.steps and due <= self.tick_now:
                for chunk in chunks:
                    chunk.finish(step)
                wave[1], wave[2] = step + 1, self.tick_now + self.lag

    def drain(self):
        while any(wave[1] < self.steps for wave in self.waves):
            self.tick()
        for wave in self.waves:
            for chunk in wave[0]:
                chunk.close()


def orders_of(bits):
    near = bits // 3
    x, y, z = list(range(near)), list(range(near, 2 * near)), list(range(2 * near, bits))
    return [
        ([CORE] + x + y + z, (0.5, 0.25, 0.1875)),
        ([CORE] + y + x + z, (0.25, 0.5, 0.1875)),
        ([CORE] + z + x + y, (0.125, 0.0625, 0.75)),
        ([CORE] + z + y + x, (0.0625, 0.125, 0.75)),
    ]


def wave_plan(rows, width, orders, loads):
    by_rows = rows >= 128
    unit = 16 if by_rows else 128
    strips = (rows if by_rows else width) // unit
    count = 2 if rows * width > 48 * 1024 else 1
    waves = []
    for item in range(count):
        low, high = strips * item // count, strips * (item + 1) // count
        taken = []
        for _ in range(low, high):
            totals = [
                [old + new * rows * width / strips for old, new in zip(loads, cost)]
                for _, cost in orders
            ]
            best = min(range(len(orders)), key=lambda which: max(totals[which]))
            loads[:] = totals[best]
            taken.append(best)
        wave = []
        for which in sorted(set(taken)):
            extent = taken.count(which)
            cut = (low * unit, extent * unit)
            low += extent
            wave.append((cut, (0, width), which) if by_rows else ((0, rows), cut, which))
        waves.append(wave)
    return waves


F32, BF16 = jnp.float32, jnp.bfloat16
BLOCK = 256
LANES = 256


def dot(left, right):
    return jnp.dot(left, right, preferred_element_type=F32)


def dot_nt(left, right):
    return lax.dot_general(left, right, (((1,), (1,)), ((), ())), preferred_element_type=F32)


def head_of_lane(rows, width=LANES):
    return lax.broadcasted_iota(jnp.int32, (rows, width), 1) // HEAD_DIM


def only_head(rows, head):
    lane = lax.broadcasted_iota(jnp.int32, rows.shape, 1)
    keep = (lane >= head * HEAD_DIM) & (lane < (head + 1) * HEAD_DIM)
    return jnp.where(keep, rows, jnp.zeros_like(rows))


def normalize(values):
    center = values - jnp.mean(values, axis=-1, keepdims=True)
    inverse = lax.rsqrt(jnp.mean(center * center, axis=-1, keepdims=True) + 1e-05)
    return center * inverse, inverse


def gelu_pair(values):
    area = 0.5 + 0.5 * lax.erf(values * 0.7071067811865476)
    slope = jnp.exp(values * values * -0.5) * 0.3989422804014327
    return values * area, area + values * slope


def softmax_columns(scores):
    peak = jnp.max(scores, axis=0, keepdims=True)
    raised = jnp.exp(scores - peak)
    return (raised * (1.0 / jnp.sum(raised, axis=0, keepdims=True))).astype(BF16)


def staggered(items, produce, consume):
    held = None
    for item in items:
        made = produce(item)
        if held is not None:
            consume(*held)
        held = (item, made)
    consume(*held)


class Loads:
    def __init__(self, sources, targets, sems, ahead):
        self.copies = [
            pltpu.make_async_copy(source, target, sems.at[item])
            for item, (source, target) in enumerate(zip(sources, targets))
        ]
        self.ahead, self.started = ahead, 0
        self.reach(ahead)

    def reach(self, count):
        for copy in self.copies[self.started : count]:
            copy.start()
        self.started = max(self.started, min(count, len(self.copies)))

    def wait(self, *items):
        for item in items:
            self.reach(item + 1 + self.ahead)
            self.copies[item].wait()


class Stores:
    def __init__(self, sems):
        self.sems, self.copies = sems, []

    def send(self, source, target):
        copy = pltpu.make_async_copy(source, target, self.sems.at[len(self.copies)])
        copy.start()
        self.copies.append(copy)

    def close(self):
        for copy in self.copies:
            copy.wait()


def row(ref, index):
    return ref[pl.ds(index, 1), :].astype(F32)


def forward_kernel(*refs):
    (sensor, norm, bias, up_bias, table, dec_norm, dec_bias, dec_up_bias, *refs) = refs
    load_hbm, refs = refs[:12], refs[12:]
    store_hbm, refs = refs[:20], refs[20:]
    load_vmem, refs = refs[:12], refs[12:]
    (
        tokens, qkv_w, out_w, up_w, down_w, embed_w, places, pos, dec_qkv_w, dec_out_w, dec_up_w,
        dec_down_w,
    ) = load_vmem
    enc_kept, dec_kept = refs[:10], refs[10:19]
    (decoded, embedded, values_t, load_sems, store_sems, block_sems, decoded_sems) = refs[19:]
    part = lax.axis_index("section")
    sources = list(load_hbm)
    sources[0] = sources[0].at[part, 0]
    sources[6] = sources[6].at[part]
    loads = Loads(sources, load_vmem, load_sems, 3)
    stores = Stores(store_sems)
    encode_rows(
        loads, stores, enc_kept, store_hbm[:10], tokens, sensor[part, 0], norm, bias, up_bias, table,
        qkv_w, out_w, up_w, down_w,
    )
    loads.wait(5)
    embedded[...] = dot(enc_kept[-1][...], embed_w[...]) + row(dec_bias, 0)
    loads.wait(6, 7, 8)
    decode_rows(
        loads, stores, dec_kept, store_hbm[10:], embedded, places, pos, dec_norm, dec_bias,
        dec_up_bias, dec_qkv_w, dec_out_w, dec_up_w, dec_down_w, decoded, values_t, block_sems,
        decoded_sems,
    )
    stores.close()


def encode_rows(
    loads, stores, kept, kept_hbm, tokens, kind, norm, bias, up_bias, table, qkv_w, out_w, up_w, down_w
):
    start_out, normed_out, packed, probs_out, attended_out, middle_out, second_out, active, slopes, encoded = kept

    def keep(item):
        stores.send(kept[item], kept_hbm[item])

    inner = out_w.shape[0]
    added = jnp.zeros((1, table.shape[1]), F32)
    for item in range(table.shape[0]):
        added = added + jnp.where(kind == item, row(table, item), 0.0)
    loads.wait(0)
    start = tokens[...].astype(F32) + added
    start_out[...] = start
    keep(0)
    normed = (normalize(start)[0] * row(norm, 0) + row(norm, 1)).astype(BF16)
    normed_out[...] = normed
    keep(1)
    loads.wait(1)
    packed[...] = dot(normed, qkv_w[...]).astype(BF16)
    keep(2)
    columns = []
    heads = LANES // HEAD_DIM
    for group in range(inner // LANES):
        base = group * LANES
        queries = packed[:, base : base + LANES] * jnp.asarray(HEAD_DIM**-0.5, BF16)
        keys = packed[:, inner + base : inner + base + LANES]
        values = packed[:, 2 * inner + base : 2 * inner + base + LANES].T

        def weigh(head, scores, group=group, values=values):
            probs = softmax_columns(scores)
            probs_out[group * heads + head] = probs
            columns.append(dot(values[head * HEAD_DIM : (head + 1) * HEAD_DIM], probs).astype(BF16))

        staggered(
            range(heads),
            lambda head, keys=keys, queries=queries: dot_nt(keys, only_head(queries, head)),
            weigh,
        )
    keep(3)
    attended = jnp.concatenate(columns, axis=0).T
    attended_out[...] = attended
    keep(4)
    loads.wait(2)
    middle = start + (dot(attended, out_w[...]) + row(bias, 0))
    middle_out[...] = middle
    keep(5)
    second = (normalize(middle)[0] * row(norm, 2) + row(norm, 3)).astype(BF16)
    second_out[...] = second
    keep(6)
    loads.wait(3)
    panel = 768

    def bend(low, lifted):
        cols = slice(low, low + panel)
        raised, slope = gelu_pair(lifted + up_bias[:, cols].astype(F32))
        active[:, cols] = raised.astype(BF16)
        slopes[:, cols] = slope.astype(BF16)

    staggered(
        range(0, up_w.shape[1], panel), lambda low: dot(second, up_w[:, low : low + panel]), bend
    )
    keep(7)
    keep(8)
    loads.wait(4)
    encoded[...] = (middle + row(bias, 1) + dot(active[...], down_w[...])).astype(BF16)
    keep(9)


def decode_rows(
    loads, stores, kept, kept_hbm, embedded, places, pos, norm, bias, up_bias, qkv_w, out_w, up_w,
    down_w, decoded, values_t, block_sems, decoded_sems,
):
    placed, normed, packed, probs, attended, middle, second, active, slopes = kept
    length = pos.shape[0]
    inner = out_w.shape[0]
    visible = embedded.shape[0]
    heads = inner // HEAD_DIM
    blocks = length // BLOCK
    high = embedded[...].astype(BF16)
    rest = (embedded[...] - high.astype(F32)).astype(BF16)
    spots = places[:, pl.ds(0, visible)]

    def place(block):
        hit = lax.broadcasted_iota(jnp.int32, (BLOCK, visible), 0) + block * BLOCK == spots
        pick = jnp.where(hit, 1.0, 0.0).astype(BF16)
        seen = jnp.sum(jnp.where(hit, 1.0, 0.0), axis=1, keepdims=True)
        return dot(pick, high) + dot(pick, rest) + (1.0 - seen) * row(bias, 3)

    def begin(block, here):
        rows = slice(block * BLOCK, (block + 1) * BLOCK)
        here = here + pos[rows, :].astype(F32)
        placed[rows, :] = here
        norm_here = (normalize(here)[0] * row(norm, 0) + row(norm, 1)).astype(BF16)
        normed[rows, :] = norm_here
        packed[rows, :] = dot(norm_here, qkv_w[...]).astype(BF16)

    staggered(range(blocks), place, begin)
    for item in range(3):
        stores.send(kept[item], kept_hbm[1 + item])
    values_t[...] = packed[:, 2 * inner :].T
    loads.wait(9, 10, 11)
    bound = [(source, target) for source, target in zip(kept[3:], kept_hbm[4:])]

    def second_pass(block, carry):
        base = pl.multiple_of(block * BLOCK, BLOCK)
        rows = pl.ds(base, BLOCK)
        slot = lax.rem(block, 2)

        def out_copy(spot):
            return pltpu.make_async_copy(
                decoded.at[lax.rem(spot, 2)],
                kept_hbm[0].at[pl.ds(pl.multiple_of(spot * BLOCK, BLOCK), BLOCK)],
                decoded_sems.at[lax.rem(spot, 2)],
            )

        queries = packed[rows, :inner] * jnp.asarray(HEAD_DIM**-0.5, BF16)
        keys = packed[:, inner : 2 * inner]
        columns = []

        def weigh(head, scores):
            probs_here = softmax_columns(scores)
            probs[block, :, pl.ds(head * BLOCK, BLOCK)] = probs_here
            columns.append(
                dot(values_t[head * HEAD_DIM : (head + 1) * HEAD_DIM, :], probs_here).astype(BF16)
            )

        staggered(range(heads), lambda head: dot_nt(keys, only_head(queries, head)), weigh)
        attended_here = jnp.concatenate(columns, axis=0).T
        attended[rows, :] = attended_here
        middle_here = placed[rows, :] + (dot(attended_here, out_w[...]) + row(bias, 1))
        middle[rows, :] = middle_here
        second_here = (normalize(middle_here)[0] * row(norm, 2) + row(norm, 3)).astype(BF16)
        second[rows, :] = second_here
        panel = 512

        def bend(low, lifted):
            cols = slice(low, low + panel)
            raised, slope = gelu_pair(lifted + up_bias[:, cols].astype(F32))
            active[rows, cols] = raised.astype(BF16)
            slopes[rows, cols] = slope.astype(BF16)

        staggered(
            range(0, up_w.shape[1], panel),
            lambda low: dot(second_here, up_w[:, low : low + panel]),
            bend,
        )

        @pl.when(block >= 2)
        def _():
            out_copy(block - 2).wait()

        decoded[slot] = middle_here + (dot(active[rows, :], down_w[...]) + row(bias, 2))
        out_copy(block).start()
        for item, (source, target) in enumerate(bound):
            spot = rows if item else block
            pltpu.make_async_copy(source.at[spot], target.at[spot], block_sems.at[item]).start()

        @pl.when(block == blocks - 1)
        def _():
            out_copy(block - 1).wait()
            out_copy(block).wait()

        return carry

    lax.fori_loop(0, blocks, second_pass, 0)
    for item, (source, target) in enumerate(bound):
        pltpu.make_async_copy(source, target, block_sems.at[item]).wait()


WHOLE = pl.BlockSpec(memory_space=pltpu.VMEM)
APART = pl.BlockSpec(memory_space=pl.ANY)
SCALARS = pl.BlockSpec(memory_space=pltpu.SMEM)
LIMIT = pltpu.CompilerParams(vmem_limit_bytes=63 * 2**20)


def like(array):
    return pltpu.VMEM(array.shape, array.dtype)


def run_forward(tokens, order, sensor, enc_w, dec_w):
    norm, qkv_w, out_w, bias, up_w, up_bias, down_w, table = enc_w
    embed_w, dec_norm, dec_qkv_w, dec_out_w, dec_bias, dec_up_w, dec_up_bias, dec_down_w, pos = dec_w
    rows, width = tokens.shape[2:]
    inner, hidden = out_w.shape[0], up_w.shape[1]
    shaped = jax.ShapeDtypeStruct
    enc_kept = [
        shaped((rows, width), F32),
        shaped((rows, width), BF16),
        shaped((rows, 3 * inner), BF16),
        shaped((inner // HEAD_DIM, rows, rows), BF16),
        shaped((rows, inner), BF16),
        shaped((rows, width), F32),
        shaped((rows, width), BF16),
        shaped((rows, hidden), BF16),
        shaped((rows, hidden), BF16),
        shaped((rows, width), BF16),
    ]
    length, dec_width = pos.shape
    dec_inner, dec_hidden = dec_out_w.shape[0], dec_up_w.shape[1]
    blocks = length // BLOCK
    dec_kept = [
        shaped((length, dec_width), F32),
        shaped((length, dec_width), BF16),
        shaped((length, 3 * dec_inner), BF16),
        shaped((blocks, length, dec_inner // HEAD_DIM * BLOCK), BF16),
        shaped((length, dec_inner), BF16),
        shaped((length, dec_width), F32),
        shaped((length, dec_width), BF16),
        shaped((length, dec_hidden), BF16),
        shaped((length, dec_hidden), BF16),
    ]
    weights = [
        qkv_w, out_w, up_w, down_w, embed_w, pos, dec_qkv_w, dec_out_w, dec_up_w, dec_down_w
    ]
    held = [like(item) for item in weights]
    results = pl.pallas_call(
        forward_kernel,
        out_shape=enc_kept + [shaped((length, dec_width), F32)] + dec_kept,
        in_specs=[SCALARS] + [WHOLE] * 7 + [APART] * 12,
        out_specs=[APART] * 20,
        scratch_shapes=[pltpu.VMEM((rows, width), BF16)]
        + held[:5]
        + [pltpu.VMEM((1, length), jnp.int32)]
        + held[5:]
        + [like(item) for item in enc_kept + dec_kept]
        + [
            pltpu.VMEM((2, BLOCK, dec_width), F32),
            pltpu.VMEM((rows, dec_width), F32),
            pltpu.VMEM((dec_inner, length), BF16),
            pltpu.SemaphoreType.DMA((12,)),
            pltpu.SemaphoreType.DMA((13,)),
            pltpu.SemaphoreType.DMA((6,)),
            pltpu.SemaphoreType.DMA((2,)),
        ],
        compiler_params=LIMIT,
        name="forward",
    )(
        sensor,
        norm,
        bias,
        up_bias.reshape(1, -1),
        table,
        dec_norm,
        dec_bias,
        dec_up_bias.reshape(1, -1),
        tokens,
        *weights[:5],
        order,
        *weights[5:],
    )
    return results[:9], results[9], results[10], results[11:]


def column_sum(values):
    return jnp.sum(values, axis=0, keepdims=True)


def norm_back(grad, values, scale):
    normal, inverse = normalize(values)
    inner = grad * scale
    mean_inner = jnp.mean(inner, axis=-1, keepdims=True)
    mean_both = jnp.mean(inner * normal, axis=-1, keepdims=True)
    return (
        inverse * (inner - mean_inner - normal * mean_both),
        column_sum(grad * normal),
        column_sum(grad),
    )


def attention_back(queries, keys, values, keys_t, probs, grad_rows, attended):
    block = queries.shape[0]
    heads = LANES // HEAD_DIM
    product = (grad_rows.astype(F32) * attended.astype(F32)).T
    scores_back, query_grads = [], []

    def through(head, probs_back):
        lanes = slice(head * HEAD_DIM, (head + 1) * HEAD_DIM)
        row_dots = column_sum(product[lanes])
        probs_here = probs[:, head * block : (head + 1) * block].astype(F32)
        scores_here = (probs_here * (probs_back - row_dots)).astype(BF16)
        scores_back.append(scores_here)
        query_grads.append(dot(keys_t[lanes], scores_here))

    staggered(range(heads), lambda head: dot_nt(values, only_head(grad_rows, head)), through)
    stacked_grad = jnp.concatenate([only_head(grad_rows, head) for head in range(heads)], axis=0)
    stacked_queries = jnp.concatenate([only_head(queries, head) for head in range(heads)], axis=0)
    grad_values = dot(probs, stacked_grad)
    grad_keys = dot(jnp.concatenate(scores_back, axis=1), stacked_queries)
    grad_queries = jnp.concatenate(query_grads, axis=0).T
    return grad_queries, grad_keys, grad_values


class Plan:
    def __init__(self, bits, blocks):
        self.bits, self.steps = bits, bits + 1
        self.waves, self.cuts = [], []
        orders, loads = orders_of(bits), [0.0, 0.0, 0.0]
        for rows, width in blocks:
            waves = []
            for wave in wave_plan(rows, width, orders, loads):
                waves.append([])
                for row_cut, col_cut, which in wave:
                    waves[-1].append((len(self.cuts), row_cut, col_cut, orders[which][0]))
                    self.cuts.append((row_cut[1], col_cut[1]))
            self.waves.append(waves)

    def scratch(self):
        lands = [
            pltpu.VMEM((2,) * (self.bits - step) + cut, BF16)
            for cut in self.cuts
            for step in range(self.steps)
        ]
        sems = pltpu.SemaphoreType.DMA((len(self.cuts), self.steps))
        return lands + [sems, sems]

    def scratch_count(self):
        return len(self.cuts) * self.steps + 2

    def bind(self, refs):
        self.refs = refs

    def chunks(self, slot, source, result):
        send_sems, recv_sems = self.refs[-2:]
        return [
            [
                Chunk(
                    source,
                    rows,
                    cols,
                    order,
                    self.refs[item * self.steps : (item + 1) * self.steps],
                    send_sems.at[item],
                    recv_sems.at[item],
                    result,
                )
                for item, rows, cols, order in wave
            ]
            for wave in self.waves[slot]
        ]


def fold(values, target):
    return values.astype(BF16).reshape(target.shape[:-1] + (values.shape[-1],))


def decode_back_kernel(plan, bits, *refs):
    (cotangent_hbm, places_hbm, norm, *refs) = refs
    load_hbm, refs = refs[:15], refs[15:]
    (returned, qkv_out, pos_out, embed_out, norm_sum, bias_sum, up_sum, *refs) = refs
    (down_done, up_done, out_done, *refs) = refs
    (cotangent, places, *refs) = refs
    load_vmem, refs = refs[:15], refs[15:]
    (
        active, down_w, slope, second, up_w, middle, attended, out_w, probs, packed,
        normed, placed, qkv_w, encoded, embed_w,
    ) = load_vmem
    (down_grad, up_grad, out_grad, grad_middle, attn_grad, grad_rows, grad_keys, grad_values,
     grad_packed, picked, load_sems, *refs) = refs
    plan.bind(refs)
    part = lax.axis_index("section")
    loads = Loads(
        [cotangent_hbm.at[part, 0], places_hbm.at[part], *load_hbm],
        [cotangent, places, *load_vmem],
        load_sems,
        6,
    )
    names = [
        "cotangent", "places", "active", "down_w", "slope", "second", "up_w", "middle", "attended",
        "out_w", "probs", "packed", "normed", "placed", "qkv_w", "encoded", "embed_w",
    ]

    def need(*wanted):
        loads.wait(*[names.index(item) for item in wanted])

    length, width = placed.shape
    inner, hidden = out_w.shape[0], up_w.shape[1]
    visible = encoded.shape[0]
    blocks = length // BLOCK
    greet(bits)
    flow = Flow(bits + 1, 2)

    def send(slot, source, result):
        for wave in plan.chunks(slot, source, result):
            flow.add(wave)

    need("cotangent", "active")
    panel = hidden // 4
    for item in range(4):
        cols = slice(item * panel, (item + 1) * panel)
        piece = dot(active[:, cols].T, cotangent[...]).astype(BF16)
        target = down_grad.at[item // 2, item % 2]
        target[...] = piece.reshape(target.shape)
    send(0, down_grad, down_done)
    bias_sum[0:1, :] = jnp.zeros((1, width), F32)
    bias_sum[2:3, :] = column_sum(cotangent[...].astype(F32))
    need("down_w", "slope", "up_w", "middle", "out_w", "second")

    def lift_back(block):
        rows = slice(block * BLOCK, (block + 1) * BLOCK)
        lifted_back = dot_nt(cotangent[rows, :], down_w[...]) * slope[rows, :].astype(F32)
        lifted_back = lifted_back.astype(BF16)
        slope[rows, :] = lifted_back
        up_part = column_sum(lifted_back.astype(F32))
        up_sum[...] = up_part + up_sum[...] if block else up_part
        return dot_nt(lifted_back, up_w[...])

    def middle_back(block, grad_second):
        rows = slice(block * BLOCK, (block + 1) * BLOCK)
        inward, scale_part, shift_part = norm_back(grad_second, middle[rows, :], row(norm, 2))
        total = cotangent[rows, :].astype(F32) + inward
        grad_middle[rows, :] = total
        rounded = total.astype(BF16)
        attn_grad[rows, :] = rounded
        bias_part = column_sum(rounded.astype(F32))
        grad_rows[rows, :] = dot_nt(rounded, out_w[...]).astype(BF16)
        if block:
            scale_part = scale_part + norm_sum[2:3, :]
            shift_part = shift_part + norm_sum[3:4, :]
            bias_part = bias_part + bias_sum[1:2, :]
        norm_sum[2:3, :] = scale_part
        norm_sum[3:4, :] = shift_part
        bias_sum[1:2, :] = bias_part
        if block % 2:
            flow.tick()

    staggered(range(blocks), lift_back, middle_back)
    second_t = second[...].T
    for item in range(4):
        cols = slice(item * panel, (item + 1) * panel)
        up_grad[:, :, :, :, :, cols] = fold(dot(second_t, slope[:, cols]), up_grad)
    send(1, up_grad, up_done)
    need("attended")
    out_grad[...] = fold(dot(attended[...].T, attn_grad[...]), out_grad)
    send(2, out_grad, out_done)
    need("probs", "packed")
    keys = packed[:, inner : 2 * inner]
    values = packed[:, 2 * inner :]
    keys_t = keys.T
    scale = HEAD_DIM**-0.5
    for block in range(blocks):
        rows = slice(block * BLOCK, (block + 1) * BLOCK)
        query_part, key_part, value_part = attention_back(
            packed[rows, :inner], keys, values, keys_t, probs[block], grad_rows[rows, :],
            attended[rows, :],
        )
        grad_packed[rows, :inner] = (query_part * scale).astype(BF16)
        if block:
            key_part = key_part + grad_keys[...]
            value_part = value_part + grad_values[...]
        if block < blocks - 1:
            grad_keys[...] = key_part
            grad_values[...] = value_part
        else:
            grad_packed[:, inner : 2 * inner] = (key_part * scale).astype(BF16)
            grad_packed[:, 2 * inner :] = value_part.astype(BF16)
        flow.tick()
    need("normed", "placed", "qkv_w", "places")
    qkv_out[...] = fold(dot(normed[...].T, grad_packed[...]), qkv_out)
    flow.tick()
    spots = places[:, pl.ds(0, visible)]

    def start_back(block, grad_normed):
        rows = slice(block * BLOCK, (block + 1) * BLOCK)
        inward, scale_part, shift_part = norm_back(grad_normed, placed[rows, :], row(norm, 0))
        total = grad_middle[rows, :] + inward
        hit = lax.broadcasted_iota(jnp.int32, (BLOCK, visible), 0) + block * BLOCK == spots
        pick = jnp.where(hit, 1.0, 0.0).astype(BF16)
        seen = jnp.sum(jnp.where(hit, 1.0, 0.0), axis=1, keepdims=True)
        fill_part = column_sum(total * (1.0 - seen))
        rounded = total.astype(BF16)
        pick_part = dot(pick.T, rounded)
        if block:
            scale_part = scale_part + norm_sum[0:1, :]
            shift_part = shift_part + norm_sum[1:2, :]
            fill_part = fill_part + bias_sum[3:4, :]
            pick_part = pick_part + picked[...]
        norm_sum[0:1, :] = scale_part
        norm_sum[1:2, :] = shift_part
        bias_sum[3:4, :] = fill_part
        picked[...] = pick_part
        pos_out[:, :, :, :, :, rows] = fold(rounded.T, pos_out)
        flow.tick()

    staggered(
        range(blocks),
        lambda block: dot_nt(grad_packed[block * BLOCK : (block + 1) * BLOCK, :], qkv_w[...]),
        start_back,
    )
    need("encoded", "embed_w")
    grad_embedded = picked[...].astype(BF16)
    bias_sum[0:1, :] = column_sum(picked[...])
    embed_out[...] = fold(dot(encoded[...].T, grad_embedded), embed_out)
    returned[...] = dot_nt(grad_embedded, embed_w[...]).astype(BF16)
    flow.drain()


def encode_back_kernel(plan, bits, *refs):
    (returned, kind, norm, dec_norm_sum, dec_bias_sum, dec_up_sum, *refs) = refs
    early, refs = refs[:3], refs[3:]
    load_hbm, refs = refs[:13], refs[13:]
    (input_grad, small_done, *refs) = refs
    done, refs = refs[:7], refs[7:]
    load_vmem, refs = refs[:13], refs[13:]
    (
        active, down_w, slope, second, up_w, middle, attended, out_w, probs, packed,
        normed, start, qkv_w,
    ) = load_vmem
    (down_grad, up_grad, out_grad, qkv_grad, grad_packed, small, small_lands, small_send,
     small_recv, load_sems, *refs) = refs
    plan.bind(refs)
    loads = Loads(load_hbm, load_vmem, load_sems, 6)
    names = [
        "active", "down_w", "slope", "second", "up_w", "middle", "attended", "out_w", "probs",
        "packed", "normed", "start", "qkv_w",
    ]

    def need(*wanted):
        loads.wait(*[names.index(item) for item in wanted])

    inner, hidden = out_w.shape[0], up_w.shape[1]
    width = start.shape[1]
    greet(bits)
    flow = Flow(bits + 1, 2)

    def send(slot, source, result, part=None):
        waves = plan.chunks(slot, source, result)
        for wave in waves if part is None else waves[part : part + 1]:
            flow.add(wave)

    for slot, source in enumerate(early):
        send(slot, source, done[slot])
    branch = returned[...]
    small[...] = jnp.zeros_like(small)
    small[5:6, :] = column_sum(branch.astype(F32))
    need("active")
    panel = hidden // 4
    for item in range(4):
        cols = slice(item * panel, (item + 1) * panel)
        target = down_grad.at[item // 2, item % 2]
        target[...] = dot(active[:, cols].T, branch).astype(BF16).reshape(target.shape)
    flow.tick()
    send(3, down_grad, done[3], 0)
    need("second", "slope", "down_w")
    second_t = second[...].T
    for item in range(4):
        cols = slice(item * panel, (item + 1) * panel)
        lifted_back = (dot_nt(branch, down_w[cols, :]) * slope[:, cols].astype(F32)).astype(BF16)
        slope[:, cols] = lifted_back
        small[10 + item : 11 + item, :] = column_sum(lifted_back.astype(F32))
        up_grad[:, :, :, :, :, cols] = fold(dot(second_t, lifted_back), up_grad)
    flow.tick()
    send(3, down_grad, done[3], 1)
    need("up_w", "middle", "out_w", "attended")
    grad_second = dot_nt(slope[...], up_w[...])
    inward, small[2:3, :], small[3:4, :] = norm_back(grad_second, middle[...], row(norm, 2))
    grad_middle = branch.astype(F32) + inward
    attn_grad = grad_middle.astype(BF16)
    small[4:5, :] = column_sum(attn_grad.astype(F32))
    flow.tick()
    send(4, up_grad, done[4], 0)
    out_grad[...] = fold(dot(attended[...].T, attn_grad), out_grad)
    grad_rows = dot_nt(attn_grad, out_w[...]).astype(BF16)
    flow.tick()
    send(4, up_grad, done[4], 1)
    need("probs", "packed")
    scale = HEAD_DIM**-0.5
    heads = LANES // HEAD_DIM
    for group in range(inner // LANES):
        base = group * LANES
        lanes = slice(base, base + LANES)
        keys = packed[:, inner + base : inner + base + LANES]
        query_part, key_part, value_part = attention_back(
            packed[:, lanes],
            keys,
            packed[:, 2 * inner + base : 2 * inner + base + LANES],
            keys.T,
            jnp.concatenate([probs[group * heads + head] for head in range(heads)], axis=1),
            grad_rows[:, lanes],
            attended[:, lanes],
        )
        grad_packed[:, lanes] = (query_part * scale).astype(BF16)
        grad_packed[:, inner + base : inner + base + LANES] = (key_part * scale).astype(BF16)
        grad_packed[:, 2 * inner + base : 2 * inner + base + LANES] = value_part.astype(BF16)
    flow.tick()
    need("normed", "start", "qkv_w")
    send(5, out_grad, done[5])
    normed_t = normed[...].T
    for item in range(3):
        cols = slice(item * inner, (item + 1) * inner)
        qkv_grad[:, :, :, :, :, cols] = fold(dot(normed_t, grad_packed[:, cols]), qkv_grad)
    flow.tick()
    send(6, qkv_grad, done[6])
    grad_normed = dot_nt(grad_packed[...], qkv_w[...])
    inward, small[0:1, :], small[1:2, :] = norm_back(grad_normed, start[...], row(norm, 0))
    grad_start = grad_middle + inward
    input_grad[...] = grad_start
    kinds = lax.broadcasted_iota(jnp.int32, (4, 1), 0)
    mine = kind[pl.ds(lax.axis_index("section"), 1), :]
    small[6:10, :] = jnp.where(kinds == mine, 1.0, 0.0) * column_sum(grad_start)
    dec_width = dec_norm_sum.shape[1]
    small[14:18, :dec_width] = dec_norm_sum[...]
    small[18:22, :dec_width] = dec_bias_sum[...]
    for item in range(4):
        small[22 + item : 23 + item, :dec_width] = dec_up_sum[
            :, item * dec_width : (item + 1) * dec_width
        ]
    flow.add([Whole(small, bits, small_lands, small_send, small_recv, small_done)])
    flow.drain()


def finish_kernel(counts, *refs):
    small_count, big_count = counts
    small, pos = refs[0], refs[1]
    big, refs = refs[2 : 2 + big_count], refs[2 + big_count :]
    tiny, pos_out = refs[:small_count], refs[small_count]
    big_out, sems = refs[small_count + 1 : -1], refs[-1]
    copies = [
        pltpu.make_async_copy(source, target, sems.at[item])
        for item, (source, target) in enumerate(zip(big, big_out))
    ]
    for copy in copies:
        copy.start()
    section, data = lax.axis_index("section"), lax.axis_index("dp")
    datas = lax.axis_size("dp")
    pos_out[...] = pos[...].T
    first = 0
    for out in tiny:
        cols = out.shape[-1]
        if out.shape[0] > 1 or first == 4:
            lines = out.shape[0]
            width = cols * datas
            here = jnp.where(
                section == 0,
                small[first : first + lines, :width],
                small[first + lines : first + 2 * lines, :width],
            )
            spot = data * cols
            first += 2 * lines
        else:
            lines = 4
            width = cols * datas * 2 // lines
            per_line = width // cols
            index = section * datas + data
            here = jnp.zeros((1, width), F32)
            for line in range(lines):
                mine = index // per_line == line
                here = here + jnp.where(mine, small[first + line : first + line + 1, :width], 0.0)
            spot = lax.rem(index, per_line) * cols
            first += lines
        here = pltpu.roll(here, lax.rem(width - spot, width), 1)
        out[...] = here[:, :cols]
    for copy in copies:
        copy.wait()


def run_finish(small, pos, big, shapes, datas):
    shaped = jax.ShapeDtypeStruct
    return pl.pallas_call(
        partial(finish_kernel, (len(shapes), len(big))),
        out_shape=[shaped(item, F32) for item in shapes]
        + [shaped(pos.shape[::-1], F32)]
        + [shaped(item.shape, F32) for item in big],
        in_specs=[WHOLE, WHOLE] + [APART] * len(big),
        out_specs=[WHOLE] * (len(shapes) + 1 + len(big)),
        scratch_shapes=[pltpu.SemaphoreType.DMA((len(big),))],
        name="finish",
    )(small, pos, *big)


def communicating(number):
    return pltpu.CompilerParams(
        collective_id=number, has_side_effects=True, vmem_limit_bytes=63 * 2**20
    )


def blocked(rows, cols, bits):
    return (2,) * bits + (rows // 2**bits, cols)


def run_decode_back(cotangent, order, stored, encoded, dec_w, bits):
    embed_w, norm, qkv_w, out_w, bias, up_w, up_bias, down_w, pos = dec_w
    placed, normed, packed, probs, attended, middle, second, active, slope = stored
    length, width = pos.shape
    inner, hidden = out_w.shape[0], up_w.shape[1]
    shaped = jax.ShapeDtypeStruct
    loaded = [
        active, down_w, slope, second, up_w, middle, attended, out_w, probs, packed, normed,
        placed, qkv_w, encoded, embed_w,
    ]
    sent = [blocked(*item.shape, bits) for item in (down_w, up_w, out_w)]
    plan = Plan(bits, [(item[-2], item[-1] // 2) for item in sent])
    later = [blocked(*qkv_w.shape, bits), blocked(width, length, bits), blocked(*embed_w.shape, bits)]
    return pl.pallas_call(
        partial(decode_back_kernel, plan, bits),
        out_shape=[shaped(encoded.shape, BF16)]
        + [shaped(item, BF16) for item in later]
        + [shaped((4, width), F32), shaped((4, width), F32), shaped((1, hidden), F32)]
        + [shaped((item[-2], item[-1] // 2), F32) for item in sent],
        in_specs=[APART, APART, WHOLE] + [APART] * len(loaded),
        out_specs=[WHOLE] * 10,
        scratch_shapes=[
            pltpu.VMEM((length, width), BF16),
            pltpu.VMEM((1, length), jnp.int32),
        ]
        + [like(item) for item in loaded]
        + [pltpu.VMEM(item, BF16) for item in sent]
        + [
            pltpu.VMEM((length, width), F32),
            pltpu.VMEM((length, width), BF16),
            pltpu.VMEM((length, inner), BF16),
            pltpu.VMEM((length, inner), F32),
            pltpu.VMEM((length, inner), F32),
            pltpu.VMEM((length, 3 * inner), BF16),
            pltpu.VMEM((encoded.shape[0], width), F32),
            pltpu.SemaphoreType.DMA((len(loaded) + 2,)),
        ]
        + plan.scratch(),
        compiler_params=communicating(1),
        name="decode_back",
    )(cotangent, order, norm, *loaded)


def run_encode_back(returned, sensor, stored, enc_w, early, dec_sums, bits):
    norm, qkv_w, out_w, bias, up_w, up_bias, down_w, table = enc_w
    start, normed, packed, probs, attended, middle, second, active, slope = stored
    shaped = jax.ShapeDtypeStruct
    loaded = [
        active, down_w, slope, second, up_w, middle, attended, out_w, probs, packed, normed,
        start, qkv_w,
    ]
    own = [blocked(*item.shape, bits) for item in (down_w, up_w, out_w, qkv_w)]
    sent = [item.shape for item in early] + own
    plan = Plan(bits, [(item[-2], item[-1] // 2) for item in sent])
    width = start.shape[1]
    small = (SMALL_ROWS, width)
    return pl.pallas_call(
        partial(encode_back_kernel, plan, bits),
        out_shape=[shaped(start.shape, F32), shaped(small, F32)]
        + [shaped((item[-2], item[-1] // 2), F32) for item in sent],
        in_specs=[WHOLE] * 9 + [APART] * len(loaded),
        out_specs=[WHOLE] * 9,
        scratch_shapes=[like(item) for item in loaded]
        + [pltpu.VMEM(item, BF16) for item in own]
        + [
            pltpu.VMEM(packed.shape, BF16),
            pltpu.VMEM(small, F32),
            pltpu.VMEM((bits + 1,) + small, F32),
            pltpu.SemaphoreType.DMA((bits + 1,)),
            pltpu.SemaphoreType.DMA((bits + 1,)),
            pltpu.SemaphoreType.DMA((len(loaded),)),
        ]
        + plan.scratch(),
        compiler_params=communicating(2),
        name="encode_back",
    )(returned, sensor, norm, *dec_sums, *early, *loaded)


def local_rows(whole, shape):
    section, data = lax.axis_index("section"), lax.axis_index("dp")
    sections, datas = lax.axis_size("section"), lax.axis_size("dp")
    if len(shape) == 1:
        count = shape[0] // (sections * datas)
        return lax.dynamic_slice_in_dim(
            whole.reshape(-1)[: shape[0]], (section * datas + data) * count, count, 0
        )
    rows, cols = shape[0] // sections, shape[1] // datas
    return lax.dynamic_slice(whole, (section * rows, data * cols), (rows, cols))


def plain_shards(tokens, order, sensor, cotangent, enc_w, dec_w):
    section_count = lax.axis_size("section")
    section_index = lax.axis_index("section")
    half_count = tokens.shape[0] // section_count

    def mine(array):
        part = lax.dynamic_slice_in_dim(array, section_index * half_count, half_count, 0)
        return part.reshape((half_count * array.shape[1],) + array.shape[2:])

    encoded, stored, picks = encode(mine(tokens), mine(sensor), enc_w)
    output, returned, dec_grads = decode(encoded, mine(order), mine(cotangent), dec_w)
    grad_input, enc_grads = encode_back(stored, picks, returned, enc_w)
    done = []
    for slot, grad in enumerate(enc_grads + dec_grads):
        if slot in (0, 3, 5, 7, 9, 12, 14):
            total = local_rows(lax.psum(grad, ("section", "dp")), grad.shape)
        else:
            side = 0 if slot == 16 else 1
            total = lax.psum_scatter(
                grad.astype(jnp.bfloat16), "section", scatter_dimension=side, tiled=True
            )
            total = lax.psum_scatter(total, "dp", scatter_dimension=1 - side, tiled=True)
        done.append(total.astype(jnp.float32))
    decoded = output.reshape((half_count,) + cotangent.shape[1:])
    input_grad = grad_input.reshape((half_count,) + tokens.shape[1:])
    return (decoded, input_grad) + tuple(done)


def shards(tokens, order, sensor, cotangent, *weights):
    enc_w, dec_w = weights[:8], weights[8:]
    sections, datas = lax.axis_size("section"), lax.axis_size("dp")
    split_rows = [enc_w[1], enc_w[2], enc_w[4], enc_w[6], dec_w[0], dec_w[2], dec_w[3], dec_w[5]]
    fits = (
        sections == 2
        and tokens.shape[:2] == (sections, 1)
        and datas & (datas - 1) == 0
        and datas >= 4
        and all(item.shape[0] % (16 * datas) == 0 for item in split_rows)
    )
    if not fits:
        return plain_shards(tokens, order, sensor, cotangent, enc_w, dec_w)
    bits = datas.bit_length() - 1
    enc_kept, encoded, decoded, dec_kept = run_forward(tokens, order, sensor, enc_w, dec_w)
    back = run_decode_back(cotangent, order, dec_kept, encoded, dec_w, bits)
    returned, early, dec_sums, dec_done = back[0], back[1:4], back[4:7], back[7:]
    input_grad, small, *rest = run_encode_back(
        returned, sensor, enc_kept, enc_w, early, dec_sums, bits
    )
    qkv_dec, pos, embed, down, up, out, qkv = rest
    tiny_slots = (0, 3, 7, 5, 9, 12, 14)
    shapes = [
        (item.shape[0] // 2, item.shape[1] // datas)
        if item.ndim == 2
        else (1, item.shape[0] // (2 * datas))
        for item in (weights[slot] for slot in tiny_slots)
    ]
    big = [input_grad, qkv, out, up, down, embed, qkv_dec, *dec_done]
    results = run_finish(small, pos, big, shapes, datas)
    done = dict(zip(tiny_slots, results))
    for slot in (5, 14):
        done[slot] = done[slot].reshape(-1)
    done[16] = results[7]
    input_grad = results[8]
    for slot, item in zip((1, 2, 4, 6, 8, 10, 15, 13, 11), results[9:]):
        done[slot] = item
    return (decoded[None, None], input_grad[None, None]) + tuple(done[slot] for slot in range(17))


def solution(mesh):
    placed = (
        P(None, "dp", None, None),
        P(None, "dp", None),
        P(None, "dp"),
        P(None, "dp", None, None),
        P(),
        P(),
        P(),
        P(),
        P(),
        P(),
        P(),
        P(),
        P(),
        P(),
        P(),
        P(),
        P(),
        P(),
        P(),
        P(),
        P(),
    )
    return jax.shard_map(
        shards,
        mesh=mesh,
        in_specs=placed,
        out_specs=(
            P("section", "dp", None, None),
            P("section", "dp", None, None),
            P("section", "dp"),
            P("dp", "section"),
            P("dp", "section"),
            P("section", "dp"),
            P("dp", "section"),
            P(("section", "dp")),
            P("dp", "section"),
            P("section", "dp"),
            P("dp", "section"),
            P("section", "dp"),
            P("dp", "section"),
            P("dp", "section"),
            P("section", "dp"),
            P("dp", "section"),
            P(("section", "dp")),
            P("dp", "section"),
            P("section", "dp"),
        ),
        check_vma=False,
    )
```

```python
import heapq
import math
from functools import partial

import jax
import jax.numpy as jnp
from jax import lax
from jax.experimental import pallas as pl
from jax.experimental.pallas import tpu as pltpu
from jax.sharding import PartitionSpec as P

HEAD_DIM = 64
MESH = pl.DeviceIdType.MESH
SMALL_ROWS = 32


def layer_norm(hidden, scales, shifts):
    center = hidden - jnp.mean(hidden, axis=-1, keepdims=True)
    spread = jnp.mean(center * center, axis=-1, keepdims=True)
    return center * lax.rsqrt(spread + 1e-05) * scales + shifts


def matmul(left_side, right_side):
    return jnp.dot(left_side, right_side, preferred_element_type=jnp.float32)


def row_contract(left_side, right_side):
    return lax.dot_general(
        left_side, right_side, (((0,), (0,)), ((), ())), preferred_element_type=jnp.float32
    )


def col_contract(left_side, right_side):
    return lax.dot_general(
        left_side, right_side, (((1,), (1,)), ((), ())), preferred_element_type=jnp.float32
    )


def gelu_exact(values):
    return jax.nn.gelu(values, approximate=False)


def block_forward(hidden, weights):
    norms, qkv_w, out_w, biases, up_w, up_bias, down_w = weights
    batch_size, length, feature_width = hidden.shape
    row_count = batch_size * length
    head_count = qkv_w.shape[1] // (3 * HEAD_DIM)
    inner_width = head_count * HEAD_DIM
    norm_rows = norms.astype(jnp.float32)
    bias_rows = biases.astype(jnp.float32)
    normed = (
        layer_norm(hidden, norm_rows[0], norm_rows[1])
        .astype(jnp.bfloat16)
        .reshape(row_count, feature_width)
    )
    packed = (
        matmul(normed, qkv_w)
        .astype(jnp.bfloat16)
        .reshape(batch_size, length, 3, head_count, HEAD_DIM)
    )
    queries = packed[:, :, 0]
    keys_all = packed[:, :, 1]
    values_all = packed[:, :, 2]
    scores = jnp.einsum(
        "bqhd,bkhd->bhqk", queries, keys_all, preferred_element_type=jnp.float32
    ) * HEAD_DIM ** (-0.5)
    row_peak = jnp.max(scores, axis=-1, keepdims=True)
    logsum = row_peak + jnp.log(jnp.sum(jnp.exp(scores - row_peak), axis=-1, keepdims=True))
    probability = jnp.exp(scores - logsum).astype(jnp.bfloat16)
    attended = jnp.einsum(
        "bhqk,bkhd->bqhd", probability, values_all, preferred_element_type=jnp.float32
    )
    attended = attended.astype(jnp.bfloat16).reshape(row_count, inner_width)
    middle = hidden + (matmul(attended, out_w) + bias_rows[0]).reshape(
        batch_size, length, feature_width
    )
    second = (
        layer_norm(middle, norm_rows[2], norm_rows[3])
        .astype(jnp.bfloat16)
        .reshape(row_count, feature_width)
    )
    lifted = matmul(second, up_w) + up_bias.astype(jnp.float32)
    active = gelu_exact(lifted).astype(jnp.bfloat16)
    output = middle + (matmul(active, down_w) + bias_rows[1]).reshape(
        batch_size, length, feature_width
    )
    stored = (hidden, normed, packed, logsum, attended, middle, second, lifted, active)
    return (output, stored)


def block_backward(stored, upstream, weights):
    norms, qkv_w, out_w, biases, up_w, up_bias, down_w = weights
    hidden, normed, packed, logsum, attended, middle, second, lifted, active = stored
    batch_size, length, feature_width = hidden.shape
    row_count = batch_size * length
    head_count = qkv_w.shape[1] // (3 * HEAD_DIM)
    inner_width = head_count * HEAD_DIM
    score_scale = HEAD_DIM ** (-0.5)
    norm_rows = norms.astype(jnp.float32)
    branch_grad = upstream.reshape(row_count, feature_width).astype(jnp.bfloat16)
    grad_down = row_contract(active, branch_grad)
    grad_bias_down = jnp.sum(branch_grad.astype(jnp.float32), axis=0)
    grad_active = col_contract(branch_grad, down_w)
    grad_lifted = jax.vjp(gelu_exact, lifted)[1](grad_active)[0].astype(jnp.bfloat16)
    grad_up = row_contract(second, grad_lifted)
    grad_up_bias = jnp.sum(grad_lifted.astype(jnp.float32), axis=0)
    grad_second = col_contract(grad_lifted, up_w).reshape(batch_size, length, feature_width)
    grad_middle, grad_scale_two, grad_shift_two = jax.vjp(
        layer_norm, middle, norm_rows[2], norm_rows[3]
    )[1](grad_second)
    grad_middle = upstream + grad_middle
    attn_grad = grad_middle.reshape(row_count, feature_width).astype(jnp.bfloat16)
    grad_out = row_contract(attended, attn_grad)
    grad_bias_out = jnp.sum(attn_grad.astype(jnp.float32), axis=0)
    grad_attended = (
        col_contract(attn_grad, out_w)
        .astype(jnp.bfloat16)
        .reshape(batch_size, length, head_count, HEAD_DIM)
    )
    queries = packed[:, :, 0]
    keys_all = packed[:, :, 1]
    values_all = packed[:, :, 2]
    scores = (
        jnp.einsum("bqhd,bkhd->bhqk", queries, keys_all, preferred_element_type=jnp.float32)
        * score_scale
    )
    probability = jnp.exp(scores - logsum)
    grad_probs = jnp.einsum(
        "bqhd,bkhd->bhqk", grad_attended, values_all, preferred_element_type=jnp.float32
    )
    grad_values = jnp.einsum(
        "bhqk,bqhd->bkhd",
        probability.astype(jnp.bfloat16),
        grad_attended,
        preferred_element_type=jnp.float32,
    )
    row_dots = jnp.sum(grad_probs * probability, axis=-1, keepdims=True)
    grad_scores = (probability * (grad_probs - row_dots)).astype(jnp.bfloat16)
    grad_queries = (
        jnp.einsum("bhqk,bkhd->bqhd", grad_scores, keys_all, preferred_element_type=jnp.float32)
        * score_scale
    )
    grad_keys = (
        jnp.einsum("bhqk,bqhd->bkhd", grad_scores, queries, preferred_element_type=jnp.float32)
        * score_scale
    )
    grad_packed = (
        jnp.stack([grad_queries, grad_keys, grad_values], axis=2)
        .astype(jnp.bfloat16)
        .reshape(row_count, 3 * inner_width)
    )
    grad_qkv = row_contract(normed, grad_packed)
    grad_normed = col_contract(grad_packed, qkv_w).reshape(batch_size, length, feature_width)
    grad_hidden, grad_scale_one, grad_shift_one = jax.vjp(
        layer_norm, hidden, norm_rows[0], norm_rows[1]
    )[1](grad_normed)
    grad_hidden = grad_middle + grad_hidden
    grad_norms = jnp.stack([grad_scale_one, grad_shift_one, grad_scale_two, grad_shift_two])
    grad_biases = jnp.stack([grad_bias_out, grad_bias_down])
    return (
        grad_hidden,
        (grad_norms, grad_qkv, grad_out, grad_biases, grad_up, grad_up_bias, grad_down),
    )


def encode(tokens_part, sensor_part, enc_w):
    table = enc_w[7].astype(jnp.float32)
    picks = (sensor_part[:, None] == jnp.arange(table.shape[0])[None, :]).astype(jnp.float32)
    start = (
        tokens_part.astype(jnp.float32)
        + jnp.sum(picks[:, :, None] * table[None], axis=1)[:, None, :]
    )
    output, stored = block_forward(start, enc_w[:7])
    return (output.astype(jnp.bfloat16), stored, picks)


def encode_back(stored, picks, returned, enc_w):
    grad_input, grads = block_backward(stored, returned.astype(jnp.float32), enc_w[:7])
    grad_table = jnp.sum(picks[:, :, None] * jnp.sum(grad_input, axis=1)[:, None, :], axis=0)
    return (grad_input, grads + (grad_table,))


def decode(arrived, place, cotangent_part, dec_w):
    dec_embed, dec_norm, dec_qkv, dec_out, dec_bias, dec_up, dec_up_bias, dec_down, dec_pos = dec_w
    batch_size, visible, model_width = arrived.shape
    patches = place.shape[1]
    bias_rows = dec_bias.astype(jnp.float32)
    flat_rows = arrived.reshape(batch_size * visible, model_width)
    embedded = (matmul(flat_rows, dec_embed) + bias_rows[0]).reshape(
        batch_size, visible, bias_rows.shape[1]
    )
    filler = jnp.broadcast_to(bias_rows[3], (batch_size, patches - visible, bias_rows.shape[1]))
    sequence = jnp.concatenate([embedded, filler], axis=1)
    image_rows = jnp.arange(batch_size)[:, None]
    placed = jnp.zeros_like(sequence).at[image_rows, place].set(sequence) + dec_pos.astype(
        jnp.float32
    )
    block_w = (dec_norm, dec_qkv, dec_out, bias_rows[1:3], dec_up, dec_up_bias, dec_down)
    output, stored = block_forward(placed, block_w)
    grad_placed, grads = block_backward(stored, cotangent_part.astype(jnp.float32), block_w)
    grad_pos = jnp.sum(grad_placed, axis=0)
    grad_sequence = jnp.take_along_axis(grad_placed, place[:, :, None], axis=1)
    grad_embedded = (
        grad_sequence[:, :visible]
        .reshape(batch_size * visible, bias_rows.shape[1])
        .astype(jnp.bfloat16)
    )
    grad_filler = jnp.sum(grad_sequence[:, visible:], axis=(0, 1))
    grad_embed = row_contract(flat_rows, grad_embedded)
    grad_bias_embed = jnp.sum(grad_embedded.astype(jnp.float32), axis=0)
    returned = (
        col_contract(grad_embedded, dec_embed)
        .astype(jnp.bfloat16)
        .reshape(batch_size, visible, model_width)
    )
    grad_norms, grad_qkv, grad_out, grad_biases, grad_up, grad_up_bias, grad_down = grads
    grad_bias = jnp.stack([grad_bias_embed, grad_biases[0], grad_biases[1], grad_filler])
    return (
        output,
        returned,
        (
            grad_embed,
            grad_norms,
            grad_qkv,
            grad_out,
            grad_bias,
            grad_up,
            grad_up_bias,
            grad_down,
            grad_pos,
        ),
    )


CORE = -1


def partner_of(stage):
    section, data = lax.axis_index("section"), lax.axis_index("dp")
    if stage == CORE:
        return (1 - section, data)
    weight = 2**stage
    bit = lax.rem(data // weight, 2)
    return (section, data + weight * (1 - 2 * bit))


def bit_of(stage):
    if stage == CORE:
        return lax.axis_index("section")
    return lax.rem(lax.axis_index("dp") // 2**stage, 2)


def greet(bits):
    barrier = pltpu.get_barrier_semaphore()
    for stage in [CORE] + list(range(bits)):
        pl.semaphore_signal(barrier, inc=1, device_id=partner_of(stage), device_id_type=MESH)


def greeted(bits):
    pl.semaphore_wait(pltpu.get_barrier_semaphore(), bits + 1)


class Chunk:
    def __init__(self, source, rows, cols, stages, lands, send_sems, recv_sems, result):
        self.source, self.rows, self.cols, self.stages = source, rows, cols, stages
        self.lands, self.send_sems, self.recv_sems = lands, send_sems, recv_sems
        self.result = result
        self.dims = list(range(len(stages) - 2, -1, -1))

    def halves(self, step):
        stage = self.stages[step]
        bit = bit_of(stage)
        if stage == CORE:
            width = self.source.shape[-1] // 2
            start, extent = self.cols

            def part(side):
                offset = pl.multiple_of(side * width + start, 128)
                return self.source.at[
                    (slice(None),) * len(self.dims)
                    + (pl.ds(self.rows[0], self.rows[1]), pl.ds(offset, extent))
                ]

            return part(1 - bit), part(bit)
        held = self.lands[step - 1]
        left = [item for item in self.dims if item not in self.stages[1:step]]
        place = left.index(stage)

        def part(side):
            return held.at[(slice(None),) * place + (side,)]

        return part(1 - bit), part(bit)

    def copy(self, step):
        return pltpu.make_async_remote_copy(
            src_ref=self.halves(step)[0],
            dst_ref=self.lands[step],
            send_sem=self.send_sems.at[step],
            recv_sem=self.recv_sems.at[step],
            device_id=partner_of(self.stages[step]),
            device_id_type=MESH,
        )

    def start(self, step):
        self.copy(step).start()

    def finish(self, step):
        self.copy(step).wait_recv()
        kept, land = self.halves(step)[1], self.lands[step]
        if len(land.shape) > 2:
            land[...] = land[...] + kept[...]
            self.start(step + 1)
        else:
            self.result[pl.ds(*self.rows), pl.ds(*self.cols)] = land[...].astype(
                jnp.float32
            ) + kept[...].astype(jnp.float32)

    def close(self):
        for step in range(len(self.stages)):
            self.copy(step).wait_send()


class Whole:
    def __init__(self, source, bits, lands, send_sems, recv_sems, result):
        self.source, self.lands, self.send_sems, self.recv_sems = source, lands, send_sems, recv_sems
        self.stages = [CORE] + list(range(bits))
        self.result = result

    def held(self, step):
        return self.source if step == 0 else self.lands.at[step - 1]

    def copy(self, step):
        return pltpu.make_async_remote_copy(
            src_ref=self.held(step),
            dst_ref=self.lands.at[step],
            send_sem=self.send_sems.at[step],
            recv_sem=self.recv_sems.at[step],
            device_id=partner_of(self.stages[step]),
            device_id_type=MESH,
        )

    def start(self, step):
        self.copy(step).start()

    def finish(self, step):
        self.copy(step).wait_recv()
        total = self.lands[step] + self.held(step)[...]
        if step == len(self.stages) - 1:
            self.result[...] = total
        else:
            self.lands[step] = total
            self.start(step + 1)

    def close(self):
        for step in range(len(self.stages)):
            self.copy(step).wait_send()


class Flow:
    def __init__(self, steps, lag):
        self.steps, self.lag = steps, lag
        self.waves, self.tick_now = [], 0

    def add(self, chunks):
        for chunk in chunks:
            chunk.start(0)
        self.waves.append([chunks, 0, self.tick_now + 1])

    def tick(self):
        self.tick_now += 1
        for wave in self.waves:
            chunks, step, due = wave
            if step < self.steps and due <= self.tick_now:
                for chunk in chunks:
                    chunk.finish(step)
                wave[1], wave[2] = step + 1, self.tick_now + self.lag

    def drain(self):
        while any(wave[1] < self.steps for wave in self.waves):
            self.tick()
        for wave in self.waves:
            for chunk in wave[0]:
                chunk.close()


def orders_of(bits):
    near = bits // 3
    x, y, z = list(range(near)), list(range(near, 2 * near)), list(range(2 * near, bits))
    return [
        ([CORE] + x + y + z, (0.5, 0.25, 0.1875)),
        ([CORE] + y + x + z, (0.25, 0.5, 0.1875)),
        ([CORE] + z + x + y, (0.125, 0.0625, 0.75)),
        ([CORE] + z + y + x, (0.0625, 0.125, 0.75)),
    ]


def wave_plan(rows, width, orders, loads):
    by_rows = rows >= 128
    unit = 16 if by_rows else 128
    strips = (rows if by_rows else width) // unit
    count = 2 if rows * width > 48 * 1024 else 1
    waves = []
    for item in range(count):
        low, high = strips * item // count, strips * (item + 1) // count
        taken = []
        for _ in range(low, high):
            totals = [
                [old + new * rows * width / strips for old, new in zip(loads, cost)]
                for _, cost in orders
            ]
            best = min(range(len(orders)), key=lambda which: max(totals[which]))
            loads[:] = totals[best]
            taken.append(best)
        wave = []
        for which in sorted(set(taken)):
            extent = taken.count(which)
            cut = (low * unit, extent * unit)
            low += extent
            wave.append((cut, (0, width), which) if by_rows else ((0, rows), cut, which))
        waves.append(wave)
    return waves


F32, BF16 = jnp.float32, jnp.bfloat16
BLOCK = 256
LANES = 256


def dot(left, right):
    return jnp.dot(left, right, preferred_element_type=F32)


def dot_nt(left, right):
    return lax.dot_general(left, right, (((1,), (1,)), ((), ())), preferred_element_type=F32)


def head_of_lane(rows, width=LANES):
    return lax.broadcasted_iota(jnp.int32, (rows, width), 1) // HEAD_DIM


def only_head(rows, head):
    lane = lax.broadcasted_iota(jnp.int32, rows.shape, 1)
    keep = (lane >= head * HEAD_DIM) & (lane < (head + 1) * HEAD_DIM)
    return jnp.where(keep, rows, jnp.zeros_like(rows))


def normalize(values):
    center = values - jnp.mean(values, axis=-1, keepdims=True)
    inverse = lax.rsqrt(jnp.mean(center * center, axis=-1, keepdims=True) + 1e-05)
    return center * inverse, inverse


def gelu_pair(values):
    area = 0.5 + 0.5 * lax.erf(values * 0.7071067811865476)
    slope = jnp.exp(values * values * -0.5) * 0.3989422804014327
    return values * area, area + values * slope


def softmax_columns(scores):
    peak = jnp.max(scores, axis=0, keepdims=True)
    raised = jnp.exp(scores - peak)
    return (raised * (1.0 / jnp.sum(raised, axis=0, keepdims=True))).astype(BF16)


def staggered(items, produce, consume):
    held = None
    for item in items:
        made = produce(item)
        if held is not None:
            consume(*held)
        held = (item, made)
    consume(*held)


class Loads:
    def __init__(self, sources, targets, sems, ahead):
        self.copies = [
            pltpu.make_async_copy(source, target, sems.at[item])
            for item, (source, target) in enumerate(zip(sources, targets))
        ]
        self.ahead, self.started = ahead, 0
        self.reach(ahead)

    def reach(self, count):
        for copy in self.copies[self.started : count]:
            copy.start()
        self.started = max(self.started, min(count, len(self.copies)))

    def wait(self, *items):
        for item in items:
            self.reach(item + 1 + self.ahead)
            self.copies[item].wait()


class Stores:
    def __init__(self, sems):
        self.sems, self.copies = sems, []

    def send(self, source, target):
        copy = pltpu.make_async_copy(source, target, self.sems.at[len(self.copies)])
        copy.start()
        self.copies.append(copy)

    def close(self):
        for copy in self.copies:
            copy.wait()


def row(ref, index):
    return ref[pl.ds(index, 1), :].astype(F32)


def forward_kernel(*refs):
    (aux, norm, bias, dec_norm, dec_bias, *refs) = refs
    width, dec_hidden = norm.shape[1], refs[10].shape[1]
    up_bias, dec_up_bias, added = aux.at[0:1], aux.at[1:2, :dec_hidden], aux.at[2:3, :width]
    load_hbm, refs = refs[:12], refs[12:]
    store_hbm, refs = refs[:20], refs[20:]
    load_vmem, refs = refs[:12], refs[12:]
    (
        tokens, qkv_w, out_w, up_w, down_w, embed_w, places, pos, dec_qkv_w, dec_out_w, dec_up_w,
        dec_down_w,
    ) = load_vmem
    enc_kept, dec_kept = refs[:10], refs[10:19]
    (decoded, embedded, values_t, load_sems, store_sems, block_sems, decoded_sems) = refs[19:]
    part = lax.axis_index("section")
    sources = list(load_hbm)
    sources[0] = sources[0].at[part, 0]
    sources[6] = sources[6].at[part]
    loads = Loads(sources, load_vmem, load_sems, 3)
    stores = Stores(store_sems)
    encode_rows(
        loads, stores, enc_kept, store_hbm[:10], tokens, added, norm, bias, up_bias, qkv_w,
        out_w, up_w, down_w,
    )
    loads.wait(5)
    embedded[...] = dot(enc_kept[-1][...], embed_w[...]) + row(dec_bias, 0)
    loads.wait(6, 7, 8)
    decode_rows(
        loads, stores, dec_kept, store_hbm[10:], embedded, places, pos, dec_norm, dec_bias,
        dec_up_bias, dec_qkv_w, dec_out_w, dec_up_w, dec_down_w, decoded, values_t, block_sems,
        decoded_sems,
    )
    stores.close()


def encode_rows(
    loads, stores, kept, kept_hbm, tokens, added, norm, bias, up_bias, qkv_w, out_w, up_w, down_w
):
    start_out, normed_out, packed, probs_out, attended_out, middle_out, second_out, active, slopes, encoded = kept

    def keep(item):
        stores.send(kept[item], kept_hbm[item])

    inner = out_w.shape[0]
    loads.wait(0)
    start = tokens[...].astype(F32) + added[...]
    start_out[...] = start
    keep(0)
    normed = (normalize(start)[0] * row(norm, 0) + row(norm, 1)).astype(BF16)
    normed_out[...] = normed
    keep(1)
    loads.wait(1)
    packed[...] = dot(normed, qkv_w[...]).astype(BF16)
    keep(2)
    columns = []
    heads = LANES // HEAD_DIM
    for group in range(inner // LANES):
        base = group * LANES
        queries = packed[:, base : base + LANES] * jnp.asarray(HEAD_DIM**-0.5, BF16)
        keys = packed[:, inner + base : inner + base + LANES]
        values = packed[:, 2 * inner + base : 2 * inner + base + LANES].T

        def weigh(head, scores, group=group, values=values):
            probs = softmax_columns(scores)
            probs_out[group * heads + head] = probs
            columns.append(dot(values[head * HEAD_DIM : (head + 1) * HEAD_DIM], probs).astype(BF16))

        staggered(
            range(heads),
            lambda head, keys=keys, queries=queries: dot_nt(keys, only_head(queries, head)),
            weigh,
        )
    keep(3)
    attended = jnp.concatenate(columns, axis=0).T
    attended_out[...] = attended
    keep(4)
    loads.wait(2)
    middle = start + (dot(attended, out_w[...]) + row(bias, 0))
    middle_out[...] = middle
    keep(5)
    second = (normalize(middle)[0] * row(norm, 2) + row(norm, 3)).astype(BF16)
    second_out[...] = second
    keep(6)
    loads.wait(3)
    panel = 768

    def bend(low, lifted):
        cols = slice(low, low + panel)
        raised, slope = gelu_pair(lifted + up_bias[:, cols].astype(F32))
        active[:, cols] = raised.astype(BF16)
        slopes[:, cols] = slope.astype(BF16)

    staggered(
        range(0, up_w.shape[1], panel), lambda low: dot(second, up_w[:, low : low + panel]), bend
    )
    keep(7)
    keep(8)
    loads.wait(4)
    encoded[...] = (middle + row(bias, 1) + dot(active[...], down_w[...])).astype(BF16)
    keep(9)


def decode_rows(
    loads, stores, kept, kept_hbm, embedded, places, pos, norm, bias, up_bias, qkv_w, out_w, up_w,
    down_w, decoded, values_t, block_sems, decoded_sems,
):
    placed, normed, packed, probs, attended, middle, second, active, slopes = kept
    length = pos.shape[0]
    inner = out_w.shape[0]
    visible = embedded.shape[0]
    heads = inner // HEAD_DIM
    blocks = length // BLOCK
    high = embedded[...].astype(BF16)
    rest = (embedded[...] - high.astype(F32)).astype(BF16)
    spots = places[:, pl.ds(0, visible)]

    def place(block):
        hit = lax.broadcasted_iota(jnp.int32, (BLOCK, visible), 0) + block * BLOCK == spots
        pick = jnp.where(hit, 1.0, 0.0).astype(BF16)
        seen = jnp.sum(jnp.where(hit, 1.0, 0.0), axis=1, keepdims=True)
        return dot(pick, high) + dot(pick, rest) + (1.0 - seen) * row(bias, 3)

    def begin(block, here):
        rows = slice(block * BLOCK, (block + 1) * BLOCK)
        here = here + pos[rows, :].astype(F32)
        placed[rows, :] = here
        norm_here = (normalize(here)[0] * row(norm, 0) + row(norm, 1)).astype(BF16)
        normed[rows, :] = norm_here
        packed[rows, :] = dot(norm_here, qkv_w[...]).astype(BF16)

    staggered(range(blocks), place, begin)
    for item in range(3):
        stores.send(kept[item], kept_hbm[1 + item])
    values_t[...] = packed[:, 2 * inner :].T
    loads.wait(9, 10, 11)
    bound = [(source, target) for source, target in zip(kept[3:], kept_hbm[4:])]

    def second_pass(block, carry):
        base = pl.multiple_of(block * BLOCK, BLOCK)
        rows = pl.ds(base, BLOCK)
        slot = lax.rem(block, 2)

        def out_copy(spot):
            return pltpu.make_async_copy(
                decoded.at[lax.rem(spot, 2)],
                kept_hbm[0].at[pl.ds(pl.multiple_of(spot * BLOCK, BLOCK), BLOCK)],
                decoded_sems.at[lax.rem(spot, 2)],
            )

        queries = packed[rows, :inner] * jnp.asarray(HEAD_DIM**-0.5, BF16)
        keys = packed[:, inner : 2 * inner]
        columns = []

        def weigh(head, scores):
            probs_here = softmax_columns(scores)
            probs[block, :, pl.ds(head * BLOCK, BLOCK)] = probs_here
            columns.append(
                dot(values_t[head * HEAD_DIM : (head + 1) * HEAD_DIM, :], probs_here).astype(BF16)
            )

        staggered(range(heads), lambda head: dot_nt(keys, only_head(queries, head)), weigh)
        attended_here = jnp.concatenate(columns, axis=0).T
        attended[rows, :] = attended_here
        middle_here = placed[rows, :] + (dot(attended_here, out_w[...]) + row(bias, 1))
        middle[rows, :] = middle_here
        second_here = (normalize(middle_here)[0] * row(norm, 2) + row(norm, 3)).astype(BF16)
        second[rows, :] = second_here
        panel = 512

        def bend(low, lifted):
            cols = slice(low, low + panel)
            raised, slope = gelu_pair(lifted + up_bias[:, cols].astype(F32))
            active[rows, cols] = raised.astype(BF16)
            slopes[rows, cols] = slope.astype(BF16)

        staggered(
            range(0, up_w.shape[1], panel),
            lambda low: dot(second_here, up_w[:, low : low + panel]),
            bend,
        )

        @pl.when(block >= 2)
        def _():
            out_copy(block - 2).wait()

        decoded[slot] = middle_here + (dot(active[rows, :], down_w[...]) + row(bias, 2))
        out_copy(block).start()
        for item, (source, target) in enumerate(bound):
            spot = rows if item else block
            pltpu.make_async_copy(source.at[spot], target.at[spot], block_sems.at[item]).start()

        @pl.when(block == blocks - 1)
        def _():
            out_copy(block - 1).wait()
            out_copy(block).wait()

        return carry

    lax.fori_loop(0, blocks, second_pass, 0)
    for item, (source, target) in enumerate(bound):
        pltpu.make_async_copy(source, target, block_sems.at[item]).wait()


WHOLE = pl.BlockSpec(memory_space=pltpu.VMEM)
APART = pl.BlockSpec(memory_space=pl.ANY)
LIMIT = pltpu.CompilerParams(vmem_limit_bytes=63 * 2**20)


def like(array):
    return pltpu.VMEM(array.shape, array.dtype)


def run_forward(tokens, order, aux, enc_w, dec_w):
    norm, qkv_w, out_w, bias, up_w, up_bias, down_w, table = enc_w
    embed_w, dec_norm, dec_qkv_w, dec_out_w, dec_bias, dec_up_w, dec_up_bias, dec_down_w, pos = dec_w
    rows, width = tokens.shape[2:]
    inner, hidden = out_w.shape[0], up_w.shape[1]
    shaped = jax.ShapeDtypeStruct
    enc_kept = [
        shaped((rows, width), F32),
        shaped((rows, width), BF16),
        shaped((rows, 3 * inner), BF16),
        shaped((inner // HEAD_DIM, rows, rows), BF16),
        shaped((rows, inner), BF16),
        shaped((rows, width), F32),
        shaped((rows, width), BF16),
        shaped((rows, hidden), BF16),
        shaped((rows, hidden), BF16),
        shaped((rows, width), BF16),
    ]
    length, dec_width = pos.shape
    dec_inner, dec_hidden = dec_out_w.shape[0], dec_up_w.shape[1]
    blocks = length // BLOCK
    dec_kept = [
        shaped((length, dec_width), F32),
        shaped((length, dec_width), BF16),
        shaped((length, 3 * dec_inner), BF16),
        shaped((blocks, length, dec_inner // HEAD_DIM * BLOCK), BF16),
        shaped((length, dec_inner), BF16),
        shaped((length, dec_width), F32),
        shaped((length, dec_width), BF16),
        shaped((length, dec_hidden), BF16),
        shaped((length, dec_hidden), BF16),
    ]
    weights = [
        qkv_w, out_w, up_w, down_w, embed_w, pos, dec_qkv_w, dec_out_w, dec_up_w, dec_down_w
    ]
    held = [like(item) for item in weights]
    results = pl.pallas_call(
        forward_kernel,
        out_shape=enc_kept + [shaped((length, dec_width), F32)] + dec_kept,
        in_specs=[WHOLE] * 5 + [APART] * 12,
        out_specs=[APART] * 20,
        scratch_shapes=[pltpu.VMEM((rows, width), BF16)]
        + held[:5]
        + [pltpu.VMEM((1, length), jnp.int32)]
        + held[5:]
        + [like(item) for item in enc_kept + dec_kept]
        + [
            pltpu.VMEM((2, BLOCK, dec_width), F32),
            pltpu.VMEM((rows, dec_width), F32),
            pltpu.VMEM((dec_inner, length), BF16),
            pltpu.SemaphoreType.DMA((12,)),
            pltpu.SemaphoreType.DMA((13,)),
            pltpu.SemaphoreType.DMA((6,)),
            pltpu.SemaphoreType.DMA((2,)),
        ],
        compiler_params=LIMIT,
        name="forward",
    )(
        aux,
        norm,
        bias,
        dec_norm,
        dec_bias,
        tokens,
        *weights[:5],
        order,
        *weights[5:],
    )
    return results[:9], results[9], results[10], results[11:]


def column_sum(values):
    return jnp.sum(values, axis=0, keepdims=True)


def norm_back(grad, values, scale):
    normal, inverse = normalize(values)
    inner = grad * scale
    mean_inner = jnp.mean(inner, axis=-1, keepdims=True)
    mean_both = jnp.mean(inner * normal, axis=-1, keepdims=True)
    return (
        inverse * (inner - mean_inner - normal * mean_both),
        column_sum(grad * normal),
        column_sum(grad),
    )


def attention_back(queries, keys, values, keys_t, probs, grad_rows, attended):
    block = queries.shape[0]
    heads = LANES // HEAD_DIM
    product = (grad_rows.astype(F32) * attended.astype(F32)).T
    scores_back, query_grads = [], []

    def through(head, probs_back):
        lanes = slice(head * HEAD_DIM, (head + 1) * HEAD_DIM)
        row_dots = column_sum(product[lanes])
        probs_here = probs[:, head * block : (head + 1) * block].astype(F32)
        scores_here = (probs_here * (probs_back - row_dots)).astype(BF16)
        scores_back.append(scores_here)
        query_grads.append(dot(keys_t[lanes], scores_here))

    staggered(range(heads), lambda head: dot_nt(values, only_head(grad_rows, head)), through)
    stacked_grad = jnp.concatenate([only_head(grad_rows, head) for head in range(heads)], axis=0)
    stacked_queries = jnp.concatenate([only_head(queries, head) for head in range(heads)], axis=0)
    grad_values = dot(probs, stacked_grad)
    grad_keys = dot(jnp.concatenate(scores_back, axis=1), stacked_queries)
    grad_queries = jnp.concatenate(query_grads, axis=0).T
    return grad_queries, grad_keys, grad_values


class Plan:
    def __init__(self, bits, blocks):
        self.bits, self.steps = bits, bits + 1
        self.waves, self.cuts = [], []
        orders, loads = orders_of(bits), [0.0, 0.0, 0.0]
        for rows, width in blocks:
            waves = []
            for wave in wave_plan(rows, width, orders, loads):
                waves.append([])
                for row_cut, col_cut, which in wave:
                    waves[-1].append((len(self.cuts), row_cut, col_cut, orders[which][0]))
                    self.cuts.append((row_cut[1], col_cut[1]))
            self.waves.append(waves)

    def scratch(self):
        lands = [
            pltpu.VMEM((2,) * (self.bits - step) + cut, BF16)
            for cut in self.cuts
            for step in range(self.steps)
        ]
        sems = pltpu.SemaphoreType.DMA((len(self.cuts), self.steps))
        return lands + [sems, sems]

    def scratch_count(self):
        return len(self.cuts) * self.steps + 2

    def bind(self, refs):
        self.refs = refs

    def chunks(self, slot, source, result):
        send_sems, recv_sems = self.refs[-2:]
        return [
            [
                Chunk(
                    source,
                    rows,
                    cols,
                    order,
                    self.refs[item * self.steps : (item + 1) * self.steps],
                    send_sems.at[item],
                    recv_sems.at[item],
                    result,
                )
                for item, rows, cols, order in wave
            ]
            for wave in self.waves[slot]
        ]


def fold(values, target):
    return values.astype(BF16).reshape(target.shape[:-1] + (values.shape[-1],))


def decode_back_kernel(plan, bits, *refs):
    (cotangent_hbm, places_hbm, norm, *refs) = refs
    load_hbm, refs = refs[:15], refs[15:]
    (returned, qkv_out, pos_out, embed_out, norm_sum, bias_sum, up_sum, *refs) = refs
    (down_done, up_done, out_done, *refs) = refs
    (cotangent, places, *refs) = refs
    load_vmem, refs = refs[:15], refs[15:]
    (
        active, down_w, slope, second, up_w, middle, attended, out_w, probs, packed,
        normed, placed, qkv_w, encoded, embed_w,
    ) = load_vmem
    (down_grad, up_grad, out_grad, grad_middle, attn_grad, grad_rows, grad_keys, grad_values,
     grad_packed, picked, load_sems, *refs) = refs
    plan.bind(refs)
    greet(bits)
    part = lax.axis_index("section")
    loads = Loads(
        [cotangent_hbm.at[part, 0], places_hbm.at[part], *load_hbm],
        [cotangent, places, *load_vmem],
        load_sems,
        6,
    )
    names = [
        "cotangent", "places", "active", "down_w", "slope", "second", "up_w", "middle", "attended",
        "out_w", "probs", "packed", "normed", "placed", "qkv_w", "encoded", "embed_w",
    ]

    def need(*wanted):
        loads.wait(*[names.index(item) for item in wanted])

    length, width = placed.shape
    inner, hidden = out_w.shape[0], up_w.shape[1]
    visible = encoded.shape[0]
    blocks = length // BLOCK
    flow = Flow(bits + 1, 2)

    def send(slot, source, result):
        for wave in plan.chunks(slot, source, result):
            flow.add(wave)

    need("cotangent", "active")
    panel = hidden // 4
    for item in range(4):
        cols = slice(item * panel, (item + 1) * panel)
        piece = dot(active[:, cols].T, cotangent[...]).astype(BF16)
        target = down_grad.at[item // 2, item % 2]
        target[...] = piece.reshape(target.shape)
    greeted(bits)
    send(0, down_grad, down_done)
    bias_sum[0:1, :] = jnp.zeros((1, width), F32)
    bias_sum[2:3, :] = column_sum(cotangent[...].astype(F32))
    need("down_w", "slope", "up_w", "middle", "out_w", "second")

    def lift_back(block):
        rows = slice(block * BLOCK, (block + 1) * BLOCK)
        lifted_back = dot_nt(cotangent[rows, :], down_w[...]) * slope[rows, :].astype(F32)
        lifted_back = lifted_back.astype(BF16)
        slope[rows, :] = lifted_back
        up_part = column_sum(lifted_back.astype(F32))
        up_sum[...] = up_part + up_sum[...] if block else up_part
        return dot_nt(lifted_back, up_w[...])

    def middle_back(block, grad_second):
        rows = slice(block * BLOCK, (block + 1) * BLOCK)
        inward, scale_part, shift_part = norm_back(grad_second, middle[rows, :], row(norm, 2))
        total = cotangent[rows, :].astype(F32) + inward
        grad_middle[rows, :] = total
        rounded = total.astype(BF16)
        attn_grad[rows, :] = rounded
        bias_part = column_sum(rounded.astype(F32))
        grad_rows[rows, :] = dot_nt(rounded, out_w[...]).astype(BF16)
        if block:
            scale_part = scale_part + norm_sum[2:3, :]
            shift_part = shift_part + norm_sum[3:4, :]
            bias_part = bias_part + bias_sum[1:2, :]
        norm_sum[2:3, :] = scale_part
        norm_sum[3:4, :] = shift_part
        bias_sum[1:2, :] = bias_part
        if block % 2:
            flow.tick()

    staggered(range(blocks), lift_back, middle_back)
    second_t = second[...].T
    for item in range(4):
        cols = slice(item * panel, (item + 1) * panel)
        up_grad[:, :, :, :, :, cols] = fold(dot(second_t, slope[:, cols]), up_grad)
    send(1, up_grad, up_done)
    need("attended")
    out_grad[...] = fold(dot(attended[...].T, attn_grad[...]), out_grad)
    send(2, out_grad, out_done)
    need("probs", "packed")
    keys = packed[:, inner : 2 * inner]
    values = packed[:, 2 * inner :]
    keys_t = keys.T
    scale = HEAD_DIM**-0.5
    for block in range(blocks):
        rows = slice(block * BLOCK, (block + 1) * BLOCK)
        query_part, key_part, value_part = attention_back(
            packed[rows, :inner], keys, values, keys_t, probs[block], grad_rows[rows, :],
            attended[rows, :],
        )
        grad_packed[rows, :inner] = (query_part * scale).astype(BF16)
        if block:
            key_part = key_part + grad_keys[...]
            value_part = value_part + grad_values[...]
        if block < blocks - 1:
            grad_keys[...] = key_part
            grad_values[...] = value_part
        else:
            grad_packed[:, inner : 2 * inner] = (key_part * scale).astype(BF16)
            grad_packed[:, 2 * inner :] = value_part.astype(BF16)
        flow.tick()
    need("normed", "placed", "qkv_w", "places")
    qkv_out[...] = fold(dot(normed[...].T, grad_packed[...]), qkv_out)
    flow.tick()
    spots = places[:, pl.ds(0, visible)]

    def start_back(block, grad_normed):
        rows = slice(block * BLOCK, (block + 1) * BLOCK)
        inward, scale_part, shift_part = norm_back(grad_normed, placed[rows, :], row(norm, 0))
        total = grad_middle[rows, :] + inward
        hit = lax.broadcasted_iota(jnp.int32, (BLOCK, visible), 0) + block * BLOCK == spots
        pick = jnp.where(hit, 1.0, 0.0).astype(BF16)
        seen = jnp.sum(jnp.where(hit, 1.0, 0.0), axis=1, keepdims=True)
        fill_part = column_sum(total * (1.0 - seen))
        rounded = total.astype(BF16)
        pick_part = dot(pick.T, rounded)
        if block:
            scale_part = scale_part + norm_sum[0:1, :]
            shift_part = shift_part + norm_sum[1:2, :]
            fill_part = fill_part + bias_sum[3:4, :]
            pick_part = pick_part + picked[...]
        norm_sum[0:1, :] = scale_part
        norm_sum[1:2, :] = shift_part
        bias_sum[3:4, :] = fill_part
        picked[...] = pick_part
        pos_out[:, :, :, :, :, rows] = fold(rounded.T, pos_out)
        flow.tick()

    staggered(
        range(blocks),
        lambda block: dot_nt(grad_packed[block * BLOCK : (block + 1) * BLOCK, :], qkv_w[...]),
        start_back,
    )
    need("encoded", "embed_w")
    grad_embedded = picked[...].astype(BF16)
    bias_sum[0:1, :] = column_sum(picked[...])
    embed_out[...] = fold(dot(encoded[...].T, grad_embedded), embed_out)
    returned[...] = dot_nt(grad_embedded, embed_w[...]).astype(BF16)
    flow.drain()


def encode_back_kernel(plan, bits, *refs):
    (returned, aux, norm, dec_norm_sum, dec_bias_sum, dec_up_sum, *refs) = refs
    early, refs = refs[:3], refs[3:]
    load_hbm, refs = refs[:13], refs[13:]
    (input_grad, small_done, *refs) = refs
    done, refs = refs[:7], refs[7:]
    load_vmem, refs = refs[:13], refs[13:]
    (
        active, down_w, slope, second, up_w, middle, attended, out_w, probs, packed,
        normed, start, qkv_w,
    ) = load_vmem
    (down_grad, up_grad, out_grad, qkv_grad, grad_packed, small, small_lands, small_send,
     small_recv, load_sems, *refs) = refs
    plan.bind(refs)
    greet(bits)
    loads = Loads(load_hbm, load_vmem, load_sems, 6)
    names = [
        "active", "down_w", "slope", "second", "up_w", "middle", "attended", "out_w", "probs",
        "packed", "normed", "start", "qkv_w",
    ]

    def need(*wanted):
        loads.wait(*[names.index(item) for item in wanted])

    inner, hidden = out_w.shape[0], up_w.shape[1]
    width = start.shape[1]
    greeted(bits)
    flow = Flow(bits + 1, 2)

    def send(slot, source, result, part=None):
        waves = plan.chunks(slot, source, result)
        for wave in waves if part is None else waves[part : part + 1]:
            flow.add(wave)

    for slot, source in enumerate(early):
        send(slot, source, done[slot])
    branch = returned[...]
    small[...] = jnp.zeros_like(small)
    small[5:6, :] = column_sum(branch.astype(F32))
    need("active")
    panel = hidden // 4
    for item in range(4):
        cols = slice(item * panel, (item + 1) * panel)
        target = down_grad.at[item // 2, item % 2]
        target[...] = dot(active[:, cols].T, branch).astype(BF16).reshape(target.shape)
    flow.tick()
    send(3, down_grad, done[3], 0)
    need("second", "slope", "down_w")
    second_t = second[...].T
    for item in range(4):
        cols = slice(item * panel, (item + 1) * panel)
        lifted_back = (dot_nt(branch, down_w[cols, :]) * slope[:, cols].astype(F32)).astype(BF16)
        slope[:, cols] = lifted_back
        small[10 + item : 11 + item, :] = column_sum(lifted_back.astype(F32))
        up_grad[:, :, :, :, :, cols] = fold(dot(second_t, lifted_back), up_grad)
    flow.tick()
    send(3, down_grad, done[3], 1)
    need("up_w", "middle", "out_w", "attended")
    grad_second = dot_nt(slope[...], up_w[...])
    inward, small[2:3, :], small[3:4, :] = norm_back(grad_second, middle[...], row(norm, 2))
    grad_middle = branch.astype(F32) + inward
    attn_grad = grad_middle.astype(BF16)
    small[4:5, :] = column_sum(attn_grad.astype(F32))
    flow.tick()
    send(4, up_grad, done[4], 0)
    out_grad[...] = fold(dot(attended[...].T, attn_grad), out_grad)
    grad_rows = dot_nt(attn_grad, out_w[...]).astype(BF16)
    flow.tick()
    send(4, up_grad, done[4], 1)
    need("probs", "packed")
    scale = HEAD_DIM**-0.5
    heads = LANES // HEAD_DIM
    for group in range(inner // LANES):
        base = group * LANES
        lanes = slice(base, base + LANES)
        keys = packed[:, inner + base : inner + base + LANES]
        query_part, key_part, value_part = attention_back(
            packed[:, lanes],
            keys,
            packed[:, 2 * inner + base : 2 * inner + base + LANES],
            keys.T,
            jnp.concatenate([probs[group * heads + head] for head in range(heads)], axis=1),
            grad_rows[:, lanes],
            attended[:, lanes],
        )
        grad_packed[:, lanes] = (query_part * scale).astype(BF16)
        grad_packed[:, inner + base : inner + base + LANES] = (key_part * scale).astype(BF16)
        grad_packed[:, 2 * inner + base : 2 * inner + base + LANES] = value_part.astype(BF16)
    flow.tick()
    need("normed", "start", "qkv_w")
    send(5, out_grad, done[5])
    normed_t = normed[...].T
    for item in range(3):
        cols = slice(item * inner, (item + 1) * inner)
        qkv_grad[:, :, :, :, :, cols] = fold(dot(normed_t, grad_packed[:, cols]), qkv_grad)
    flow.tick()
    send(6, qkv_grad, done[6])
    grad_normed = dot_nt(grad_packed[...], qkv_w[...])
    inward, small[0:1, :], small[1:2, :] = norm_back(grad_normed, start[...], row(norm, 0))
    grad_start = grad_middle + inward
    input_grad[...] = grad_start
    small[6:10, :] = aux[4:8, : start.shape[1]] * column_sum(grad_start)
    dec_width = dec_norm_sum.shape[1]
    small[14:18, :dec_width] = dec_norm_sum[...]
    small[18:22, :dec_width] = dec_bias_sum[...]
    for item in range(4):
        small[22 + item : 23 + item, :dec_width] = dec_up_sum[
            :, item * dec_width : (item + 1) * dec_width
        ]
    flow.add([Whole(small, bits, small_lands, small_send, small_recv, small_done)])
    flow.drain()


def finish_kernel(counts, *refs):
    small_count, big_count = counts
    small, big, refs = refs[0], refs[1 : 1 + big_count], refs[1 + big_count :]
    tiny, big_out, sems = refs[:small_count], refs[small_count:-1], refs[-1]
    copies = [
        pltpu.make_async_copy(source, target, sems.at[item])
        for item, (source, target) in enumerate(zip(big, big_out))
    ]
    for copy in copies:
        copy.start()
    section, data = lax.axis_index("section"), lax.axis_index("dp")
    datas = lax.axis_size("dp")
    first = 0
    for out in tiny:
        cols = out.shape[-1]
        if out.shape[0] > 1 or first == 4:
            lines = out.shape[0]
            width = cols * datas
            here = jnp.where(
                section == 0,
                small[first : first + lines, :width],
                small[first + lines : first + 2 * lines, :width],
            )
            spot = data * cols
            first += 2 * lines
        else:
            lines = 4
            width = cols * datas * 2 // lines
            per_line = width // cols
            index = section * datas + data
            here = jnp.zeros((1, width), F32)
            for line in range(lines):
                mine = index // per_line == line
                here = here + jnp.where(mine, small[first + line : first + line + 1, :width], 0.0)
            spot = lax.rem(index, per_line) * cols
            first += lines
        here = pltpu.roll(here, lax.rem(width - spot, width), 1)
        out[...] = here[:, :cols]
    for copy in copies:
        copy.wait()


def run_finish(small, big, shapes):
    shaped = jax.ShapeDtypeStruct
    return pl.pallas_call(
        partial(finish_kernel, (len(shapes), len(big))),
        out_shape=[shaped(item, F32) for item in shapes]
        + [shaped(item.shape, F32) for item in big],
        in_specs=[WHOLE] + [APART] * len(big),
        out_specs=[WHOLE] * (len(shapes) + len(big)),
        scratch_shapes=[pltpu.SemaphoreType.DMA((len(big),))],
        name="finish",
    )(small, *big)


def communicating(number):
    return pltpu.CompilerParams(
        collective_id=number, has_side_effects=True, vmem_limit_bytes=63 * 2**20
    )


def blocked(rows, cols, bits):
    return (2,) * bits + (rows // 2**bits, cols)


def run_decode_back(cotangent, order, stored, encoded, dec_w, bits):
    embed_w, norm, qkv_w, out_w, bias, up_w, up_bias, down_w, pos = dec_w
    placed, normed, packed, probs, attended, middle, second, active, slope = stored
    length, width = pos.shape
    inner, hidden = out_w.shape[0], up_w.shape[1]
    shaped = jax.ShapeDtypeStruct
    loaded = [
        active, down_w, slope, second, up_w, middle, attended, out_w, probs, packed, normed,
        placed, qkv_w, encoded, embed_w,
    ]
    sent = [blocked(*item.shape, bits) for item in (down_w, up_w, out_w)]
    plan = Plan(bits, [(item[-2], item[-1] // 2) for item in sent])
    later = [blocked(*qkv_w.shape, bits), blocked(width, length, bits), blocked(*embed_w.shape, bits)]
    return pl.pallas_call(
        partial(decode_back_kernel, plan, bits),
        out_shape=[shaped(encoded.shape, BF16)]
        + [shaped(item, BF16) for item in later]
        + [shaped((4, width), F32), shaped((4, width), F32), shaped((1, hidden), F32)]
        + [shaped((item[-2], item[-1] // 2), F32) for item in sent],
        in_specs=[APART, APART, WHOLE] + [APART] * len(loaded),
        out_specs=[WHOLE] * 10,
        scratch_shapes=[
            pltpu.VMEM((length, width), BF16),
            pltpu.VMEM((1, length), jnp.int32),
        ]
        + [like(item) for item in loaded]
        + [pltpu.VMEM(item, BF16) for item in sent]
        + [
            pltpu.VMEM((length, width), F32),
            pltpu.VMEM((length, width), BF16),
            pltpu.VMEM((length, inner), BF16),
            pltpu.VMEM((length, inner), F32),
            pltpu.VMEM((length, inner), F32),
            pltpu.VMEM((length, 3 * inner), BF16),
            pltpu.VMEM((encoded.shape[0], width), F32),
            pltpu.SemaphoreType.DMA((len(loaded) + 2,)),
        ]
        + plan.scratch(),
        compiler_params=communicating(1),
        name="decode_back",
    )(cotangent, order, norm, *loaded)


def run_encode_back(returned, aux, stored, enc_w, early, dec_sums, bits):
    norm, qkv_w, out_w, bias, up_w, up_bias, down_w, table = enc_w
    start, normed, packed, probs, attended, middle, second, active, slope = stored
    shaped = jax.ShapeDtypeStruct
    loaded = [
        active, down_w, slope, second, up_w, middle, attended, out_w, probs, packed, normed,
        start, qkv_w,
    ]
    own = [blocked(*item.shape, bits) for item in (down_w, up_w, out_w, qkv_w)]
    sent = [item.shape for item in early] + own
    plan = Plan(bits, [(item[-2], item[-1] // 2) for item in sent])
    width = start.shape[1]
    small = (SMALL_ROWS, width)
    return pl.pallas_call(
        partial(encode_back_kernel, plan, bits),
        out_shape=[shaped(start.shape, F32), shaped(small, F32)]
        + [shaped((item[-2], item[-1] // 2), F32) for item in sent],
        in_specs=[WHOLE] * 9 + [APART] * len(loaded),
        out_specs=[WHOLE] * 9,
        scratch_shapes=[like(item) for item in loaded]
        + [pltpu.VMEM(item, BF16) for item in own]
        + [
            pltpu.VMEM(packed.shape, BF16),
            pltpu.VMEM(small, F32),
            pltpu.VMEM((bits + 1,) + small, F32),
            pltpu.SemaphoreType.DMA((bits + 1,)),
            pltpu.SemaphoreType.DMA((bits + 1,)),
            pltpu.SemaphoreType.DMA((len(loaded),)),
        ]
        + plan.scratch(),
        compiler_params=communicating(2),
        name="encode_back",
    )(returned, aux, norm, *dec_sums, *early, *loaded)


def local_rows(whole, shape):
    section, data = lax.axis_index("section"), lax.axis_index("dp")
    sections, datas = lax.axis_size("section"), lax.axis_size("dp")
    if len(shape) == 1:
        count = shape[0] // (sections * datas)
        return lax.dynamic_slice_in_dim(
            whole.reshape(-1)[: shape[0]], (section * datas + data) * count, count, 0
        )
    rows, cols = shape[0] // sections, shape[1] // datas
    return lax.dynamic_slice(whole, (section * rows, data * cols), (rows, cols))


def plain_shards(tokens, order, sensor, cotangent, enc_w, dec_w):
    section_count = lax.axis_size("section")
    section_index = lax.axis_index("section")
    half_count = tokens.shape[0] // section_count

    def mine(array):
        part = lax.dynamic_slice_in_dim(array, section_index * half_count, half_count, 0)
        return part.reshape((half_count * array.shape[1],) + array.shape[2:])

    encoded, stored, picks = encode(mine(tokens), mine(sensor), enc_w)
    output, returned, dec_grads = decode(encoded, mine(order), mine(cotangent), dec_w)
    grad_input, enc_grads = encode_back(stored, picks, returned, enc_w)
    done = []
    for slot, grad in enumerate(enc_grads + dec_grads):
        if slot in (0, 3, 5, 7, 9, 12, 14):
            total = local_rows(lax.psum(grad, ("section", "dp")), grad.shape)
        else:
            side = 0 if slot == 16 else 1
            total = lax.psum_scatter(
                grad.astype(jnp.bfloat16), "section", scatter_dimension=side, tiled=True
            )
            total = lax.psum_scatter(total, "dp", scatter_dimension=1 - side, tiled=True)
        done.append(total.astype(jnp.float32))
    decoded = output.reshape((half_count,) + cotangent.shape[1:])
    input_grad = grad_input.reshape((half_count,) + tokens.shape[1:])
    return (decoded, input_grad) + tuple(done)


def shards(tokens, order, sensor, cotangent, *weights):
    enc_w, dec_w = weights[:8], weights[8:]
    sections, datas = lax.axis_size("section"), lax.axis_size("dp")
    split_rows = [enc_w[1], enc_w[2], enc_w[4], enc_w[6], dec_w[0], dec_w[2], dec_w[3], dec_w[5]]
    fits = (
        sections == 2
        and tokens.shape[:2] == (sections, 1)
        and datas & (datas - 1) == 0
        and datas >= 4
        and all(item.shape[0] % (16 * datas) == 0 for item in split_rows)
    )
    if not fits:
        return plain_shards(tokens, order, sensor, cotangent, enc_w, dec_w)
    bits = datas.bit_length() - 1
    kind = lax.dynamic_index_in_dim(sensor, lax.axis_index("section"), 0, keepdims=False)
    kinds = (jnp.arange(enc_w[7].shape[0]) == kind).astype(F32)[:, None]
    hidden = enc_w[4].shape[1]

    def wide(item):
        return jnp.pad(item, ((0, 0), (0, hidden - item.shape[1])))

    aux = jnp.concatenate(
        [
            enc_w[5].astype(F32)[None],
            wide(dec_w[6].astype(F32)[None]),
            wide(jnp.sum(kinds * enc_w[7].astype(F32), axis=0, keepdims=True)),
            jnp.zeros((1, hidden), F32),
            jnp.broadcast_to(kinds, (kinds.shape[0], hidden)),
        ]
    )
    enc_kept, encoded, decoded, dec_kept = run_forward(tokens, order, aux, enc_w, dec_w)
    back = run_decode_back(cotangent, order, dec_kept, encoded, dec_w, bits)
    returned, early, dec_sums, dec_done = back[0], back[1:4], back[4:7], back[7:]
    down_dec, up_dec, out_dec = dec_done
    input_grad, small, *rest = run_encode_back(
        returned, aux, enc_kept, enc_w, early, dec_sums, bits
    )
    qkv_dec, pos, embed, down, up, out, qkv = rest
    tiny_slots = (0, 3, 7, 5, 9, 12, 14)
    shapes = [
        (item.shape[0] // 2, item.shape[1] // datas)
        if item.ndim == 2
        else (1, item.shape[0] // (2 * datas))
        for item in (weights[slot] for slot in tiny_slots)
    ]
    large = {
        1: qkv, 2: out, 4: up, 6: down, 8: embed, 10: qkv_dec, 11: out_dec, 13: up_dec, 15: down_dec,
        16: pos,
    }
    results = run_finish(small, [input_grad, *large.values()], shapes)
    done = dict(zip([*tiny_slots, "input", *large], results))
    for slot in (5, 14):
        done[slot] = done[slot].reshape(-1)
    done[16] = done[16].T
    return (decoded[None, None], done["input"][None, None]) + tuple(
        done[slot] for slot in range(17)
    )


def solution(mesh):
    placed = (
        P(None, "dp", None, None),
        P(None, "dp", None),
        P(None, "dp"),
        P(None, "dp", None, None),
        P(),
        P(),
        P(),
        P(),
        P(),
        P(),
        P(),
        P(),
        P(),
        P(),
        P(),
        P(),
        P(),
        P(),
        P(),
        P(),
        P(),
    )
    return jax.shard_map(
        shards,
        mesh=mesh,
        in_specs=placed,
        out_specs=(
            P("section", "dp", None, None),
            P("section", "dp", None, None),
            P("section", "dp"),
            P("dp", "section"),
            P("dp", "section"),
            P("section", "dp"),
            P("dp", "section"),
            P(("section", "dp")),
            P("dp", "section"),
            P("section", "dp"),
            P("dp", "section"),
            P("section", "dp"),
            P("dp", "section"),
            P("dp", "section"),
            P("section", "dp"),
            P("dp", "section"),
            P(("section", "dp")),
            P("dp", "section"),
            P("section", "dp"),
        ),
        check_vma=False,
    )
```

```python
import heapq
import math
from functools import partial

import jax
import jax.numpy as jnp
from jax import lax
from jax.experimental import pallas as pl
from jax.experimental.pallas import tpu as pltpu
from jax.sharding import PartitionSpec as P

HEAD_DIM = 64
MESH = pl.DeviceIdType.MESH
SMALL_ROWS = 32


def layer_norm(hidden, scales, shifts):
    center = hidden - jnp.mean(hidden, axis=-1, keepdims=True)
    spread = jnp.mean(center * center, axis=-1, keepdims=True)
    return center * lax.rsqrt(spread + 1e-05) * scales + shifts


def matmul(left_side, right_side):
    return jnp.dot(left_side, right_side, preferred_element_type=jnp.float32)


def row_contract(left_side, right_side):
    return lax.dot_general(
        left_side, right_side, (((0,), (0,)), ((), ())), preferred_element_type=jnp.float32
    )


def col_contract(left_side, right_side):
    return lax.dot_general(
        left_side, right_side, (((1,), (1,)), ((), ())), preferred_element_type=jnp.float32
    )


def gelu_exact(values):
    return jax.nn.gelu(values, approximate=False)


def block_forward(hidden, weights):
    norms, qkv_w, out_w, biases, up_w, up_bias, down_w = weights
    batch_size, length, feature_width = hidden.shape
    row_count = batch_size * length
    head_count = qkv_w.shape[1] // (3 * HEAD_DIM)
    inner_width = head_count * HEAD_DIM
    norm_rows = norms.astype(jnp.float32)
    bias_rows = biases.astype(jnp.float32)
    normed = (
        layer_norm(hidden, norm_rows[0], norm_rows[1])
        .astype(jnp.bfloat16)
        .reshape(row_count, feature_width)
    )
    packed = (
        matmul(normed, qkv_w)
        .astype(jnp.bfloat16)
        .reshape(batch_size, length, 3, head_count, HEAD_DIM)
    )
    queries = packed[:, :, 0]
    keys_all = packed[:, :, 1]
    values_all = packed[:, :, 2]
    scores = jnp.einsum(
        "bqhd,bkhd->bhqk", queries, keys_all, preferred_element_type=jnp.float32
    ) * HEAD_DIM ** (-0.5)
    row_peak = jnp.max(scores, axis=-1, keepdims=True)
    logsum = row_peak + jnp.log(jnp.sum(jnp.exp(scores - row_peak), axis=-1, keepdims=True))
    probability = jnp.exp(scores - logsum).astype(jnp.bfloat16)
    attended = jnp.einsum(
        "bhqk,bkhd->bqhd", probability, values_all, preferred_element_type=jnp.float32
    )
    attended = attended.astype(jnp.bfloat16).reshape(row_count, inner_width)
    middle = hidden + (matmul(attended, out_w) + bias_rows[0]).reshape(
        batch_size, length, feature_width
    )
    second = (
        layer_norm(middle, norm_rows[2], norm_rows[3])
        .astype(jnp.bfloat16)
        .reshape(row_count, feature_width)
    )
    lifted = matmul(second, up_w) + up_bias.astype(jnp.float32)
    active = gelu_exact(lifted).astype(jnp.bfloat16)
    output = middle + (matmul(active, down_w) + bias_rows[1]).reshape(
        batch_size, length, feature_width
    )
    stored = (hidden, normed, packed, logsum, attended, middle, second, lifted, active)
    return (output, stored)


def block_backward(stored, upstream, weights):
    norms, qkv_w, out_w, biases, up_w, up_bias, down_w = weights
    hidden, normed, packed, logsum, attended, middle, second, lifted, active = stored
    batch_size, length, feature_width = hidden.shape
    row_count = batch_size * length
    head_count = qkv_w.shape[1] // (3 * HEAD_DIM)
    inner_width = head_count * HEAD_DIM
    score_scale = HEAD_DIM ** (-0.5)
    norm_rows = norms.astype(jnp.float32)
    branch_grad = upstream.reshape(row_count, feature_width).astype(jnp.bfloat16)
    grad_down = row_contract(active, branch_grad)
    grad_bias_down = jnp.sum(branch_grad.astype(jnp.float32), axis=0)
    grad_active = col_contract(branch_grad, down_w)
    grad_lifted = jax.vjp(gelu_exact, lifted)[1](grad_active)[0].astype(jnp.bfloat16)
    grad_up = row_contract(second, grad_lifted)
    grad_up_bias = jnp.sum(grad_lifted.astype(jnp.float32), axis=0)
    grad_second = col_contract(grad_lifted, up_w).reshape(batch_size, length, feature_width)
    grad_middle, grad_scale_two, grad_shift_two = jax.vjp(
        layer_norm, middle, norm_rows[2], norm_rows[3]
    )[1](grad_second)
    grad_middle = upstream + grad_middle
    attn_grad = grad_middle.reshape(row_count, feature_width).astype(jnp.bfloat16)
    grad_out = row_contract(attended, attn_grad)
    grad_bias_out = jnp.sum(attn_grad.astype(jnp.float32), axis=0)
    grad_attended = (
        col_contract(attn_grad, out_w)
        .astype(jnp.bfloat16)
        .reshape(batch_size, length, head_count, HEAD_DIM)
    )
    queries = packed[:, :, 0]
    keys_all = packed[:, :, 1]
    values_all = packed[:, :, 2]
    scores = (
        jnp.einsum("bqhd,bkhd->bhqk", queries, keys_all, preferred_element_type=jnp.float32)
        * score_scale
    )
    probability = jnp.exp(scores - logsum)
    grad_probs = jnp.einsum(
        "bqhd,bkhd->bhqk", grad_attended, values_all, preferred_element_type=jnp.float32
    )
    grad_values = jnp.einsum(
        "bhqk,bqhd->bkhd",
        probability.astype(jnp.bfloat16),
        grad_attended,
        preferred_element_type=jnp.float32,
    )
    row_dots = jnp.sum(grad_probs * probability, axis=-1, keepdims=True)
    grad_scores = (probability * (grad_probs - row_dots)).astype(jnp.bfloat16)
    grad_queries = (
        jnp.einsum("bhqk,bkhd->bqhd", grad_scores, keys_all, preferred_element_type=jnp.float32)
        * score_scale
    )
    grad_keys = (
        jnp.einsum("bhqk,bqhd->bkhd", grad_scores, queries, preferred_element_type=jnp.float32)
        * score_scale
    )
    grad_packed = (
        jnp.stack([grad_queries, grad_keys, grad_values], axis=2)
        .astype(jnp.bfloat16)
        .reshape(row_count, 3 * inner_width)
    )
    grad_qkv = row_contract(normed, grad_packed)
    grad_normed = col_contract(grad_packed, qkv_w).reshape(batch_size, length, feature_width)
    grad_hidden, grad_scale_one, grad_shift_one = jax.vjp(
        layer_norm, hidden, norm_rows[0], norm_rows[1]
    )[1](grad_normed)
    grad_hidden = grad_middle + grad_hidden
    grad_norms = jnp.stack([grad_scale_one, grad_shift_one, grad_scale_two, grad_shift_two])
    grad_biases = jnp.stack([grad_bias_out, grad_bias_down])
    return (
        grad_hidden,
        (grad_norms, grad_qkv, grad_out, grad_biases, grad_up, grad_up_bias, grad_down),
    )


def encode(tokens_part, sensor_part, enc_w):
    table = enc_w[7].astype(jnp.float32)
    picks = (sensor_part[:, None] == jnp.arange(table.shape[0])[None, :]).astype(jnp.float32)
    start = (
        tokens_part.astype(jnp.float32)
        + jnp.sum(picks[:, :, None] * table[None], axis=1)[:, None, :]
    )
    output, stored = block_forward(start, enc_w[:7])
    return (output.astype(jnp.bfloat16), stored, picks)


def encode_back(stored, picks, returned, enc_w):
    grad_input, grads = block_backward(stored, returned.astype(jnp.float32), enc_w[:7])
    grad_table = jnp.sum(picks[:, :, None] * jnp.sum(grad_input, axis=1)[:, None, :], axis=0)
    return (grad_input, grads + (grad_table,))


def decode(arrived, place, cotangent_part, dec_w):
    dec_embed, dec_norm, dec_qkv, dec_out, dec_bias, dec_up, dec_up_bias, dec_down, dec_pos = dec_w
    batch_size, visible, model_width = arrived.shape
    patches = place.shape[1]
    bias_rows = dec_bias.astype(jnp.float32)
    flat_rows = arrived.reshape(batch_size * visible, model_width)
    embedded = (matmul(flat_rows, dec_embed) + bias_rows[0]).reshape(
        batch_size, visible, bias_rows.shape[1]
    )
    filler = jnp.broadcast_to(bias_rows[3], (batch_size, patches - visible, bias_rows.shape[1]))
    sequence = jnp.concatenate([embedded, filler], axis=1)
    image_rows = jnp.arange(batch_size)[:, None]
    placed = jnp.zeros_like(sequence).at[image_rows, place].set(sequence) + dec_pos.astype(
        jnp.float32
    )
    block_w = (dec_norm, dec_qkv, dec_out, bias_rows[1:3], dec_up, dec_up_bias, dec_down)
    output, stored = block_forward(placed, block_w)
    grad_placed, grads = block_backward(stored, cotangent_part.astype(jnp.float32), block_w)
    grad_pos = jnp.sum(grad_placed, axis=0)
    grad_sequence = jnp.take_along_axis(grad_placed, place[:, :, None], axis=1)
    grad_embedded = (
        grad_sequence[:, :visible]
        .reshape(batch_size * visible, bias_rows.shape[1])
        .astype(jnp.bfloat16)
    )
    grad_filler = jnp.sum(grad_sequence[:, visible:], axis=(0, 1))
    grad_embed = row_contract(flat_rows, grad_embedded)
    grad_bias_embed = jnp.sum(grad_embedded.astype(jnp.float32), axis=0)
    returned = (
        col_contract(grad_embedded, dec_embed)
        .astype(jnp.bfloat16)
        .reshape(batch_size, visible, model_width)
    )
    grad_norms, grad_qkv, grad_out, grad_biases, grad_up, grad_up_bias, grad_down = grads
    grad_bias = jnp.stack([grad_bias_embed, grad_biases[0], grad_biases[1], grad_filler])
    return (
        output,
        returned,
        (
            grad_embed,
            grad_norms,
            grad_qkv,
            grad_out,
            grad_bias,
            grad_up,
            grad_up_bias,
            grad_down,
            grad_pos,
        ),
    )


CORE = -1


def partner_of(stage):
    section, data = lax.axis_index("section"), lax.axis_index("dp")
    if stage == CORE:
        return (1 - section, data)
    weight = 2**stage
    bit = lax.rem(data // weight, 2)
    return (section, data + weight * (1 - 2 * bit))


def bit_of(stage):
    if stage == CORE:
        return lax.axis_index("section")
    return lax.rem(lax.axis_index("dp") // 2**stage, 2)


def greet(bits):
    barrier = pltpu.get_barrier_semaphore()
    for stage in [CORE] + list(range(bits)):
        pl.semaphore_signal(barrier, inc=1, device_id=partner_of(stage), device_id_type=MESH)


def greeted(bits):
    pl.semaphore_wait(pltpu.get_barrier_semaphore(), bits + 1)


class Chunk:
    def __init__(self, source, rows, cols, stages, dims, lands, send_sems, recv_sems, result):
        self.source, self.rows, self.cols, self.stages = source, rows, cols, stages
        self.lands, self.send_sems, self.recv_sems = lands, send_sems, recv_sems
        self.result, self.dims = result, dims

    def halves(self, step):
        stage = self.stages[step]
        bit = bit_of(stage)
        if stage == CORE:
            width = self.source.shape[-1] // 2
            start, extent = self.cols

            def part(side):
                offset = pl.multiple_of(side * width + start, 128)
                return self.source.at[
                    (slice(None),) * len(self.dims)
                    + (pl.ds(self.rows[0], self.rows[1]), pl.ds(offset, extent))
                ]

            return part(1 - bit), part(bit)
        held = self.lands[step - 1] if step else self.source
        left = [item for item in self.dims if item not in self.stages[:step]]
        place = left.index(stage)

        def part(side):
            return held.at[(slice(None),) * place + (side,)]

        return part(1 - bit), part(bit)

    def copy(self, step):
        return pltpu.make_async_remote_copy(
            src_ref=self.halves(step)[0],
            dst_ref=self.lands[step],
            send_sem=self.send_sems[step],
            recv_sem=self.recv_sems[step],
            device_id=partner_of(self.stages[step]),
            device_id_type=MESH,
        )

    def start(self, step):
        self.copy(step).start()

    def finish(self, step):
        self.copy(step).wait_recv()
        kept, land = self.halves(step)[1], self.lands[step]
        if step + 1 < len(self.stages):
            land[...] = land[...] + kept[...]
            self.start(step + 1)
        elif len(land.shape) > 2:
            self.result[...] = land[...] + kept[...]
        else:
            self.result[pl.ds(*self.rows), pl.ds(*self.cols)] = land[...].astype(
                jnp.float32
            ) + kept[...].astype(jnp.float32)

    def close(self):
        for step in range(len(self.stages)):
            self.copy(step).wait_send()


class Whole:
    def __init__(self, source, bits, lands, send_sems, recv_sems, result):
        self.source, self.lands, self.send_sems, self.recv_sems = source, lands, send_sems, recv_sems
        self.stages = [CORE] + list(range(bits))
        self.result = result

    def held(self, step):
        return self.source if step == 0 else self.lands.at[step - 1]

    def copy(self, step):
        return pltpu.make_async_remote_copy(
            src_ref=self.held(step),
            dst_ref=self.lands.at[step],
            send_sem=self.send_sems.at[step],
            recv_sem=self.recv_sems.at[step],
            device_id=partner_of(self.stages[step]),
            device_id_type=MESH,
        )

    def start(self, step):
        self.copy(step).start()

    def finish(self, step):
        self.copy(step).wait_recv()
        total = self.lands[step] + self.held(step)[...]
        if step == len(self.stages) - 1:
            self.result[...] = total
        else:
            self.lands[step] = total
            self.start(step + 1)

    def close(self):
        for step in range(len(self.stages)):
            self.copy(step).wait_send()


class Flow:
    def __init__(self, lag):
        self.lag, self.waves, self.tick_now = lag, [], 0

    def add(self, chunks):
        for chunk in chunks:
            chunk.start(0)
        self.waves.append([chunks, 0, self.tick_now + 1])

    def tick(self):
        self.tick_now += 1
        for wave in self.waves:
            chunks, step, due = wave
            if step < len(chunks[0].stages) and due <= self.tick_now:
                for chunk in chunks:
                    chunk.finish(step)
                wave[1], wave[2] = step + 1, self.tick_now + self.lag

    def drain(self):
        while any(step < len(chunks[0].stages) for chunks, step, _ in self.waves):
            self.tick()
        for chunks, _, _ in self.waves:
            for chunk in chunks:
                chunk.close()


def orders_of(bits):
    near = bits // 3
    x, y, z = list(range(near)), list(range(near, 2 * near)), list(range(2 * near, bits))
    return [
        ([CORE] + x + y + z, (0.5, 0.25, 0.1875)),
        ([CORE] + y + x + z, (0.25, 0.5, 0.1875)),
        ([CORE] + z + x + y, (0.125, 0.0625, 0.75)),
        ([CORE] + z + y + x, (0.0625, 0.125, 0.75)),
    ]


def wave_plan(rows, width, orders, loads):
    by_rows = rows >= 128
    unit = 16 if by_rows else 128
    strips = (rows if by_rows else width) // unit
    count = 2 if rows * width > 48 * 1024 else 1
    waves = []
    for item in range(count):
        low, high = strips * item // count, strips * (item + 1) // count
        taken = []
        for _ in range(low, high):
            totals = [
                [old + new * rows * width / strips for old, new in zip(loads, cost)]
                for _, cost in orders
            ]
            best = min(range(len(orders)), key=lambda which: max(totals[which]))
            loads[:] = totals[best]
            taken.append(best)
        wave = []
        for which in sorted(set(taken)):
            extent = taken.count(which)
            cut = (low * unit, extent * unit)
            low += extent
            wave.append((cut, (0, width), which) if by_rows else ((0, rows), cut, which))
        waves.append(wave)
    return waves


F32, BF16 = jnp.float32, jnp.bfloat16
BLOCK = 256
LANES = 256


def dot(left, right):
    return jnp.dot(left, right, preferred_element_type=F32)


def dot_nt(left, right):
    return lax.dot_general(left, right, (((1,), (1,)), ((), ())), preferred_element_type=F32)


def head_of_lane(rows, width=LANES):
    return lax.broadcasted_iota(jnp.int32, (rows, width), 1) // HEAD_DIM


def only_head(rows, head):
    lane = lax.broadcasted_iota(jnp.int32, rows.shape, 1)
    keep = (lane >= head * HEAD_DIM) & (lane < (head + 1) * HEAD_DIM)
    return jnp.where(keep, rows, jnp.zeros_like(rows))


def normalize(values):
    center = values - jnp.mean(values, axis=-1, keepdims=True)
    inverse = lax.rsqrt(jnp.mean(center * center, axis=-1, keepdims=True) + 1e-05)
    return center * inverse, inverse


def gelu_pair(values):
    area = 0.5 + 0.5 * lax.erf(values * 0.7071067811865476)
    slope = jnp.exp(values * values * -0.5) * 0.3989422804014327
    return values * area, area + values * slope


def softmax_columns(scores):
    peak = jnp.max(scores, axis=0, keepdims=True)
    raised = jnp.exp(scores - peak)
    return (raised * (1.0 / jnp.sum(raised, axis=0, keepdims=True))).astype(BF16)


def staggered(items, produce, consume):
    held = None
    for item in items:
        made = produce(item)
        if held is not None:
            consume(*held)
        held = (item, made)
    consume(*held)


class Loads:
    def __init__(self, sources, targets, sems, ahead):
        self.copies = [
            pltpu.make_async_copy(source, target, sems.at[item])
            for item, (source, target) in enumerate(zip(sources, targets))
        ]
        self.ahead, self.started = ahead, 0
        self.reach(ahead)

    def reach(self, count):
        for copy in self.copies[self.started : count]:
            copy.start()
        self.started = max(self.started, min(count, len(self.copies)))

    def wait(self, *items):
        for item in items:
            self.reach(item + 1 + self.ahead)
            self.copies[item].wait()


class Stores:
    def __init__(self, sems):
        self.sems, self.copies = sems, []

    def send(self, source, target):
        copy = pltpu.make_async_copy(source, target, self.sems.at[len(self.copies)])
        copy.start()
        self.copies.append(copy)

    def close(self):
        for copy in self.copies:
            copy.wait()


def line(ref, cols):
    return ref[cols].astype(F32).reshape(1, -1)


def row(ref, index):
    return ref[pl.ds(index, 1), :].astype(F32)


def forward_kernel(*refs):
    (sensor, norm, bias, up_bias, table, dec_norm, dec_bias, dec_up_bias, *refs) = refs
    load_hbm, refs = refs[:12], refs[12:]
    store_hbm, refs = refs[:20], refs[20:]
    load_vmem, refs = refs[:12], refs[12:]
    (
        tokens, qkv_w, out_w, up_w, down_w, embed_w, places, pos, dec_qkv_w, dec_out_w, dec_up_w,
        dec_down_w,
    ) = load_vmem
    enc_kept, dec_kept = refs[:10], refs[10:19]
    (decoded, embedded, values_t, load_sems, store_sems, block_sems, decoded_sems) = refs[19:]
    part = lax.axis_index("section")
    sources = list(load_hbm)
    sources[0] = sources[0].at[part, 0]
    sources[6] = sources[6].at[part]
    loads = Loads(sources, load_vmem, load_sems, 3)
    stores = Stores(store_sems)
    encode_rows(
        loads, stores, enc_kept, store_hbm[:10], tokens, sensor[part], norm, bias, up_bias,
        table, qkv_w, out_w, up_w, down_w,
    )
    loads.wait(5)
    embedded[...] = dot(enc_kept[-1][...], embed_w[...]) + row(dec_bias, 0)
    loads.wait(6, 7, 8)
    decode_rows(
        loads, stores, dec_kept, store_hbm[10:], embedded, places, pos, dec_norm, dec_bias,
        dec_up_bias, dec_qkv_w, dec_out_w, dec_up_w, dec_down_w, decoded, values_t, block_sems,
        decoded_sems,
    )
    stores.close()


def encode_rows(
    loads, stores, kept, kept_hbm, tokens, kind, norm, bias, up_bias, table, qkv_w, out_w, up_w,
    down_w,
):
    start_out, normed_out, packed, probs_out, attended_out, middle_out, second_out, active, slopes, encoded = kept

    def keep(item):
        stores.send(kept[item], kept_hbm[item])

    inner = out_w.shape[0]
    added = jnp.zeros((1, table.shape[1]), F32)
    for item in range(table.shape[0]):
        added = added + jnp.where(kind == item, row(table, item), 0.0)
    loads.wait(0)
    start = tokens[...].astype(F32) + added
    start_out[...] = start
    keep(0)
    normed = (normalize(start)[0] * row(norm, 0) + row(norm, 1)).astype(BF16)
    normed_out[...] = normed
    keep(1)
    loads.wait(1)
    packed[...] = dot(normed, qkv_w[...]).astype(BF16)
    keep(2)
    columns = []
    heads = LANES // HEAD_DIM
    for group in range(inner // LANES):
        base = group * LANES
        queries = packed[:, base : base + LANES] * jnp.asarray(HEAD_DIM**-0.5, BF16)
        keys = packed[:, inner + base : inner + base + LANES]
        values = packed[:, 2 * inner + base : 2 * inner + base + LANES].T

        def weigh(head, scores, group=group, values=values):
            probs = softmax_columns(scores)
            probs_out[group * heads + head] = probs
            columns.append(dot(values[head * HEAD_DIM : (head + 1) * HEAD_DIM], probs).astype(BF16))

        staggered(
            range(heads),
            lambda head, keys=keys, queries=queries: dot_nt(keys, only_head(queries, head)),
            weigh,
        )
    keep(3)
    attended = jnp.concatenate(columns, axis=0).T
    attended_out[...] = attended
    keep(4)
    loads.wait(2)
    middle = start + (dot(attended, out_w[...]) + row(bias, 0))
    middle_out[...] = middle
    keep(5)
    second = (normalize(middle)[0] * row(norm, 2) + row(norm, 3)).astype(BF16)
    second_out[...] = second
    keep(6)
    loads.wait(3)
    panel = 768

    def bend(low, lifted):
        cols = slice(low, low + panel)
        raised, slope = gelu_pair(lifted + line(up_bias, cols))
        active[:, cols] = raised.astype(BF16)
        slopes[:, cols] = slope.astype(BF16)

    staggered(
        range(0, up_w.shape[1], panel), lambda low: dot(second, up_w[:, low : low + panel]), bend
    )
    keep(7)
    keep(8)
    loads.wait(4)
    encoded[...] = (middle + row(bias, 1) + dot(active[...], down_w[...])).astype(BF16)
    keep(9)


def decode_rows(
    loads, stores, kept, kept_hbm, embedded, places, pos, norm, bias, up_bias, qkv_w, out_w, up_w,
    down_w, decoded, values_t, block_sems, decoded_sems,
):
    placed, normed, packed, probs, attended, middle, second, active, slopes = kept
    length = pos.shape[0]
    inner = out_w.shape[0]
    visible = embedded.shape[0]
    heads = inner // HEAD_DIM
    blocks = length // BLOCK
    high = embedded[...].astype(BF16)
    rest = (embedded[...] - high.astype(F32)).astype(BF16)
    spots = places[:, pl.ds(0, visible)]

    def place(block):
        hit = lax.broadcasted_iota(jnp.int32, (BLOCK, visible), 0) + block * BLOCK == spots
        pick = jnp.where(hit, 1.0, 0.0).astype(BF16)
        seen = jnp.sum(jnp.where(hit, 1.0, 0.0), axis=1, keepdims=True)
        return dot(pick, high) + dot(pick, rest) + (1.0 - seen) * row(bias, 3)

    def begin(block, here):
        rows = slice(block * BLOCK, (block + 1) * BLOCK)
        here = here + pos[rows, :].astype(F32)
        placed[rows, :] = here
        norm_here = (normalize(here)[0] * row(norm, 0) + row(norm, 1)).astype(BF16)
        normed[rows, :] = norm_here
        packed[rows, :] = dot(norm_here, qkv_w[...]).astype(BF16)

    staggered(range(blocks), place, begin)
    for item in range(3):
        stores.send(kept[item], kept_hbm[1 + item])
    values_t[...] = packed[:, 2 * inner :].T
    loads.wait(9, 10, 11)
    bound = [(source, target) for source, target in zip(kept[3:], kept_hbm[4:])]

    def second_pass(block, carry):
        base = pl.multiple_of(block * BLOCK, BLOCK)
        rows = pl.ds(base, BLOCK)
        slot = lax.rem(block, 2)

        def out_copy(spot):
            return pltpu.make_async_copy(
                decoded.at[lax.rem(spot, 2)],
                kept_hbm[0].at[pl.ds(pl.multiple_of(spot * BLOCK, BLOCK), BLOCK)],
                decoded_sems.at[lax.rem(spot, 2)],
            )

        queries = packed[rows, :inner] * jnp.asarray(HEAD_DIM**-0.5, BF16)
        keys = packed[:, inner : 2 * inner]
        columns = []

        def weigh(head, scores):
            probs_here = softmax_columns(scores)
            probs[block, :, pl.ds(head * BLOCK, BLOCK)] = probs_here
            columns.append(
                dot(values_t[head * HEAD_DIM : (head + 1) * HEAD_DIM, :], probs_here).astype(BF16)
            )

        staggered(range(heads), lambda head: dot_nt(keys, only_head(queries, head)), weigh)
        attended_here = jnp.concatenate(columns, axis=0).T
        attended[rows, :] = attended_here
        middle_here = placed[rows, :] + (dot(attended_here, out_w[...]) + row(bias, 1))
        middle[rows, :] = middle_here
        second_here = (normalize(middle_here)[0] * row(norm, 2) + row(norm, 3)).astype(BF16)
        second[rows, :] = second_here
        panel = 512

        def bend(low, lifted):
            cols = slice(low, low + panel)
            raised, slope = gelu_pair(lifted + line(up_bias, cols))
            active[rows, cols] = raised.astype(BF16)
            slopes[rows, cols] = slope.astype(BF16)

        staggered(
            range(0, up_w.shape[1], panel),
            lambda low: dot(second_here, up_w[:, low : low + panel]),
            bend,
        )

        @pl.when(block >= 2)
        def _():
            out_copy(block - 2).wait()

        decoded[slot] = middle_here + (dot(active[rows, :], down_w[...]) + row(bias, 2))
        out_copy(block).start()
        for item, (source, target) in enumerate(bound):
            spot = rows if item else block
            pltpu.make_async_copy(source.at[spot], target.at[spot], block_sems.at[item]).start()

        @pl.when(block == blocks - 1)
        def _():
            out_copy(block - 1).wait()
            out_copy(block).wait()

        return carry

    lax.fori_loop(0, blocks, second_pass, 0)
    for item, (source, target) in enumerate(bound):
        pltpu.make_async_copy(source, target, block_sems.at[item]).wait()


WHOLE = pl.BlockSpec(memory_space=pltpu.VMEM)
APART = pl.BlockSpec(memory_space=pl.ANY)
SCALARS = pl.BlockSpec(memory_space=pltpu.SMEM)
LIMIT = pltpu.CompilerParams(vmem_limit_bytes=63 * 2**20)


def like(array):
    return pltpu.VMEM(array.shape, array.dtype)


def run_forward(tokens, order, sensor, enc_w, dec_w):
    norm, qkv_w, out_w, bias, up_w, up_bias, down_w, table = enc_w
    embed_w, dec_norm, dec_qkv_w, dec_out_w, dec_bias, dec_up_w, dec_up_bias, dec_down_w, pos = dec_w
    rows, width = tokens.shape[2:]
    inner, hidden = out_w.shape[0], up_w.shape[1]
    shaped = jax.ShapeDtypeStruct
    enc_kept = [
        shaped((rows, width), F32),
        shaped((rows, width), BF16),
        shaped((rows, 3 * inner), BF16),
        shaped((inner // HEAD_DIM, rows, rows), BF16),
        shaped((rows, inner), BF16),
        shaped((rows, width), F32),
        shaped((rows, width), BF16),
        shaped((rows, hidden), BF16),
        shaped((rows, hidden), BF16),
        shaped((rows, width), BF16),
    ]
    length, dec_width = pos.shape
    dec_inner, dec_hidden = dec_out_w.shape[0], dec_up_w.shape[1]
    blocks = length // BLOCK
    dec_kept = [
        shaped((length, dec_width), F32),
        shaped((length, dec_width), BF16),
        shaped((length, 3 * dec_inner), BF16),
        shaped((blocks, length, dec_inner // HEAD_DIM * BLOCK), BF16),
        shaped((length, dec_inner), BF16),
        shaped((length, dec_width), F32),
        shaped((length, dec_width), BF16),
        shaped((length, dec_hidden), BF16),
        shaped((length, dec_hidden), BF16),
    ]
    weights = [
        qkv_w, out_w, up_w, down_w, embed_w, pos, dec_qkv_w, dec_out_w, dec_up_w, dec_down_w
    ]
    held = [like(item) for item in weights]
    results = pl.pallas_call(
        forward_kernel,
        out_shape=enc_kept + [shaped((length, dec_width), F32)] + dec_kept,
        in_specs=[SCALARS] + [WHOLE] * 7 + [APART] * 12,
        out_specs=[APART] * 20,
        scratch_shapes=[pltpu.VMEM((rows, width), BF16)]
        + held[:5]
        + [pltpu.VMEM((1, length), jnp.int32)]
        + held[5:]
        + [like(item) for item in enc_kept + dec_kept]
        + [
            pltpu.VMEM((2, BLOCK, dec_width), F32),
            pltpu.VMEM((rows, dec_width), F32),
            pltpu.VMEM((dec_inner, length), BF16),
            pltpu.SemaphoreType.DMA((12,)),
            pltpu.SemaphoreType.DMA((13,)),
            pltpu.SemaphoreType.DMA((6,)),
            pltpu.SemaphoreType.DMA((2,)),
        ],
        compiler_params=LIMIT,
        name="forward",
    )(
        sensor,
        norm,
        bias,
        up_bias,
        table,
        dec_norm,
        dec_bias,
        dec_up_bias,
        tokens,
        *weights[:5],
        order,
        *weights[5:],
    )
    return results[:9], results[9], results[10], results[11:]


def column_sum(values):
    return jnp.sum(values, axis=0, keepdims=True)


def norm_back(grad, values, scale):
    normal, inverse = normalize(values)
    inner = grad * scale
    mean_inner = jnp.mean(inner, axis=-1, keepdims=True)
    mean_both = jnp.mean(inner * normal, axis=-1, keepdims=True)
    return (
        inverse * (inner - mean_inner - normal * mean_both),
        column_sum(grad * normal),
        column_sum(grad),
    )


def attention_back(queries, keys, values, keys_t, probs, grad_rows, attended):
    block = queries.shape[0]
    heads = LANES // HEAD_DIM
    product = (grad_rows.astype(F32) * attended.astype(F32)).T
    scores_back, query_grads = [], []

    def through(head, probs_back):
        lanes = slice(head * HEAD_DIM, (head + 1) * HEAD_DIM)
        row_dots = column_sum(product[lanes])
        probs_here = probs[:, head * block : (head + 1) * block].astype(F32)
        scores_here = (probs_here * (probs_back - row_dots)).astype(BF16)
        scores_back.append(scores_here)
        query_grads.append(dot(keys_t[lanes], scores_here))

    staggered(range(heads), lambda head: dot_nt(values, only_head(grad_rows, head)), through)
    stacked_grad = jnp.concatenate([only_head(grad_rows, head) for head in range(heads)], axis=0)
    stacked_queries = jnp.concatenate([only_head(queries, head) for head in range(heads)], axis=0)
    grad_values = dot(probs, stacked_grad)
    grad_keys = dot(jnp.concatenate(scores_back, axis=1), stacked_queries)
    grad_queries = jnp.concatenate(query_grads, axis=0).T
    return grad_queries, grad_keys, grad_values


class Plan:
    def __init__(self, bits, parts):
        self.bits, self.parts = bits, parts
        self.spans, count = [], 0
        for waves, begin, end in parts:
            for wave in waves:
                for _ in wave:
                    self.spans.append((count, count + end - begin))
                    count += end - begin

    def shape(self, cut, step):
        rows, cols, _ = cut
        return (2,) * (self.bits - step) + (rows[1], cols[1])

    def cuts(self, slot):
        return [cut for wave in self.parts[slot][0] for cut in wave]

    def handed(self, slot):
        return [self.shape(cut, self.parts[slot][2] - 1) for cut in self.cuts(slot)]

    def scratch(self):
        lands = [
            pltpu.VMEM(self.shape(cut, step), BF16)
            for slot, (_, begin, end) in enumerate(self.parts)
            for cut in self.cuts(slot)
            for step in range(begin, end)
        ]
        sems = pltpu.SemaphoreType.DMA((len(lands),))
        return lands + [sems, sems]

    def bind(self, refs):
        self.refs = refs

    def chunks(self, slot, sources, results):
        send_sems, recv_sems = self.refs[-2:]
        orders = orders_of(self.bits)
        waves, begin, end = self.parts[slot]
        item = sum(len(self.cuts(other)) for other in range(slot))
        made, local = [], 0
        for wave in waves:
            made.append([])
            for rows, cols, which in wave:
                order = orders[which][0]
                low, high = self.spans[item + local]
                dims = [bit for bit in range(self.bits - 1, -1, -1) if bit not in order[:begin]]
                made[-1].append(
                    Chunk(
                        sources[local] if isinstance(sources, (list, tuple)) else sources,
                        rows,
                        cols,
                        order[begin:end],
                        dims,
                        self.refs[low:high],
                        [send_sems.at[spot] for spot in range(low, high)],
                        [recv_sems.at[spot] for spot in range(low, high)],
                        results[local] if isinstance(results, (list, tuple)) else results,
                    )
                )
                local += 1
        return made


def wave_lists(bits, blocks, loads):
    return [wave_plan(rows, width, orders_of(bits), loads) for rows, width in blocks]


def fold(values, target):
    return values.astype(BF16).reshape(target.shape[:-1] + (values.shape[-1],))


def decode_back_kernel(plan, bits, *refs):
    (cotangent_hbm, places_hbm, norm, *refs) = refs
    load_hbm, refs = refs[:15], refs[15:]
    (returned, pos_out, embed_out, norm_sum, bias_sum, up_sum, down_done, *refs) = refs
    handed = []
    for slot in (1, 2, 3):
        count = len(plan.cuts(slot))
        handed.append(refs[:count])
        refs = refs[count:]
    (cotangent, places, *refs) = refs
    load_vmem, refs = refs[:15], refs[15:]
    (
        active, down_w, slope, second, up_w, middle, attended, out_w, probs, packed,
        normed, placed, qkv_w, encoded, embed_w,
    ) = load_vmem
    (down_grad, up_grad, out_grad, qkv_grad, grad_middle, attn_grad, grad_rows, grad_keys, grad_values,
     grad_packed, picked, load_sems, *refs) = refs
    plan.bind(refs)
    greet(bits)
    part = lax.axis_index("section")
    loads = Loads(
        [cotangent_hbm.at[part, 0], places_hbm.at[part], *load_hbm],
        [cotangent, places, *load_vmem],
        load_sems,
        6,
    )
    names = [
        "cotangent", "places", "active", "down_w", "slope", "second", "up_w", "middle", "attended",
        "out_w", "probs", "packed", "normed", "placed", "qkv_w", "encoded", "embed_w",
    ]

    def need(*wanted):
        loads.wait(*[names.index(item) for item in wanted])

    length, width = placed.shape
    inner, hidden = out_w.shape[0], up_w.shape[1]
    visible = encoded.shape[0]
    blocks = length // BLOCK
    flow = Flow(2)

    def send(slot, source, result):
        for wave in plan.chunks(slot, source, result):
            flow.add(wave)

    need("cotangent", "active")
    panel = hidden // 4
    for item in range(4):
        cols = slice(item * panel, (item + 1) * panel)
        piece = dot(active[:, cols].T, cotangent[...]).astype(BF16)
        target = down_grad.at[item // 2, item % 2]
        target[...] = piece.reshape(target.shape)
    greeted(bits)
    send(0, down_grad, down_done)
    bias_sum[0:1, :] = jnp.zeros((1, width), F32)
    bias_sum[2:3, :] = column_sum(cotangent[...].astype(F32))
    need("down_w", "slope", "up_w", "middle", "out_w", "second")

    def lift_back(block):
        rows = slice(block * BLOCK, (block + 1) * BLOCK)
        lifted_back = dot_nt(cotangent[rows, :], down_w[...]) * slope[rows, :].astype(F32)
        lifted_back = lifted_back.astype(BF16)
        slope[rows, :] = lifted_back
        up_part = column_sum(lifted_back.astype(F32))
        up_sum[...] = up_part + up_sum[...] if block else up_part
        return dot_nt(lifted_back, up_w[...])

    def middle_back(block, grad_second):
        rows = slice(block * BLOCK, (block + 1) * BLOCK)
        inward, scale_part, shift_part = norm_back(grad_second, middle[rows, :], row(norm, 2))
        total = cotangent[rows, :].astype(F32) + inward
        grad_middle[rows, :] = total
        rounded = total.astype(BF16)
        attn_grad[rows, :] = rounded
        bias_part = column_sum(rounded.astype(F32))
        grad_rows[rows, :] = dot_nt(rounded, out_w[...]).astype(BF16)
        if block:
            scale_part = scale_part + norm_sum[2:3, :]
            shift_part = shift_part + norm_sum[3:4, :]
            bias_part = bias_part + bias_sum[1:2, :]
        norm_sum[2:3, :] = scale_part
        norm_sum[3:4, :] = shift_part
        bias_sum[1:2, :] = bias_part
        if block % 2:
            flow.tick()

    staggered(range(blocks), lift_back, middle_back)
    second_t = second[...].T
    for item in range(4):
        cols = slice(item * panel, (item + 1) * panel)
        up_grad[:, :, :, :, :, cols] = fold(dot(second_t, slope[:, cols]), up_grad)
    send(1, up_grad, handed[0])
    need("attended")
    out_grad[...] = fold(dot(attended[...].T, attn_grad[...]), out_grad)
    send(2, out_grad, handed[1])
    need("probs", "packed")
    keys = packed[:, inner : 2 * inner]
    values = packed[:, 2 * inner :]
    keys_t = keys.T
    scale = HEAD_DIM**-0.5
    for block in range(blocks):
        rows = slice(block * BLOCK, (block + 1) * BLOCK)
        query_part, key_part, value_part = attention_back(
            packed[rows, :inner], keys, values, keys_t, probs[block], grad_rows[rows, :],
            attended[rows, :],
        )
        grad_packed[rows, :inner] = (query_part * scale).astype(BF16)
        if block:
            key_part = key_part + grad_keys[...]
            value_part = value_part + grad_values[...]
        if block < blocks - 1:
            grad_keys[...] = key_part
            grad_values[...] = value_part
        else:
            grad_packed[:, inner : 2 * inner] = (key_part * scale).astype(BF16)
            grad_packed[:, 2 * inner :] = value_part.astype(BF16)
        flow.tick()
    need("normed", "placed", "qkv_w", "places")
    qkv_grad[...] = fold(dot(normed[...].T, grad_packed[...]), qkv_grad)
    flow.tick()
    send(3, qkv_grad, handed[2])
    spots = places[:, pl.ds(0, visible)]

    def start_back(block, grad_normed):
        rows = slice(block * BLOCK, (block + 1) * BLOCK)
        inward, scale_part, shift_part = norm_back(grad_normed, placed[rows, :], row(norm, 0))
        total = grad_middle[rows, :] + inward
        hit = lax.broadcasted_iota(jnp.int32, (BLOCK, visible), 0) + block * BLOCK == spots
        pick = jnp.where(hit, 1.0, 0.0).astype(BF16)
        seen = jnp.sum(jnp.where(hit, 1.0, 0.0), axis=1, keepdims=True)
        fill_part = column_sum(total * (1.0 - seen))
        rounded = total.astype(BF16)
        pick_part = dot(pick.T, rounded)
        if block:
            scale_part = scale_part + norm_sum[0:1, :]
            shift_part = shift_part + norm_sum[1:2, :]
            fill_part = fill_part + bias_sum[3:4, :]
            pick_part = pick_part + picked[...]
        norm_sum[0:1, :] = scale_part
        norm_sum[1:2, :] = shift_part
        bias_sum[3:4, :] = fill_part
        picked[...] = pick_part
        pos_out[:, :, :, :, :, rows] = fold(rounded.T, pos_out)
        if block == 1:
            flow.tick()

    staggered(
        range(blocks),
        lambda block: dot_nt(grad_packed[block * BLOCK : (block + 1) * BLOCK, :], qkv_w[...]),
        start_back,
    )
    need("encoded", "embed_w")
    grad_embedded = picked[...].astype(BF16)
    bias_sum[0:1, :] = column_sum(picked[...])
    embed_out[...] = fold(dot(encoded[...].T, grad_embedded), embed_out)
    returned[...] = dot_nt(grad_embedded, embed_w[...]).astype(BF16)
    flow.drain()


def encode_back_kernel(plan, bits, *refs):
    (sensor, returned, norm, dec_norm_sum, dec_bias_sum, dec_up_sum, *refs) = refs
    early, refs = refs[:2], refs[2:]
    handed = []
    for slot in (0, 1, 2):
        count = len(plan.cuts(slot))
        handed.append(refs[:count])
        refs = refs[count:]
    load_hbm, refs = refs[:13], refs[13:]
    (input_grad, small_done, *refs) = refs
    done, refs = refs[:9], refs[9:]
    load_vmem, refs = refs[:13], refs[13:]
    (
        active, down_w, slope, second, up_w, middle, attended, out_w, probs, packed,
        normed, start, qkv_w,
    ) = load_vmem
    (down_grad, up_grad, out_grad, qkv_grad, grad_packed, small, small_lands, small_send,
     small_recv, load_sems, *refs) = refs
    plan.bind(refs)
    greet(bits)
    loads = Loads(load_hbm, load_vmem, load_sems, 6)
    names = [
        "active", "down_w", "slope", "second", "up_w", "middle", "attended", "out_w", "probs",
        "packed", "normed", "start", "qkv_w",
    ]

    def need(*wanted):
        loads.wait(*[names.index(item) for item in wanted])

    inner, hidden = out_w.shape[0], up_w.shape[1]
    width = start.shape[1]
    greeted(bits)
    flow = Flow(2)

    def send(slot, source, result, part=None):
        waves = plan.chunks(slot, source, result)
        for wave in waves if part is None else waves[part : part + 1]:
            flow.add(wave)

    for slot, source in enumerate([*handed, *early]):
        send(slot, source, done[slot])
    branch = returned[...]
    small[...] = jnp.zeros_like(small)
    small[5:6, :] = column_sum(branch.astype(F32))
    need("active")
    panel = hidden // 4
    for item in range(4):
        cols = slice(item * panel, (item + 1) * panel)
        target = down_grad.at[item // 2, item % 2]
        target[...] = dot(active[:, cols].T, branch).astype(BF16).reshape(target.shape)
    flow.tick()
    send(5, down_grad, done[5], 0)
    need("second", "slope", "down_w")
    second_t = second[...].T
    for item in range(4):
        cols = slice(item * panel, (item + 1) * panel)
        lifted_back = (dot_nt(branch, down_w[cols, :]) * slope[:, cols].astype(F32)).astype(BF16)
        slope[:, cols] = lifted_back
        small[10 + item : 11 + item, :] = column_sum(lifted_back.astype(F32))
        up_grad[:, :, :, :, :, cols] = fold(dot(second_t, lifted_back), up_grad)
        if item % 2:
            flow.tick()
    send(5, down_grad, done[5], 1)
    need("up_w", "middle", "out_w", "attended")
    grad_second = dot_nt(slope[...], up_w[...])
    inward, small[2:3, :], small[3:4, :] = norm_back(grad_second, middle[...], row(norm, 2))
    grad_middle = branch.astype(F32) + inward
    attn_grad = grad_middle.astype(BF16)
    small[4:5, :] = column_sum(attn_grad.astype(F32))
    flow.tick()
    send(6, up_grad, done[6], 0)
    out_grad[...] = fold(dot(attended[...].T, attn_grad), out_grad)
    grad_rows = dot_nt(attn_grad, out_w[...]).astype(BF16)
    flow.tick()
    send(6, up_grad, done[6], 1)
    need("probs", "packed")
    scale = HEAD_DIM**-0.5
    heads = LANES // HEAD_DIM
    for group in range(inner // LANES):
        base = group * LANES
        lanes = slice(base, base + LANES)
        keys = packed[:, inner + base : inner + base + LANES]
        query_part, key_part, value_part = attention_back(
            packed[:, lanes],
            keys,
            packed[:, 2 * inner + base : 2 * inner + base + LANES],
            keys.T,
            jnp.concatenate([probs[group * heads + head] for head in range(heads)], axis=1),
            grad_rows[:, lanes],
            attended[:, lanes],
        )
        grad_packed[:, lanes] = (query_part * scale).astype(BF16)
        grad_packed[:, inner + base : inner + base + LANES] = (key_part * scale).astype(BF16)
        grad_packed[:, 2 * inner + base : 2 * inner + base + LANES] = value_part.astype(BF16)
    flow.tick()
    need("normed", "start", "qkv_w")
    send(7, out_grad, done[7])
    normed_t = normed[...].T
    for item in range(3):
        cols = slice(item * inner, (item + 1) * inner)
        qkv_grad[:, :, :, :, :, cols] = fold(dot(normed_t, grad_packed[:, cols]), qkv_grad)
    flow.tick()
    send(8, qkv_grad, done[8])
    grad_normed = dot_nt(grad_packed[...], qkv_w[...])
    inward, small[0:1, :], small[1:2, :] = norm_back(grad_normed, start[...], row(norm, 0))
    grad_start = grad_middle + inward
    input_grad[...] = grad_start
    kinds = lax.broadcasted_iota(jnp.int32, (4, width), 0)
    mine = kinds == sensor[lax.axis_index("section")]
    small[6:10, :] = jnp.where(mine, column_sum(grad_start), 0.0)
    dec_width = dec_norm_sum.shape[1]
    small[14:18, :dec_width] = dec_norm_sum[...]
    small[18:22, :dec_width] = dec_bias_sum[...]
    for item in range(4):
        small[22 + item : 23 + item, :dec_width] = dec_up_sum[
            :, item * dec_width : (item + 1) * dec_width
        ]
    flow.add([Whole(small, bits, small_lands, small_send, small_recv, small_done)])
    flow.drain()


def finish_kernel(counts, *refs):
    small_count, big_count = counts
    small, big, refs = refs[0], refs[1 : 1 + big_count], refs[1 + big_count :]
    tiny, big_out, sems = refs[:small_count], refs[small_count:-1], refs[-1]
    copies = [
        pltpu.make_async_copy(source, target, sems.at[item])
        for item, (source, target) in enumerate(zip(big, big_out))
    ]
    for copy in copies:
        copy.start()
    section, data = lax.axis_index("section"), lax.axis_index("dp")
    datas = lax.axis_size("dp")
    first = 0
    for out in tiny:
        cols = out.shape[-1]
        if out.shape[0] > 1 or first == 4:
            lines = out.shape[0]
            width = cols * datas
            here = jnp.where(
                section == 0,
                small[first : first + lines, :width],
                small[first + lines : first + 2 * lines, :width],
            )
            spot = data * cols
            first += 2 * lines
        else:
            lines = 4
            width = cols * datas * 2 // lines
            per_line = width // cols
            index = section * datas + data
            here = jnp.zeros((1, width), F32)
            for line in range(lines):
                mine = index // per_line == line
                here = here + jnp.where(mine, small[first + line : first + line + 1, :width], 0.0)
            spot = lax.rem(index, per_line) * cols
            first += lines
        here = pltpu.roll(here, lax.rem(width - spot, width), 1)
        out[...] = here[:, :cols]
    for copy in copies:
        copy.wait()


def run_finish(small, big, shapes):
    shaped = jax.ShapeDtypeStruct
    return pl.pallas_call(
        partial(finish_kernel, (len(shapes), len(big))),
        out_shape=[shaped(item, F32) for item in shapes]
        + [shaped(item.shape, F32) for item in big],
        in_specs=[WHOLE] + [APART] * len(big),
        out_specs=[WHOLE] * (len(shapes) + len(big)),
        scratch_shapes=[pltpu.SemaphoreType.DMA((len(big),))],
        name="finish",
    )(small, *big)


def communicating(number):
    return pltpu.CompilerParams(
        collective_id=number, has_side_effects=True, vmem_limit_bytes=63 * 2**20
    )


def blocked(rows, cols, bits):
    return (2,) * bits + (rows // 2**bits, cols)


def run_decode_back(cotangent, order, stored, encoded, dec_w, bits):
    embed_w, norm, qkv_w, out_w, bias, up_w, up_bias, down_w, pos = dec_w
    placed, normed, packed, probs, attended, middle, second, active, slope = stored
    length, width = pos.shape
    inner, hidden = out_w.shape[0], up_w.shape[1]
    shaped = jax.ShapeDtypeStruct
    loaded = [
        active, down_w, slope, second, up_w, middle, attended, out_w, probs, packed, normed,
        placed, qkv_w, encoded, embed_w,
    ]
    sent = [blocked(*item.shape, bits) for item in (down_w, up_w, out_w, qkv_w)]
    later = [blocked(width, length, bits), blocked(*embed_w.shape, bits)]
    waves = wave_lists(bits, [(item[-2], item[-1] // 2) for item in sent], [0.0, 0.0, 0.0])
    ends = (bits + 1, 2, 2, 1)
    plan = Plan(bits, [(wave, 0, end) for wave, end in zip(waves, ends)])
    handed = [plan.handed(slot) for slot in (1, 2, 3)]
    results = pl.pallas_call(
        partial(decode_back_kernel, plan, bits),
        out_shape=[shaped(encoded.shape, BF16)]
        + [shaped(item, BF16) for item in later]
        + [shaped((4, width), F32), shaped((4, width), F32), shaped((1, hidden), F32)]
        + [shaped((sent[0][-2], sent[0][-1] // 2), F32)]
        + [shaped(item, BF16) for group in handed for item in group],
        in_specs=[APART, APART, WHOLE] + [APART] * len(loaded),
        out_specs=[WHOLE] * (7 + sum(len(group) for group in handed)),
        scratch_shapes=[
            pltpu.VMEM((length, width), BF16),
            pltpu.VMEM((1, length), jnp.int32),
        ]
        + [like(item) for item in loaded]
        + [pltpu.VMEM(item, BF16) for item in sent]
        + [
            pltpu.VMEM((length, width), F32),
            pltpu.VMEM((length, width), BF16),
            pltpu.VMEM((length, inner), BF16),
            pltpu.VMEM((length, inner), F32),
            pltpu.VMEM((length, inner), F32),
            pltpu.VMEM((length, 3 * inner), BF16),
            pltpu.VMEM((encoded.shape[0], width), F32),
            pltpu.SemaphoreType.DMA((len(loaded) + 2,)),
        ]
        + plan.scratch(),
        compiler_params=communicating(1),
        name="decode_back",
    )(cotangent, order, norm, *loaded)
    rest = results[7:]
    parts = [
        (waves[slot], ends[slot], (sent[slot][-2], sent[slot][-1] // 2)) for slot in (1, 2, 3)
    ]
    return results[0], results[1:3], results[3:6], results[6], rest, parts


def run_encode_back(returned, sensor, stored, enc_w, early, dec_sums, handed, parts, bits):
    norm, qkv_w, out_w, bias, up_w, up_bias, down_w, table = enc_w
    start, normed, packed, probs, attended, middle, second, active, slope = stored
    shaped = jax.ShapeDtypeStruct
    loaded = [
        active, down_w, slope, second, up_w, middle, attended, out_w, probs, packed, normed,
        start, qkv_w,
    ]
    own = [blocked(*item.shape, bits) for item in (down_w, up_w, out_w, qkv_w)]
    whole = [item.shape for item in early] + own
    blocks = [(item[-2], item[-1] // 2) for item in whole]
    waves = wave_lists(bits, blocks, [0.0, 0.0, 0.0])
    plan = Plan(
        bits,
        [(wave, begin, bits + 1) for wave, begin, _ in parts]
        + [(wave, 0, bits + 1) for wave in waves],
    )
    blocks = [block for _, _, block in parts] + blocks
    width = start.shape[1]
    small = (SMALL_ROWS, width)
    return pl.pallas_call(
        partial(encode_back_kernel, plan, bits),
        out_shape=[shaped(start.shape, F32), shaped(small, F32)]
        + [shaped(block, F32) for block in blocks],
        in_specs=[SCALARS] + [WHOLE] * (7 + len(handed)) + [APART] * len(loaded),
        out_specs=[WHOLE] * 11,
        scratch_shapes=[like(item) for item in loaded]
        + [pltpu.VMEM(item, BF16) for item in own]
        + [
            pltpu.VMEM(packed.shape, BF16),
            pltpu.VMEM(small, F32),
            pltpu.VMEM((bits + 1,) + small, F32),
            pltpu.SemaphoreType.DMA((bits + 1,)),
            pltpu.SemaphoreType.DMA((bits + 1,)),
            pltpu.SemaphoreType.DMA((len(loaded),)),
        ]
        + plan.scratch(),
        compiler_params=communicating(2),
        name="encode_back",
    )(sensor, returned, norm, *dec_sums, *early, *handed, *loaded)


def local_rows(whole, shape):
    section, data = lax.axis_index("section"), lax.axis_index("dp")
    sections, datas = lax.axis_size("section"), lax.axis_size("dp")
    if len(shape) == 1:
        count = shape[0] // (sections * datas)
        return lax.dynamic_slice_in_dim(
            whole.reshape(-1)[: shape[0]], (section * datas + data) * count, count, 0
        )
    rows, cols = shape[0] // sections, shape[1] // datas
    return lax.dynamic_slice(whole, (section * rows, data * cols), (rows, cols))


def plain_shards(tokens, order, sensor, cotangent, enc_w, dec_w):
    section_count = lax.axis_size("section")
    section_index = lax.axis_index("section")
    half_count = tokens.shape[0] // section_count

    def mine(array):
        part = lax.dynamic_slice_in_dim(array, section_index * half_count, half_count, 0)
        return part.reshape((half_count * array.shape[1],) + array.shape[2:])

    encoded, stored, picks = encode(mine(tokens), mine(sensor), enc_w)
    output, returned, dec_grads = decode(encoded, mine(order), mine(cotangent), dec_w)
    grad_input, enc_grads = encode_back(stored, picks, returned, enc_w)
    done = []
    for slot, grad in enumerate(enc_grads + dec_grads):
        if slot in (0, 3, 5, 7, 9, 12, 14):
            total = local_rows(lax.psum(grad, ("section", "dp")), grad.shape)
        else:
            side = 0 if slot == 16 else 1
            total = lax.psum_scatter(
                grad.astype(jnp.bfloat16), "section", scatter_dimension=side, tiled=True
            )
            total = lax.psum_scatter(total, "dp", scatter_dimension=1 - side, tiled=True)
        done.append(total.astype(jnp.float32))
    decoded = output.reshape((half_count,) + cotangent.shape[1:])
    input_grad = grad_input.reshape((half_count,) + tokens.shape[1:])
    return (decoded, input_grad) + tuple(done)


def shards(tokens, order, sensor, cotangent, *weights):
    enc_w, dec_w = weights[:8], weights[8:]
    sections, datas = lax.axis_size("section"), lax.axis_size("dp")
    split_rows = [enc_w[1], enc_w[2], enc_w[4], enc_w[6], dec_w[0], dec_w[2], dec_w[3], dec_w[5]]
    fits = (
        sections == 2
        and tokens.shape[:2] == (sections, 1)
        and datas & (datas - 1) == 0
        and datas >= 4
        and all(item.shape[0] % (16 * datas) == 0 for item in split_rows)
    )
    if not fits:
        return plain_shards(tokens, order, sensor, cotangent, enc_w, dec_w)
    bits = datas.bit_length() - 1
    kinds = sensor.reshape(-1)
    enc_kept, encoded, decoded, dec_kept = run_forward(tokens, order, kinds, enc_w, dec_w)
    returned, early, dec_sums, down_dec, handed, parts = run_decode_back(
        cotangent, order, dec_kept, encoded, dec_w, bits
    )
    input_grad, small, *rest = run_encode_back(
        returned, kinds, enc_kept, enc_w, early, dec_sums, handed, parts, bits
    )
    up_dec, out_dec, qkv_dec, pos, embed, down, up, out, qkv = rest
    tiny_slots = (0, 3, 7, 5, 9, 12, 14)
    shapes = [
        (item.shape[0] // 2, item.shape[1] // datas)
        if item.ndim == 2
        else (1, item.shape[0] // (2 * datas))
        for item in (weights[slot] for slot in tiny_slots)
    ]
    large = {
        1: qkv, 2: out, 4: up, 6: down, 8: embed, 10: qkv_dec, 11: out_dec, 13: up_dec, 15: down_dec,
        16: pos,
    }
    results = run_finish(small, [input_grad, *large.values()], shapes)
    done = dict(zip([*tiny_slots, "input", *large], results))
    for slot in (5, 14):
        done[slot] = done[slot].reshape(-1)
    done[16] = done[16].T
    return (decoded[None, None], done["input"][None, None]) + tuple(
        done[slot] for slot in range(17)
    )


def solution(mesh):
    placed = (
        P(None, "dp", None, None),
        P(None, "dp", None),
        P(None, "dp"),
        P(None, "dp", None, None),
        P(),
        P(),
        P(),
        P(),
        P(),
        P(),
        P(),
        P(),
        P(),
        P(),
        P(),
        P(),
        P(),
        P(),
        P(),
        P(),
        P(),
    )
    return jax.shard_map(
        shards,
        mesh=mesh,
        in_specs=placed,
        out_specs=(
            P("section", "dp", None, None),
            P("section", "dp", None, None),
            P("section", "dp"),
            P("dp", "section"),
            P("dp", "section"),
            P("section", "dp"),
            P("dp", "section"),
            P(("section", "dp")),
            P("dp", "section"),
            P("section", "dp"),
            P("dp", "section"),
            P("section", "dp"),
            P("dp", "section"),
            P("dp", "section"),
            P("section", "dp"),
            P("dp", "section"),
            P(("section", "dp")),
            P("dp", "section"),
            P("section", "dp"),
        ),
        check_vma=False,
    )
```
